128 devices in a mesh: dp: 4 (over y), ctx: 32 (over z, x, core).
Axes of the slice: x: 4, y: 4, z: 4, core: 2. Of those that a mesh axis runs over, the one named last changes fastest.
Arguments:
- queries: bfloat16 [4, 8192, 1024], P('dp', 'ctx'), may hold values from -36 to 36
- key_rows: bfloat16 [4, 8192, 128], P('dp', 'ctx'), may hold values from -12 to 12
- value_rows: bfloat16 [4, 8192, 128], P('dp', 'ctx'), may hold values from -6 to 6
- forward_out: bfloat16 [4, 8192, 1024], P('dp', 'ctx'), may hold values from -6 to 6
- out_grad: bfloat16 [4, 8192, 1024], P('dp', 'ctx'), may hold values from -6 to 6
- layer_input: bfloat16 [4, 8192, 4096], P('dp', 'ctx'), may hold values from -0.21875 to 0.21875
- doc_lengths: int32 [4, 4], P('dp'), may hold values from 1 to 4096, 8192 in all within a row
- held_span: int32 [4, 32], P('dp'), may hold values from 0 to 31, each once within a row
Outputs:
- query_grad: bfloat16 [4, 8192, 1024], P('dp', 'ctx')
- key_grad: bfloat16 [4, 8192, 128], P('dp', 'ctx')
- value_grad: bfloat16 [4, 8192, 128], P('dp', 'ctx')
- weight_grad: float32 [4096, 1280], P(('dp', 'ctx'))
The draws below stay inside these ranges and needn't reach their ends.
Inputs may be any that keep to these rules, and one draw needn't show every extreme that they name: `doc_lengths`: each row sums to 8192. `held_span`: each row holds every number of 0 to 31 once.
All inputs are finite; a program needn't handle non-finite values.
Results may differ from the reference program's by a relative error of at most 0.011.
Values may be sent and summed in bfloat16 or wider, within the bound.
A program may use at most 128 MiB of HBM per device.

```python
import math
import jax
import jax.numpy as jnp
import numpy as np
from jax import lax

HQ = 8
DH = 128
D = 4096
DOCS = 4
TOK_DEV = 256
SEQ = 8192
N_DP = 4
N_CTX = 32


def shared_keys(key):
    return jax.random.truncated_normal(key, -4.0, 4.0, (N_DP, SEQ, DH), jnp.float32)


def draw_key_rows(key, part):
    base_rows = shared_keys(key)
    return base_rows.astype(jnp.bfloat16)


def draw_queries(key, part):
    key = jax.random.fold_in(key, 5)
    drawn = jax.random.truncated_normal(key, -4.0, 4.0, (N_DP, SEQ, HQ * DH), jnp.float32)
    return drawn.astype(jnp.bfloat16)


def with_spikes(array, own_key, source, target, shards_of, factor):
    def block_of(dim):
        return (jnp.arange(array.shape[dim]) // (array.shape[dim] // shards_of)).reshape((-1,) + (1,) * (array.ndim - 1 - dim))

    first = jax.random.permutation(own_key, shards_of)[block_of(target)]
    second = (block_of(target) + shards_of // 2) % shards_of
    return jnp.where((block_of(source) == first) | (block_of(source) == second), factor * array, array)


def block_levels(rng, dims, cuts, least, top_value):
    def one(axis_at, blocks):
        heights = jax.random.uniform(jax.random.fold_in(jax.random.fold_in(rng, 6), axis_at), (blocks,), jnp.float32, least / len(cuts), top_value / len(cuts))
        return jnp.repeat(jnp.exp(heights), dims[axis_at] // blocks).reshape((-1,) + (1,) * (len(dims) - axis_at - 1))

    loudness = one(*cuts[0])
    for cut in cuts[1:]:
        loudness = loudness * one(*cut)
    return loudness


def split_up(amount, total, bound, slope):
    weights = [(1 << 20) // math.isqrt(rank ** slope) + 1 for rank in range(2, amount + 1)]
    surplus, holding = total - bound - (amount - 1), [1] * (amount - 1)
    while surplus > 0:
        movable = [i for i in range(amount - 1) if holding[i] < bound]
        mass, budget = sum([weights[i] for i in movable]), surplus
        for i in movable:
            extra = min(bound - holding[i], max(1, budget * weights[i] // mass), surplus)
            holding[i] = holding[i] + extra
            surplus = surplus - extra
    return np.array([bound] + holding)


def ragged(key, number_of, total, most, lean):
    if number_of == 2:
        one = jax.random.randint(key, (), max(1, total - most), min(most, total - 1) + 1)
        return jnp.stack([one, total - one])
    lengths = jnp.asarray(split_up(number_of, total, most, lean), jnp.int32)
    twos = (number_of - 1) // 2
    donor, sink = lengths[1:1 + 2 * twos:2], lengths[2:2 + 2 * twos:2]
    margin = jnp.minimum(donor - 1, most - sink)
    passed = jax.random.randint(jax.random.fold_in(key, 1), (twos,), 0, 1 << 20) % (margin + 1)
    lengths = lengths.at[1:1 + 2 * twos:2].set(donor - passed).at[2:2 + 2 * twos:2].set(sink + passed)
    return lengths[jax.random.permutation(jax.random.fold_in(key, 2), number_of)]


def centred(rng, dims, scale, bound, cuts=(), kind=jnp.bfloat16):
    loudness = block_levels(rng, dims, cuts, -0.22, 0.18) if cuts else 1.0
    array = jax.random.normal(rng, dims, jnp.float32) * scale * loudness
    return jnp.minimum(jnp.maximum(array, -bound), bound).astype(kind)


def gaussian_with(stream_key, dims, deviation, most, cuts, heavy, kind=jnp.bfloat16):
    drawn = deviation * jax.random.normal(stream_key, dims, jnp.float32)
    if cuts:
        drawn = drawn * block_levels(stream_key, dims, cuts, -0.22, 0.18)
    return jnp.clip(with_spikes(drawn, jax.random.fold_in(stream_key, 3), *heavy), -most, most).astype(kind)


def setup_inputs(seed: int = 0) -> dict:
    keys = jax.random.split(jax.random.key(seed), 9)
    queries = draw_queries(jax.random.fold_in(keys[8], 71), 0)
    key_rows = draw_key_rows(jax.random.fold_in(keys[8], 71), 0)
    value_rows = centred(keys[2], (N_DP, SEQ, DH), 1.0, 6.0, ((0, 4), (1, 32)))
    forward_out = centred(keys[3], (N_DP, SEQ, HQ * DH), 1.0, 6.0, ((0, 4), (1, 32)))
    out_grad = centred(keys[4], (N_DP, SEQ, HQ * DH), 1.0, 6.0, ((0, 4), (1, 32)))
    layer_input = gaussian_with(keys[5], (N_DP, SEQ, D), 0.0078125, 0.21875, ((0, 4), (1, 32)), (1, 2, 32, 2.75))
    doc_lengths = jax.vmap(lambda own: ragged(own, DOCS, SEQ, SEQ // 2, 2))(jax.random.split(keys[6], N_DP)).reshape((N_DP, DOCS)).astype(jnp.int32)
    held_span = jax.vmap(lambda own: jax.random.permutation(own, N_CTX))(jax.random.split(keys[7], N_DP)).reshape((N_DP, N_CTX)).astype(jnp.int32)
    return dict(queries=queries, key_rows=key_rows, value_rows=value_rows, forward_out=forward_out, out_grad=out_grad, layer_input=layer_input, doc_lengths=doc_lengths, held_span=held_span)


MASK_FILL = -1e+30

def document_of(positions, doc_ends):
    return lax.optimization_barrier(jnp.sum((positions[:, None] >= doc_ends[None, :]).astype(jnp.int32), axis=1))

def group_grads(queries, key_rows, value_rows, forward_out, out_grad, doc_lengths, held_span):
    seq_tokens = queries.shape[0]
    head_dim = key_rows.shape[1]
    head_count = queries.shape[1] // head_dim
    logit_scale = 1.0 / math.sqrt(head_dim)
    doc_ends = jnp.cumsum(doc_lengths)
    row_ids = jnp.arange(seq_tokens, dtype=jnp.int32)
    positions = (held_span[row_ids // TOK_DEV] * TOK_DEV + row_ids % TOK_DEV).astype(jnp.int32)
    documents = document_of(positions, doc_ends)

    def one_block(kv_grads, block_index):
        first_row = (block_index * TOK_DEV).astype(jnp.int32)
        query_block = lax.dynamic_slice_in_dim(queries, first_row, TOK_DEV, 0)
        grad_block = lax.dynamic_slice_in_dim(out_grad, first_row, TOK_DEV, 0)
        out_block = lax.dynamic_slice_in_dim(forward_out, first_row, TOK_DEV, 0)
        query_pos = lax.dynamic_slice_in_dim(positions, first_row, TOK_DEV, 0)
        query_doc = lax.dynamic_slice_in_dim(documents, first_row, TOK_DEV, 0)
        visible = (documents[None, :] == query_doc[:, None]) & (positions[None, :] <= query_pos[:, None])
        visible = visible[:, None, :]
        query_flat = query_block.reshape(TOK_DEV * head_count, head_dim)
        grad_flat = grad_block.reshape(TOK_DEV * head_count, head_dim)
        logits = jnp.dot(query_flat, key_rows.T, preferred_element_type=jnp.float32)
        logits = logits.reshape(TOK_DEV, head_count, seq_tokens) * logit_scale
        masked = jnp.where(visible, logits, MASK_FILL)
        row_max = lax.optimization_barrier(jnp.max(masked, axis=2))
        total_exp = lax.optimization_barrier(jnp.sum(jnp.where(visible, jnp.exp(masked - row_max[:, :, None]), 0.0), axis=2))
        log_norm = row_max + jnp.log(total_exp)
        probs = jnp.where(visible, jnp.exp(logits - log_norm[:, :, None]), 0.0)
        probs_low = probs.reshape(TOK_DEV * head_count, seq_tokens).astype(jnp.bfloat16)
        products = grad_block.astype(jnp.float32) * out_block.astype(jnp.float32)
        row_delta = lax.optimization_barrier(jnp.sum(products.reshape(TOK_DEV, head_count, head_dim), axis=2))
        prob_grad = jnp.dot(grad_flat, value_rows.T, preferred_element_type=jnp.float32)
        prob_grad = prob_grad.reshape(TOK_DEV, head_count, seq_tokens)
        logit_grad = (probs * (prob_grad - row_delta[:, :, None])).reshape(TOK_DEV * head_count, seq_tokens)
        logit_grad = logit_grad.astype(jnp.bfloat16)
        query_grad = logit_scale * jnp.dot(logit_grad, key_rows, preferred_element_type=jnp.float32)
        query_grad = query_grad.reshape(TOK_DEV, head_count * head_dim).astype(jnp.bfloat16)
        key_term = jnp.dot(logit_grad.T, query_flat, preferred_element_type=jnp.float32)
        value_term = jnp.dot(probs_low.T, grad_flat, preferred_element_type=jnp.float32)
        return (kv_grads + jnp.concatenate([key_term, value_term], axis=1), query_grad)
    start_grads = jnp.zeros((seq_tokens, 2 * head_dim), jnp.float32)
    kv_grads, query_grads = lax.scan(one_block, start_grads, jnp.arange(seq_tokens // TOK_DEV, dtype=jnp.int32))
    query_grads = query_grads.reshape(seq_tokens, head_count * head_dim)
    key_grad = (logit_scale * kv_grads[:, :head_dim]).astype(jnp.bfloat16)
    value_grad = kv_grads[:, head_dim:].astype(jnp.bfloat16)
    return (query_grads, key_grad, value_grad)

def reference(queries, key_rows, value_rows, forward_out, out_grad, layer_input, doc_lengths, held_span):
    query_list = []
    key_list = []
    value_list = []
    weight_grad = jnp.zeros((layer_input.shape[2], queries.shape[2] + 2 * key_rows.shape[2]), jnp.float32)
    for group in range(queries.shape[0]):
        query_grad, key_grad, value_grad = group_grads(queries[group], key_rows[group], value_rows[group], forward_out[group], out_grad[group], doc_lengths[group], held_span[group])
        joined = jnp.concatenate([query_grad, key_grad, value_grad], axis=1)
        weight_grad = weight_grad + jnp.dot(layer_input[group].T, joined, preferred_element_type=jnp.float32)
        query_list.append(query_grad)
        key_list.append(key_grad)
        value_list.append(value_grad)
    return (jnp.stack(query_list), jnp.stack(key_list), jnp.stack(value_list), weight_grad)
```

```python
import functools, math
import jax, jax.numpy as jnp
from jax import lax
from jax.experimental import pallas as pl
from jax.experimental.pallas import tpu as pltpu

F32 = jnp.float32
BF16 = jnp.bfloat16
NEG = -1e30


def dot(a, b):
    return jnp.dot(a, b, preferred_element_type=F32)


def attention_kernel(sets, heads, tok, dim, blocks,
                     ends_ref, held_ref, own_ref,
                     q_ref, do_ref, delta_ref, k_ref, v_ref,
                     dq_ref, dk_ref, dv_ref,
                     qt, dot_, kt, dqt, dka, dva, stat_m, stat_l, bias, seen):
    logit_scale = 1.0 / math.sqrt(dim)
    log2_scale = logit_scale * math.log2(math.e)

    dka[...] = jnp.zeros_like(dka)
    dva[...] = jnp.zeros_like(dva)
    for b in range(blocks):
        kt[b] = k_ref[b].T

    for rs in range(sets):
        own = own_ref[rs]
        span = held_ref[own]
        first = span * tok

        def count(d, lo):
            end = ends_ref[d]
            return jnp.where(end <= first, jnp.maximum(lo, end), lo)

        doc_count = ends_ref.shape[0]
        lo_first = lax.fori_loop(0, doc_count, count, jnp.int32(0))
        seen[0] = own

        def collect(b, n):
            h = held_ref[b]
            take = (h < span) & (h * tok + (tok - 1) >= lo_first)

            @pl.when(take)
            def _():
                seen[n] = b

            return n + take.astype(jnp.int32)

        total = lax.fori_loop(0, blocks, collect, jnp.int32(1))
        for h in range(heads):
            rows = pl.ds(h * dim, dim)
            qt[rows, :] = q_ref[rs, :, rows].T
            dot_[rows, :] = do_ref[rs, :, rows].T
        pos = first + lax.broadcasted_iota(jnp.int32, (1, tok), 1)
        low = jnp.zeros((1, tok), jnp.int32)
        for d in range(doc_count):
            end = ends_ref[d]
            low = jnp.where(pos >= end, jnp.maximum(low, end), low)

        stat_m[...] = jnp.full_like(stat_m, NEG)
        stat_l[...] = jnp.zeros_like(stat_l)
        dqt[...] = jnp.zeros_like(dqt)

        def set_bias(b):
            kp = held_ref[b] * tok + lax.broadcasted_iota(jnp.int32, (tok, tok), 0)
            bias[...] = jnp.where((kp >= low) & (kp <= pos), 0.0, NEG)

        def pass_one(i, carry):
            b = seen[i]
            set_bias(b)
            k = k_ref[b]
            for h in range(heads):
                s = dot(k, qt[pl.ds(h * dim, dim), :]) * log2_scale + bias[...]
                m_old = stat_m[pl.ds(h, 1), :]
                m_new = jnp.maximum(m_old, jnp.max(s, axis=0, keepdims=True))
                add = jnp.sum(jnp.exp2(s - m_new), axis=0, keepdims=True)
                stat_l[pl.ds(h, 1), :] = stat_l[pl.ds(h, 1), :] * jnp.exp2(m_old - m_new) + add
                stat_m[pl.ds(h, 1), :] = m_new
            return carry

        lax.fori_loop(0, total, pass_one, 0)
        stat_m[...] = stat_m[...] + jnp.log2(stat_l[...])

        def pass_two(i, carry):
            b = seen[i]
            set_bias(b)
            k = k_ref[b]
            v = v_ref[b]
            ktb = kt[b]
            dk = dka[b]
            dv = dva[b]
            for h in range(heads):
                rows = pl.ds(h * dim, dim)
                s = dot(k, qt[rows, :]) * log2_scale + bias[...]
                p = jnp.exp2(s - stat_m[pl.ds(h, 1), :])
                dp = dot(v, dot_[rows, :])
                ds = (p * (dp - delta_ref[rs, pl.ds(h, 1), :])).astype(BF16)
                dv = dv + dot(p.astype(BF16), do_ref[rs, :, rows])
                dk = dk + dot(ds, q_ref[rs, :, rows])
                dqt[rows, :] += dot(ktb, ds)
            dka[b] = dk
            dva[b] = dv
            return carry

        lax.fori_loop(0, total, pass_two, 0)
        for h in range(heads):
            rows = pl.ds(h * dim, dim)
            dq_ref[rs, :, rows] = (logit_scale * dqt[rows, :]).T.astype(BF16)

    def write(b, carry):
        dk_ref[b] = dka[b].astype(dk_ref.dtype)
        dv_ref[b] = dva[b].astype(dv_ref.dtype)
        return carry

    lax.fori_loop(0, blocks, write, 0)


def attention(ends, held, own, q, do, delta, k, v, out_dtype=BF16):
    sets, tok, width = q.shape
    blocks, _, dim = k.shape
    heads = width // dim
    smem = pl.BlockSpec(memory_space=pltpu.SMEM)
    vmem = pl.BlockSpec(memory_space=pltpu.VMEM)
    return pl.pallas_call(
        functools.partial(attention_kernel, sets, heads, tok, dim, blocks),
        out_shape=(
            jax.ShapeDtypeStruct(q.shape, BF16),
            jax.ShapeDtypeStruct(k.shape, out_dtype),
            jax.ShapeDtypeStruct(k.shape, out_dtype),
        ),
        in_specs=[smem, smem, smem, vmem, vmem, vmem, vmem, vmem],
        out_specs=(vmem, vmem, vmem),
        scratch_shapes=[
            pltpu.VMEM((width, tok), BF16),
            pltpu.VMEM((width, tok), BF16),
            pltpu.VMEM((blocks, dim, tok), BF16),
            pltpu.VMEM((width, tok), F32),
            pltpu.VMEM((blocks, tok, dim), F32),
            pltpu.VMEM((blocks, tok, dim), F32),
            pltpu.VMEM((heads, tok), F32),
            pltpu.VMEM((heads, tok), F32),
            pltpu.VMEM((tok, tok), F32),
            pltpu.SMEM((blocks + 1,), jnp.int32),
        ],
        compiler_params=pltpu.CompilerParams(vmem_limit_bytes=56 * 2**20),
        name="attention",
    )(ends, held, own, q, do, delta, k, v)


def local(
    queries, key_rows, value_rows, forward_out, out_grad, layer_input, doc_lengths, held_span
):
    tok = queries.shape[1]
    dim = key_rows.shape[2]
    heads = queries.shape[2] // dim
    scale = 1.0 / math.sqrt(dim)
    ctx = lax.axis_size("ctx")
    me = lax.axis_index("ctx").astype(jnp.int32)
    ends = jnp.cumsum(doc_lengths[0]).astype(jnp.int32)
    held = held_span[0]
    stacked = jnp.stack([key_rows[0], value_rows[0]])
    both = lax.all_gather(stacked, "ctx", axis=0)
    k, v = both[:, 0], both[:, 1]
    delta = jnp.sum(
        (out_grad[0].astype(F32) * forward_out[0].astype(F32)).reshape(tok, heads, dim), axis=2
    ).T[None]
    dq, dk, dv = attention(ends, held, me[None], queries, out_grad, delta, k, v, F32)
    grads = jnp.concatenate([dk, dv], axis=2).reshape(ctx * tok, 2 * dim)
    own = lax.psum_scatter(grads, "ctx", scatter_dimension=0, tiled=True)
    key_local = (scale * own[:, :dim]).astype(BF16)
    value_local = own[:, dim:].astype(BF16)
    joined = jnp.concatenate([dq[0], key_local, value_local], axis=1)
    weight = lax.psum_scatter(
        lax.dot_general(layer_input[0], joined, (((0,), (0,)), ((), ())), preferred_element_type=F32),
        ("dp", "ctx"), scatter_dimension=0, tiled=True,
    )
    return dq, key_local[None], value_local[None], weight


def solution(mesh):
    from jax.sharding import PartitionSpec as P
    row = P("dp", "ctx", None)
    flat = P("dp", None)
    return jax.shard_map(
        local, mesh=mesh, in_specs=(row,) * 6 + (flat,) * 2,
        out_specs=(row, row, row, P(("dp", "ctx"), None)), check_vma=False,
    )
```

```python
import functools, math
import jax, jax.numpy as jnp
from jax import lax
from jax.experimental import pallas as pl
from jax.experimental.pallas import tpu as pltpu
from jax.sharding import PartitionSpec as P

F32 = jnp.float32
BF16 = jnp.bfloat16
MESH = pl.DeviceIdType.MESH
NEG = -1e30


def dot(a, b):
    return jnp.dot(a, b, preferred_element_type=F32)


def attention_kernel(sets, heads, tok, dim, blocks,
                     ends_ref, held_ref, own_ref,
                     q_ref, do_ref, delta_ref, k_ref, v_ref,
                     dq_ref, dkv_ref,
                     qt, dot_, kt, dqt, dka, dva, stat_m, stat_l, bias, seen):
    logit_scale = 1.0 / math.sqrt(dim)
    log2_scale = logit_scale * math.log2(math.e)

    dka[...] = jnp.zeros_like(dka)
    dva[...] = jnp.zeros_like(dva)
    for rs in range(sets):
        own = own_ref[rs]
        span = held_ref[own]
        first = span * tok

        def count(d, lo):
            end = ends_ref[d]
            return jnp.where(end <= first, jnp.maximum(lo, end), lo)

        doc_count = ends_ref.shape[0]
        lo_first = lax.fori_loop(0, doc_count, count, jnp.int32(0))
        seen[0] = own

        def collect(b, n):
            h = held_ref[b]
            take = (h < span) & (h * tok + (tok - 1) >= lo_first)

            @pl.when(take)
            def _():
                seen[n] = b

            return n + take.astype(jnp.int32)

        total = lax.fori_loop(0, blocks, collect, jnp.int32(1))
        for h in range(heads):
            rows = pl.ds(h * dim, dim)
            qt[rows, :] = q_ref[rs, :, rows].T
            dot_[rows, :] = do_ref[rs, :, rows].T
        pos = first + lax.broadcasted_iota(jnp.int32, (1, tok), 1)
        low = jnp.zeros((1, tok), jnp.int32)
        for d in range(doc_count):
            end = ends_ref[d]
            low = jnp.where(pos >= end, jnp.maximum(low, end), low)

        stat_m[...] = jnp.full_like(stat_m, NEG)
        stat_l[...] = jnp.zeros_like(stat_l)
        dqt[...] = jnp.zeros_like(dqt)

        def set_bias(b):
            kp = held_ref[b] * tok + lax.broadcasted_iota(jnp.int32, (tok, tok), 0)
            bias[...] = jnp.where((kp >= low) & (kp <= pos), 0.0, NEG)

        def pass_one(i, carry):
            b = seen[i]
            set_bias(b)
            k = k_ref[b]
            kt[b] = k.T
            for h in range(heads):
                s = dot(k, qt[pl.ds(h * dim, dim), :]) * log2_scale + bias[...]
                m_old = stat_m[pl.ds(h, 1), :]
                m_new = jnp.maximum(m_old, jnp.max(s, axis=0, keepdims=True))
                add = jnp.sum(jnp.exp2(s - m_new), axis=0, keepdims=True)
                stat_l[pl.ds(h, 1), :] = stat_l[pl.ds(h, 1), :] * jnp.exp2(m_old - m_new) + add
                stat_m[pl.ds(h, 1), :] = m_new
            return carry

        lax.fori_loop(0, total, pass_one, 0)
        stat_m[...] = stat_m[...] + jnp.log2(stat_l[...])

        def pass_two(i, carry):
            b = seen[i]
            set_bias(b)
            k = k_ref[b]
            v = v_ref[b]
            ktb = kt[b]
            dk = dka[b]
            dv = dva[b]
            for h in range(heads):
                rows = pl.ds(h * dim, dim)
                s = dot(k, qt[rows, :]) * log2_scale + bias[...]
                p = jnp.exp2(s - stat_m[pl.ds(h, 1), :])
                dp = dot(v, dot_[rows, :])
                ds = (p * (dp - delta_ref[rs, pl.ds(h, 1), :])).astype(BF16)
                dv = dv + dot(p.astype(BF16), do_ref[rs, :, rows])
                dk = dk + dot(ds, q_ref[rs, :, rows])
                dqt[rows, :] += dot(ktb, ds)
            dka[b] = dk
            dva[b] = dv
            return carry

        lax.fori_loop(0, total, pass_two, 0)
        for h in range(heads):
            rows = pl.ds(h * dim, dim)
            dq_ref[rs, :, rows] = (logit_scale * dqt[rows, :]).T.astype(BF16)

    def write(b, carry):
        dkv_ref[0, b] = dka[b].astype(BF16)
        dkv_ref[1, b] = dva[b].astype(BF16)
        return carry

    lax.fori_loop(0, blocks, write, 0)


def attention(ends, held, own, q, do, delta, k, v):
    sets, tok, width = q.shape
    blocks, _, dim = k.shape
    heads = width // dim
    smem = pl.BlockSpec(memory_space=pltpu.SMEM)
    vmem = pl.BlockSpec(memory_space=pltpu.VMEM)
    return pl.pallas_call(
        functools.partial(attention_kernel, sets, heads, tok, dim, blocks),
        out_shape=(
            jax.ShapeDtypeStruct(q.shape, BF16),
            jax.ShapeDtypeStruct((2,) + k.shape, BF16),
        ),
        in_specs=[smem, smem, smem, vmem, vmem, vmem, vmem, vmem],
        out_specs=(vmem, vmem),
        scratch_shapes=[
            pltpu.VMEM((width, tok), BF16),
            pltpu.VMEM((width, tok), BF16),
            pltpu.VMEM((blocks, dim, tok), BF16),
            pltpu.VMEM((width, tok), F32),
            pltpu.VMEM((blocks, tok, dim), F32),
            pltpu.VMEM((blocks, tok, dim), F32),
            pltpu.VMEM((heads, tok), F32),
            pltpu.VMEM((heads, tok), F32),
            pltpu.VMEM((tok, tok), F32),
            pltpu.SMEM((blocks + 1,), jnp.int32),
        ],
        compiler_params=pltpu.CompilerParams(vmem_limit_bytes=56 * 2**20),
        name="attention",
    )(ends, held, own, q, do, delta, k, v)


def split_axis(t):
    return t // 2, lax.rem(t + t // 2, 2)


class Place:
    def __init__(self, with_dp):
        y = lax.axis_index("dp")
        me = lax.axis_index("ctx")
        z, x, c = me // 8, lax.rem(me // 2, 4), lax.rem(me, 2)
        self.core = c
        self.sibling = {"dp": y, "ctx": me + 1 - 2 * c}

        def at(y, z, x):
            return {"dp": y, "ctx": z * 8 + x * 2 + c}

        def low(t):
            return t + 1 - 2 * lax.rem(t, 2)

        self.bits = split_axis(z) + split_axis(x)
        self.partners = (at(y, 3 - z, x), at(y, low(z), x), at(y, z, 3 - x), at(y, z, low(x)))
        if with_dp:
            self.bits = split_axis(y) + self.bits
            self.partners = (at(3 - y, z, x), at(low(y), z, x)) + self.partners
        self.dims = len(self.bits)

    def greet(self):
        barrier = pltpu.get_barrier_semaphore()
        everyone = (self.sibling,) + self.partners
        for other in everyone:
            pl.semaphore_signal(barrier, inc=1, device_id=other, device_id_type=MESH)
        pl.semaphore_wait(barrier, len(everyone))

    def spot(self, free, flipped=None):
        found = []
        for d in range(self.dims):
            if d in free:
                found.append(slice(None))
            elif d == flipped:
                found.append(1 - self.bits[d])
            else:
                found.append(self.bits[d])
        return tuple(found)


def remote(src, dst, send, recv, to):
    return pltpu.make_async_remote_copy(
        src_ref=src, dst_ref=dst, send_sem=send, recv_sem=recv, device_id=to, device_id_type=MESH
    )


def turns(dims, start):
    return [(start + s) % dims for s in range(dims)]


def gather_kernel(k_ref, v_ref, q_ref, do_ref, o_ref, x_ref,
                  k_all, v_all, q_two, do_two, delta_two, xt_two,
                  x_buf, do_buf, o_buf, xt_buf, delta_buf,
                  hop_send, hop_recv, pass_send, pass_recv, side_send, side_recv, local_sem):
    tok, dim = k_ref.shape
    half = q_two.shape[2]
    here = Place(False)
    c = here.core
    dims = here.dims
    quarter = tok // dims
    sources, targets = (k_ref, v_ref), (k_all, v_all)

    loads = [
        pltpu.make_async_copy(do_ref, do_buf, local_sem.at[0]),
        pltpu.make_async_copy(o_ref, o_buf, local_sem.at[1]),
        pltpu.make_async_copy(x_ref, x_buf, local_sem.at[2]),
    ]
    keeps = [
        pltpu.make_async_copy(k_ref, k_all.at[here.bits + (c,)], local_sem.at[3]),
        pltpu.make_async_copy(v_ref, v_all.at[here.bits + (c,)], local_sem.at[4]),
        pltpu.make_async_copy(q_ref.at[:, pl.ds(c * half, half)], q_two.at[c], local_sem.at[5]),
        pltpu.make_async_copy(do_ref.at[:, pl.ds(c * half, half)], do_two.at[c], local_sem.at[6]),
    ]
    for copy in loads + keeps:
        copy.start()
    here.greet()

    def rows(p):
        return (pl.ds(p * quarter, quarter), slice(None))

    hops = {}
    for p in range(dims):
        for kind in range(2):
            n = (p * dims) * 2 + kind
            hops[p, 0, kind] = remote(
                sources[kind].at[rows(p)],
                targets[kind].at[here.bits + (c,) + rows(p)],
                hop_send.at[n], hop_recv.at[n], here.partners[turns(dims, p)[0]],
            )
            hops[p, 0, kind].start()
    sides = []
    to_side = [
        (k_ref, k_all.at[here.bits + (c,)]),
        (v_ref, v_all.at[here.bits + (c,)]),
        (q_ref.at[:, pl.ds((1 - c) * half, half)], q_two.at[c]),
        (do_ref.at[:, pl.ds((1 - c) * half, half)], do_two.at[c]),
    ]

    def aside(src, dst):
        n = len(sides)
        sides.append(remote(src, dst, side_send.at[n], side_recv.at[n], here.sibling))
        sides[-1].start()

    for src, dst in to_side:
        aside(src, dst)

    passes = []

    def hand_on(p, s):
        order = turns(dims, p)
        for kind in range(2):
            n = (p * dims + s) * 2 + kind
            hops[p, s, kind].wait_recv()
            part = targets[kind].at[here.spot(order[:s], order[s]) + (c,) + rows(p)]
            copy = remote(part, part, pass_send.at[n], pass_recv.at[n], here.sibling)
            copy.start()
            passes.append(copy)

    def hop(p, s):
        order = turns(dims, p)
        for kind in range(2):
            n = (p * dims + s) * 2 + kind
            part = targets[kind].at[here.spot(order[:s]) + (c,) + rows(p)]
            hops[p, s, kind] = remote(
                part, part, hop_send.at[n], hop_recv.at[n], here.partners[order[s]]
            )
            hops[p, s, kind].start()

    for copy in keeps:
        copy.wait()

    loads[0].wait()
    loads[1].wait()
    heads = half // dim
    for h in range(2 * heads):
        cols = pl.ds(h * dim, dim)
        products = do_buf[:, cols].astype(F32) * o_buf[:, cols].astype(F32)
        delta_buf[h // heads, pl.ds(h % heads, 1), :] = jnp.sum(products.T, axis=0, keepdims=True)
    for h in range(heads, delta_buf.shape[1]):
        delta_buf[:, pl.ds(h, 1), :] = jnp.zeros((2, 1, tok), F32)
    own_delta = pltpu.make_async_copy(delta_buf.at[c], delta_two.at[c], local_sem.at[7])
    own_delta.start()
    aside(delta_buf.at[1 - c], delta_two.at[c])

    for p in range(dims):
        hand_on(p, 0)
        hop(p, 1)
    loads[2].wait()

    def turn(i, carry):
        xt_buf[pl.ds(i * 128, 128), :] = x_buf[:, pl.ds(i * 128, 128)].T
        return carry

    steps = x_ref.shape[1] // 128
    lax.fori_loop(0, steps // 2, turn, 0)
    for p in range(dims):
        hand_on(p, 1)
        hop(p, 2)
    lax.fori_loop(steps // 2, steps, turn, 0)
    mine = xt_two.at[:, pl.ds(c * tok, tok)]
    own_xt = pltpu.make_async_copy(xt_buf, mine, local_sem.at[8])
    own_xt.start()
    for p in range(dims):
        hand_on(p, 2)
        hop(p, 3)
    aside(xt_buf, mine)
    for p in range(dims):
        hand_on(p, 3)
    own_delta.wait()
    own_xt.wait()
    for copy in hops.values():
        copy.wait_send()
    for copy in passes:
        copy.wait()
    for copy in sides:
        copy.wait()


def gather(k, v, q, do, o, x):
    tok, dim = k.shape
    half = q.shape[1] // 2
    anywhere = pl.BlockSpec(memory_space=pl.ANY)
    dma = pltpu.SemaphoreType.DMA
    full = jax.ShapeDtypeStruct((2, 2, 2, 2, 2, tok, dim), BF16)
    return pl.pallas_call(
        gather_kernel,
        out_shape=(
            full, full,
            jax.ShapeDtypeStruct((2, tok, half), BF16),
            jax.ShapeDtypeStruct((2, tok, half), BF16),
            jax.ShapeDtypeStruct((2, 8, tok), F32),
            jax.ShapeDtypeStruct((x.shape[1], 2 * tok), BF16),
        ),
        in_specs=[anywhere] * 6,
        out_specs=(anywhere,) * 6,
        scratch_shapes=[
            pltpu.VMEM(x.shape, BF16),
            pltpu.VMEM(q.shape, BF16),
            pltpu.VMEM(q.shape, BF16),
            pltpu.VMEM((x.shape[1], tok), BF16),
            pltpu.VMEM((2, 8, tok), F32),
            dma((32,)), dma((32,)), dma((32,)), dma((32,)), dma((6,)), dma((6,)), dma((9,)),
        ],
        compiler_params=pltpu.CompilerParams(
            collective_id=1, has_side_effects=True, vmem_limit_bytes=40 * 2**20
        ),
        name="gather",
    )(k, v, q, do, o, x)


def wide_parts(rows, cols):
    cut = cols // 4 * 3
    quarter, half = rows // 4, rows // 2
    return [(i * quarter, quarter, 0, cut) for i in range(4)] + [
        (i * half, half, cut, cols - cut) for i in range(2)
    ]


def thin_parts(rows, cols):
    return [(i * (rows // 4), rows // 4, 0, cols) for i in range(4)]


class Halving:
    def __init__(self, here, acc, parts, orders, landing, send, recv):
        self.here, self.acc, self.parts, self.orders = here, acc, parts, orders
        self.landing, self.send_sem, self.recv_sem = landing, send, recv
        self.copies = {}

    def index(self, p, s, flip):
        r0, nr, c0, nc = self.parts[p]
        order = self.orders[p]
        free = order[s + 1:]
        d = order[s]
        return self.here.spot(free, d if flip else None) + self.cut(r0, nr, c0, nc)

    def cut(self, r0, nr, c0, nc):
        return (slice(None),) * (len(self.acc.shape) - self.here.dims - 2) + (
            pl.ds(r0, nr), pl.ds(c0, nc))

    def send(self, p, s):
        dims = self.here.dims
        n = p * dims + s
        copy = remote(
            self.acc.at[self.index(p, s, True)], self.landing[n],
            self.send_sem.at[n], self.recv_sem.at[n], self.here.partners[self.orders[p][s]],
        )
        copy.start()
        self.copies[p, s] = copy

    def total(self, p, s):
        self.copies[p, s].wait_recv()
        n = p * self.here.dims + s
        return self.acc[self.index(p, s, False)].astype(F32) + self.landing[n][...].astype(F32)

    def add(self, p, s):
        self.acc[self.index(p, s, False)] = self.total(p, s).astype(self.acc.dtype)

    def finish(self):
        for copy in self.copies.values():
            copy.wait_send()


def landing_shapes(parts, orders, extra):
    shapes = []
    for (_, nr, _, nc), order in zip(parts, orders):
        for s in range(len(order)):
            shapes.append((2,) * (len(order) - 1 - s) + extra + (nr, nc))
    return shapes


def layout(tok, dim, half, features):
    row_chunk = features // 64
    kv_parts = thin_parts(tok, dim)
    kv_orders = [turns(4, p) for p in range(4)]
    wide = wide_parts(row_chunk, half)
    wide_orders = [turns(6, p) for p in range(6)]
    thin = thin_parts(row_chunk, dim)
    thin_orders = [turns(6, p) for p in (0, 2, 3, 5)]
    return row_chunk, kv_parts, kv_orders, wide, wide_orders, thin, thin_orders


def reduce_kernel(plan, scale, dkv_ref, dq_ref, xt_ref, qg_ref, kvg_ref, wg_ref, *scratch):
    row_chunk, kv_parts, kv_orders, wide, wide_orders, thin, thin_orders = plan
    (kv_acc, kv_in, kv_mine, w_acc, t_acc, xt, dq, fin, kv_send, kv_recv, w_send, w_recv, t_send, t_recv,
     side_send, side_recv, local_sem) = scratch[:17]
    landing = scratch[17:]
    tok, dim = dkv_ref.shape[-2:]
    half = dq_ref.shape[2]
    here_w = Place(True)
    here = Place(False)
    c = here.core
    n_kv, n_w = 16, 36
    kv = Halving(here, kv_acc, kv_parts, kv_orders, landing[:n_kv], kv_send, kv_recv)
    w = Halving(here_w, w_acc, wide, wide_orders, landing[n_kv:n_kv + n_w], w_send, w_recv)
    t = Halving(here_w, t_acc, thin, thin_orders, landing[n_kv + n_w:], t_send, t_recv)

    loads = [
        pltpu.make_async_copy(dq_ref, dq, local_sem.at[0]),
        pltpu.make_async_copy(xt_ref, xt, local_sem.at[1]),
        pltpu.make_async_copy(dkv_ref.at[c], kv_acc, local_sem.at[2]),
        pltpu.make_async_copy(dq_ref.at[c], qg_ref.at[:, pl.ds(c * half, half)], local_sem.at[3]),
    ]
    for copy in loads:
        copy.start()
    here_w.greet()
    sides = []

    def aside(src, dst):
        n = len(sides)
        sides.append(remote(src, dst, side_send.at[n], side_recv.at[n], here.sibling))
        sides[-1].start()

    rest = (slice(None),) * 5
    for p in range(4):
        r0, nr, _, _ = kv_parts[p]
        aside(dkv_ref.at[(1 - c,) + rest + (pl.ds(r0, nr),)], kv_in.at[rest + (pl.ds(r0, nr),)])
    aside(dq_ref.at[1 - c], qg_ref.at[:, pl.ds(c * half, half)])

    loads[2].wait()
    for p in range(4):
        r0, nr, _, _ = kv_parts[p]
        sides[p].wait_recv()

        def join(i, carry, r0=r0, nr=nr):
            at = (i // 8, lax.rem(i // 4, 2), lax.rem(i // 2, 2), lax.rem(i, 2), slice(None), pl.ds(r0, nr))
            kv_acc[at] = (kv_acc[at].astype(F32) + kv_in[at].astype(F32)).astype(BF16)
            return carry

        lax.fori_loop(0, 16, join, 0)
        kv.send(p, 0)

    loads[0].wait()
    loads[1].wait()

    def products(i, right, acc):
        block = dot(xt[pl.ds(i * 8 * row_chunk, 8 * row_chunk), :], right).astype(BF16)
        y = i // 2
        for j in range(8):
            z = 2 * lax.rem(i, 2) + j // 4
            x = j % 4
            at = split_axis(y) + split_axis(z) + (x // 2, (x + x // 2) % 2)
            acc[at] = block[j * row_chunk:(j + 1) * row_chunk]

    both = dq[...].reshape(2 * tok, half)

    def wide_products(i, carry):
        products(i, both, w_acc)
        return carry

    lax.fori_loop(0, 8, wide_products, 0)
    for p in range(6):
        w.send(p, 0)
    for s in range(1, 4):
        for p in range(4):
            kv.add(p, s - 1)
            kv.send(p, s)
    kv_scale = jnp.where(c == 0, scale, 1.0).astype(F32)
    for p in range(4):
        r0, nr, _, _ = kv_parts[p]
        kv_mine[:, pl.ds(r0, nr), :] = (kv.total(p, 3) * kv_scale).astype(BF16)
    own_kv = pltpu.make_async_copy(kv_mine.at[c], kvg_ref.at[c], local_sem.at[4])
    own_kv.start()
    aside(kv_mine.at[1 - c], kvg_ref.at[c])
    mine = kv_mine[...].reshape(2 * tok, dim)

    def thin_products(i, carry):
        products(i, mine, t_acc)
        return carry

    lax.fori_loop(0, 8, thin_products, 0)
    for p in range(4):
        t.send(p, 0)
    for s in range(1, 6):
        for p in range(6):
            w.add(p, s - 1)
            w.send(p, s)
        for p in range(4):
            t.add(p, s - 1)
            t.send(p, s)
    for p, (r0, nr, c0, nc) in enumerate(wide):
        fin[pl.ds(r0, nr), pl.ds(c0, nc)] = w.total(p, 5)
    for p, (r0, nr, c0, nc) in enumerate(thin):
        fin[pl.ds(r0, nr), pl.ds(half, nc)] = t.total(p, 5)
    rows_out = row_chunk // 2
    pieces = [(0, c * half, half), (half, 2 * half + c * dim, dim)]
    own_w = []
    for n, (src, dst, width) in enumerate(pieces):
        own_w.append(pltpu.make_async_copy(
            fin.at[pl.ds(c * rows_out, rows_out), pl.ds(src, width)],
            wg_ref.at[:, pl.ds(dst, width)], local_sem.at[5 + n]))
        own_w[-1].start()
        aside(fin.at[pl.ds((1 - c) * rows_out, rows_out), pl.ds(src, width)],
              wg_ref.at[:, pl.ds(dst, width)])
    loads[3].wait()
    own_kv.wait()
    for copy in own_w:
        copy.wait()
    for n, copy in enumerate(sides):
        copy.wait_send()
        if n >= 4:
            copy.wait_recv()
    kv.finish()
    w.finish()
    t.finish()


def reduce(dkv, dq, xt, scale):
    tok, dim = dkv.shape[-2:]
    half = dq.shape[2]
    features = xt.shape[0]
    plan = layout(tok, dim, half, features)
    row_chunk, kv_parts, kv_orders, wide, wide_orders, thin, thin_orders = plan
    anywhere = pl.BlockSpec(memory_space=pl.ANY)
    dma = pltpu.SemaphoreType.DMA
    shapes = (landing_shapes(kv_parts, kv_orders, (2,)) + landing_shapes(wide, wide_orders, ())
              + landing_shapes(thin, thin_orders, ()))
    return pl.pallas_call(
        functools.partial(reduce_kernel, plan, scale),
        out_shape=(
            jax.ShapeDtypeStruct((tok, 2 * half), BF16),
            jax.ShapeDtypeStruct((2, tok, dim), BF16),
            jax.ShapeDtypeStruct((row_chunk // 2, 2 * half + 2 * dim), F32),
        ),
        in_specs=[anywhere] * 3,
        out_specs=(anywhere,) * 3,
        scratch_shapes=[
            pltpu.VMEM(dkv.shape[1:], BF16),
            pltpu.VMEM(dkv.shape[1:], BF16),
            pltpu.VMEM((2, tok, dim), BF16),
            pltpu.VMEM((2,) * 6 + (row_chunk, half), BF16),
            pltpu.VMEM((2,) * 6 + (row_chunk, dim), BF16),
            pltpu.VMEM(xt.shape, BF16),
            pltpu.VMEM(dq.shape, BF16),
            pltpu.VMEM((row_chunk, half + dim), F32),
            dma((16,)), dma((16,)), dma((36,)), dma((36,)), dma((24,)), dma((24,)),
            dma((8,)), dma((8,)), dma((8,)),
        ] + [pltpu.VMEM(shape, BF16) for shape in shapes],
        compiler_params=pltpu.CompilerParams(
            collective_id=2, has_side_effects=True, vmem_limit_bytes=56 * 2**20
        ),
        name="reduce",
    )(dkv, dq, xt)


GRAY = (0, 1, 3, 2)


def local(
    queries, key_rows, value_rows, forward_out, out_grad, layer_input, doc_lengths, held_span
):
    tok = queries.shape[1]
    dim = key_rows.shape[2]
    me = lax.axis_index("ctx").astype(jnp.int32)
    z, x = me // 8, lax.rem(me // 2, 4)
    chip = (z // 2) * 8 + lax.rem(z + z // 2, 2) * 4 + (x // 2) * 2 + lax.rem(x + x // 2, 2)
    own = jnp.stack([2 * chip, 2 * chip + 1]).astype(jnp.int32)
    ends = jnp.cumsum(doc_lengths[0]).astype(jnp.int32)
    held = held_span[0].reshape(4, 4, 2)
    turned = jnp.stack([held[t] for t in GRAY])
    held = jnp.stack([turned[:, t] for t in GRAY], axis=1).reshape(-1)
    k, v, q, do, delta, xt = gather(
        key_rows[0], value_rows[0], queries[0], out_grad[0], forward_out[0], layer_input[0]
    )
    dq, dkv = attention(
        ends, held, own, q, do, delta, k.reshape(-1, tok, dim), v.reshape(-1, tok, dim)
    )
    dkv = dkv.reshape(2, 2, 2, 2, 2, 2, tok, dim)
    qg, kvg, wg = reduce(dkv, dq, xt, 1.0 / math.sqrt(dim))
    return qg[None], kvg[0][None], kvg[1][None], wg


def solution(mesh):
    row = P("dp", "ctx", None)
    flat = P("dp", None)
    return jax.shard_map(
        local, mesh=mesh, in_specs=(row,) * 6 + (flat,) * 2,
        out_specs=(row, row, row, P(("dp", "ctx"), None)), check_vma=False,
    )
```

```python
import functools, math
import jax, jax.numpy as jnp
from jax import lax
from jax.experimental import pallas as pl
from jax.experimental.pallas import tpu as pltpu
from jax.sharding import PartitionSpec as P

F32 = jnp.float32
BF16 = jnp.bfloat16
MESH = pl.DeviceIdType.MESH
NEG = -1e30


def dot(a, b):
    return jnp.dot(a, b, preferred_element_type=F32)


def split_axis(t):
    return t // 2, lax.rem(t + t // 2, 2)


def join_bits(bits):
    return ((bits[0] * 2 + bits[1]) * 2 + bits[2]) * 2 + bits[3]


def attention_kernel(sets, heads, tok, dim, blocks,
                     lengths_ref, span_ref,
                     q_in, do_in, delta_in, k_in, v_in,
                     dq_out, dkv_out,
                     qt, dot_, kt, dqt, dka, dva, stat_m, stat_l, bias, seen,
                     ends_ref, held_ref, q_ref, do_ref, delta_ref, k_ref, v_ref, loads,
                     dq_ref, dkv_ref, q_stores, kv_stores):
    logit_scale = 1.0 / math.sqrt(dim)
    log2_scale = logit_scale * math.log2(math.e)

    pairs = ((q_in, q_ref), (do_in, do_ref), (delta_in, delta_ref), (k_in, k_ref), (v_in, v_ref))
    copies = [pltpu.make_async_copy(src, dst, loads.at[n]) for n, (src, dst) in enumerate(pairs)]
    for copy in copies:
        copy.start()
    me = lax.axis_index("ctx")
    own_chip = join_bits(split_axis(me // 8) + split_axis(lax.rem(me // 2, 4)))
    doc_count = lengths_ref.shape[1]
    end = jnp.int32(0)
    for d in range(doc_count):
        end = end + lengths_ref[0, d]
        ends_ref[d] = end

    def place(i, carry):
        chip = join_bits(split_axis(i // 8) + split_axis(lax.rem(i // 2, 4)))
        held_ref[2 * chip + lax.rem(i, 2)] = span_ref[0, i]
        return carry

    lax.fori_loop(0, blocks, place, 0)
    dka[...] = jnp.zeros_like(dka)
    dva[...] = jnp.zeros_like(dva)
    for copy in copies:
        copy.wait()

    for rs in range(sets):
        own = 2 * own_chip + rs
        span = held_ref[own]
        first = span * tok

        def count(d, lo):
            end = ends_ref[d]
            return jnp.where(end <= first, jnp.maximum(lo, end), lo)

        lo_first = lax.fori_loop(0, doc_count, count, jnp.int32(0))
        seen[0] = own

        def collect(b, n):
            h = held_ref[b]
            take = (h < span) & (h * tok + (tok - 1) >= lo_first)

            @pl.when(take)
            def _():
                seen[n] = b

            return n + take.astype(jnp.int32)

        total = lax.fori_loop(0, blocks, collect, jnp.int32(1))
        for h in range(heads):
            rows = pl.ds(h * dim, dim)
            qt[rows, :] = q_ref[rs, :, rows].T
            dot_[rows, :] = do_ref[rs, :, rows].T
        pos = first + lax.broadcasted_iota(jnp.int32, (1, tok), 1)
        low = jnp.zeros((1, tok), jnp.int32)
        for d in range(doc_count):
            end = ends_ref[d]
            low = jnp.where(pos >= end, jnp.maximum(low, end), low)

        stat_m[...] = jnp.full_like(stat_m, NEG)
        stat_l[...] = jnp.zeros_like(stat_l)
        dqt[...] = jnp.zeros_like(dqt)

        def set_bias(b):
            kp = held_ref[b] * tok + lax.broadcasted_iota(jnp.int32, (tok, tok), 0)
            bias[...] = jnp.where((kp >= low) & (kp <= pos), 0.0, NEG)

        def pass_one(i, carry):
            b = seen[i]
            set_bias(b)
            k = k_ref[b]
            kt[b] = k.T
            for h in range(heads):
                s = dot(k, qt[pl.ds(h * dim, dim), :]) * log2_scale + bias[...]
                m_old = stat_m[pl.ds(h, 1), :]
                m_new = jnp.maximum(m_old, jnp.max(s, axis=0, keepdims=True))
                add = jnp.sum(jnp.exp2(s - m_new), axis=0, keepdims=True)
                stat_l[pl.ds(h, 1), :] = stat_l[pl.ds(h, 1), :] * jnp.exp2(m_old - m_new) + add
                stat_m[pl.ds(h, 1), :] = m_new
            return carry

        lax.fori_loop(0, total, pass_one, 0)
        stat_m[...] = stat_m[...] + jnp.log2(stat_l[...])

        def pass_two(i, carry):
            b = seen[i]
            set_bias(b)
            k = k_ref[b]
            v = v_ref[b]
            ktb = kt[b]
            dk = dka[b]
            dv = dva[b]
            for h in range(heads):
                rows = pl.ds(h * dim, dim)
                s = dot(k, qt[rows, :]) * log2_scale + bias[...]
                p = jnp.exp2(s - stat_m[pl.ds(h, 1), :])
                dp = dot(v, dot_[rows, :])
                ds = (p * (dp - delta_ref[rs, pl.ds(h, 1), :])).astype(BF16)
                dv = dv + dot(p.astype(BF16), do_ref[rs, :, rows])
                dk = dk + dot(ds, q_ref[rs, :, rows])
                dqt[rows, :] += dot(ktb, ds)
            dka[b] = dk
            dva[b] = dv
            return carry

        lax.fori_loop(0, total, pass_two, 0)
        for h in range(heads):
            rows = pl.ds(h * dim, dim)
            dq_ref[rs, :, rows] = (logit_scale * dqt[rows, :]).T.astype(BF16)
        pltpu.make_async_copy(dq_ref.at[rs], dq_out.at[rs], q_stores.at[rs]).start()

    def write(b, carry):
        for kind, acc in enumerate((dka, dva)):
            dkv_ref[kind, b] = acc[b].astype(BF16)
            store(kind, b).start()
        return carry

    def store(kind, b):
        return pltpu.make_async_copy(dkv_ref.at[kind, b], dkv_out.at[kind, b], kv_stores.at[kind, b])

    def stored(b, carry):
        store(0, b).wait()
        store(1, b).wait()
        return carry

    lax.fori_loop(0, blocks, write, 0)
    lax.fori_loop(0, blocks, stored, 0)
    for rs in range(sets):
        pltpu.make_async_copy(dq_ref.at[rs], dq_out.at[rs], q_stores.at[rs]).wait()


def attention(lengths, spans, q, do, delta, k, v):
    sets, tok, width = q.shape
    blocks, _, dim = k.shape
    heads = width // dim
    smem = pl.BlockSpec(memory_space=pltpu.SMEM)
    return pl.pallas_call(
        functools.partial(attention_kernel, sets, heads, tok, dim, blocks),
        out_shape=(
            jax.ShapeDtypeStruct(q.shape, BF16),
            jax.ShapeDtypeStruct((2,) + k.shape, BF16),
        ),
        in_specs=[smem, smem] + [pl.BlockSpec(memory_space=pltpu.HBM)] * 5,
        out_specs=(pl.BlockSpec(memory_space=pltpu.HBM),) * 2,
        scratch_shapes=[
            pltpu.VMEM((width, tok), BF16),
            pltpu.VMEM((width, tok), BF16),
            pltpu.VMEM((blocks, dim, tok), BF16),
            pltpu.VMEM((width, tok), F32),
            pltpu.VMEM((blocks, tok, dim), F32),
            pltpu.VMEM((blocks, tok, dim), F32),
            pltpu.VMEM((heads, tok), F32),
            pltpu.VMEM((heads, tok), F32),
            pltpu.VMEM((tok, tok), F32),
            pltpu.SMEM((blocks + 1,), jnp.int32),
            pltpu.SMEM((8,), jnp.int32),
            pltpu.SMEM((blocks,), jnp.int32),
            pltpu.VMEM(q.shape, BF16),
            pltpu.VMEM(do.shape, BF16),
            pltpu.VMEM(delta.shape, F32),
            pltpu.VMEM(k.shape, BF16),
            pltpu.VMEM(v.shape, BF16),
            pltpu.SemaphoreType.DMA((5,)),
            pltpu.VMEM(q.shape, BF16),
            pltpu.VMEM((2,) + k.shape, BF16),
            pltpu.SemaphoreType.DMA((sets,)),
            pltpu.SemaphoreType.DMA((2, blocks)),
        ],
        compiler_params=pltpu.CompilerParams(vmem_limit_bytes=59 * 2**20),
        name="attention",
    )(lengths, spans, q, do, delta, k, v)


class Place:
    def __init__(self, with_dp):
        y = lax.axis_index("dp")
        me = lax.axis_index("ctx")
        z, x, c = me // 8, lax.rem(me // 2, 4), lax.rem(me, 2)
        self.core = c
        self.sibling = {"dp": y, "ctx": me + 1 - 2 * c}

        def at(y, z, x):
            return {"dp": y, "ctx": z * 8 + x * 2 + c}

        def low(t):
            return t + 1 - 2 * lax.rem(t, 2)

        self.bits = split_axis(z) + split_axis(x)
        self.partners = (at(y, 3 - z, x), at(y, low(z), x), at(y, z, 3 - x), at(y, z, low(x)))
        if with_dp:
            self.bits = split_axis(y) + self.bits
            self.partners = (at(3 - y, z, x), at(low(y), z, x)) + self.partners
        self.dims = len(self.bits)

    def greet(self):
        barrier = pltpu.get_barrier_semaphore()
        everyone = (self.sibling,) + self.partners
        for other in everyone:
            pl.semaphore_signal(barrier, inc=1, device_id=other, device_id_type=MESH)
        pl.semaphore_wait(barrier, len(everyone))

    def spot(self, free, flipped=None):
        found = []
        for d in range(self.dims):
            if d in free:
                found.append(slice(None))
            elif d == flipped:
                found.append(1 - self.bits[d])
            else:
                found.append(self.bits[d])
        return tuple(found)


def remote(src, dst, send, recv, to):
    return pltpu.make_async_remote_copy(
        src_ref=src, dst_ref=dst, send_sem=send, recv_sem=recv, device_id=to, device_id_type=MESH
    )


def turns(dims, start):
    return [(start + s) % dims for s in range(dims)]


def gather_kernel(k_ref, v_ref, q_ref, do_ref, o_ref, x_ref,
                  k_all, v_all, q_two, do_two, delta_two, xt_two,
                  x_buf, do_buf, o_buf, xt_buf, delta_buf,
                  hop_send, hop_recv, pass_send, pass_recv, side_send, side_recv, local_sem):
    tok, dim = k_ref.shape
    half = q_two.shape[2]
    here = Place(False)
    c = here.core
    dims = here.dims
    quarter = tok // dims
    sources, targets = (k_ref, v_ref), (k_all, v_all)

    loads = [
        pltpu.make_async_copy(do_ref, do_buf, local_sem.at[0]),
        pltpu.make_async_copy(o_ref, o_buf, local_sem.at[1]),
        pltpu.make_async_copy(x_ref, x_buf, local_sem.at[2]),
    ]
    keeps = [
        pltpu.make_async_copy(k_ref, k_all.at[here.bits + (c,)], local_sem.at[3]),
        pltpu.make_async_copy(v_ref, v_all.at[here.bits + (c,)], local_sem.at[4]),
        pltpu.make_async_copy(q_ref.at[:, pl.ds(c * half, half)], q_two.at[c], local_sem.at[5]),
        pltpu.make_async_copy(do_ref.at[:, pl.ds(c * half, half)], do_two.at[c], local_sem.at[6]),
    ]
    for copy in loads + keeps:
        copy.start()
    here.greet()

    def rows(p):
        return (pl.ds(p * quarter, quarter), slice(None))

    hops = {}
    for p in range(dims):
        for kind in range(2):
            n = (p * dims) * 2 + kind
            hops[p, 0, kind] = remote(
                sources[kind].at[rows(p)],
                targets[kind].at[here.bits + (c,) + rows(p)],
                hop_send.at[n], hop_recv.at[n], here.partners[turns(dims, p)[0]],
            )
            hops[p, 0, kind].start()
    sides = []
    to_side = [
        (k_ref, k_all.at[here.bits + (c,)]),
        (v_ref, v_all.at[here.bits + (c,)]),
        (q_ref.at[:, pl.ds((1 - c) * half, half)], q_two.at[c]),
        (do_ref.at[:, pl.ds((1 - c) * half, half)], do_two.at[c]),
    ]

    def aside(src, dst):
        n = len(sides)
        sides.append(remote(src, dst, side_send.at[n], side_recv.at[n], here.sibling))
        sides[-1].start()

    for src, dst in to_side:
        aside(src, dst)

    passes = []

    def hand_on(p, s):
        order = turns(dims, p)
        for kind in range(2):
            n = (p * dims + s) * 2 + kind
            hops[p, s, kind].wait_recv()
            part = targets[kind].at[here.spot(order[:s], order[s]) + (c,) + rows(p)]
            copy = remote(part, part, pass_send.at[n], pass_recv.at[n], here.sibling)
            copy.start()
            passes.append(copy)

    def hop(p, s):
        order = turns(dims, p)
        for kind in range(2):
            n = (p * dims + s) * 2 + kind
            part = targets[kind].at[here.spot(order[:s]) + (c,) + rows(p)]
            hops[p, s, kind] = remote(
                part, part, hop_send.at[n], hop_recv.at[n], here.partners[order[s]]
            )
            hops[p, s, kind].start()

    for copy in keeps:
        copy.wait()

    loads[0].wait()
    loads[1].wait()
    heads = half // dim
    for h in range(2 * heads):
        cols = pl.ds(h * dim, dim)
        products = do_buf[:, cols].astype(F32) * o_buf[:, cols].astype(F32)
        delta_buf[h // heads, pl.ds(h % heads, 1), :] = jnp.sum(products.T, axis=0, keepdims=True)
    for h in range(heads, delta_buf.shape[1]):
        delta_buf[:, pl.ds(h, 1), :] = jnp.zeros((2, 1, tok), F32)
    own_delta = pltpu.make_async_copy(delta_buf.at[c], delta_two.at[c], local_sem.at[7])
    own_delta.start()
    aside(delta_buf.at[1 - c], delta_two.at[c])

    for p in range(dims):
        hand_on(p, 0)
        hop(p, 1)
    loads[2].wait()

    def turn(i, carry):
        xt_buf[pl.ds(i * 128, 128), :] = x_buf[:, pl.ds(i * 128, 128)].T
        return carry

    steps = x_ref.shape[1] // 128
    lax.fori_loop(0, steps // 2, turn, 0)
    for p in range(dims):
        hand_on(p, 1)
        hop(p, 2)
    lax.fori_loop(steps // 2, steps, turn, 0)
    mine = xt_two.at[:, pl.ds(c * tok, tok)]
    own_xt = pltpu.make_async_copy(xt_buf, mine, local_sem.at[8])
    own_xt.start()
    for p in range(dims):
        hand_on(p, 2)
        hop(p, 3)
    aside(xt_buf, mine)
    for p in range(dims):
        hand_on(p, 3)
    own_delta.wait()
    own_xt.wait()
    for copy in hops.values():
        copy.wait_send()
    for copy in passes:
        copy.wait()
    for copy in sides:
        copy.wait()


def gather(k, v, q, do, o, x):
    tok, dim = k.shape
    half = q.shape[1] // 2
    anywhere = pl.BlockSpec(memory_space=pltpu.HBM)
    dma = pltpu.SemaphoreType.DMA
    full = jax.ShapeDtypeStruct((2, 2, 2, 2, 2, tok, dim), BF16)
    return pl.pallas_call(
        gather_kernel,
        out_shape=(
            full, full,
            jax.ShapeDtypeStruct((2, tok, half), BF16),
            jax.ShapeDtypeStruct((2, tok, half), BF16),
            jax.ShapeDtypeStruct((2, 8, tok), F32),
            jax.ShapeDtypeStruct((x.shape[1], 2 * tok), BF16),
        ),
        in_specs=[anywhere] * 6,
        out_specs=(anywhere,) * 6,
        scratch_shapes=[
            pltpu.VMEM(x.shape, BF16),
            pltpu.VMEM(q.shape, BF16),
            pltpu.VMEM(q.shape, BF16),
            pltpu.VMEM((x.shape[1], tok), BF16),
            pltpu.VMEM((2, 8, tok), F32),
            dma((32,)), dma((32,)), dma((32,)), dma((32,)), dma((6,)), dma((6,)), dma((9,)),
        ],
        compiler_params=pltpu.CompilerParams(
            collective_id=1, has_side_effects=True, vmem_limit_bytes=59 * 2**20
        ),
        name="gather",
    )(k, v, q, do, o, x)


def wide_parts(rows, cols):
    cut = cols // 4 * 3
    quarter, half = rows // 4, rows // 2
    return [(i * quarter, quarter, 0, cut) for i in range(4)] + [
        (i * half, half, cut, cols - cut) for i in range(2)
    ]


def thin_parts(rows, cols):
    return [(i * (rows // 4), rows // 4, 0, cols) for i in range(4)]


class Halving:
    def __init__(self, here, acc, parts, orders, landing, send, recv):
        self.here, self.acc, self.parts, self.orders = here, acc, parts, orders
        self.landing, self.send_sem, self.recv_sem = landing, send, recv
        self.copies = {}

    def index(self, p, s, flip):
        r0, nr, c0, nc = self.parts[p]
        order = self.orders[p]
        free = order[s + 1:]
        d = order[s]
        return self.here.spot(free, d if flip else None) + self.cut(r0, nr, c0, nc)

    def cut(self, r0, nr, c0, nc):
        return (slice(None),) * (len(self.acc.shape) - self.here.dims - 2) + (
            pl.ds(r0, nr), pl.ds(c0, nc))

    def send(self, p, s):
        dims = self.here.dims
        n = p * dims + s
        copy = remote(
            self.acc.at[self.index(p, s, True)], self.landing[n],
            self.send_sem.at[n], self.recv_sem.at[n], self.here.partners[self.orders[p][s]],
        )
        copy.start()
        self.copies[p, s] = copy

    def total(self, p, s):
        self.copies[p, s].wait_recv()
        n = p * self.here.dims + s
        return self.acc[self.index(p, s, False)].astype(F32) + self.landing[n][...].astype(F32)

    def add(self, p, s):
        self.acc[self.index(p, s, False)] = self.total(p, s).astype(self.acc.dtype)

    def finish(self):
        for copy in self.copies.values():
            copy.wait_send()


def landing_shapes(parts, orders, extra):
    shapes = []
    for (_, nr, _, nc), order in zip(parts, orders):
        for s in range(len(order)):
            shapes.append((2,) * (len(order) - 1 - s) + extra + (nr, nc))
    return shapes


def layout(tok, dim, half, features):
    row_chunk = features // 64
    kv_parts = thin_parts(tok, dim)
    kv_orders = [turns(4, p) for p in range(4)]
    wide = wide_parts(row_chunk, half)
    wide_orders = [turns(6, p) for p in range(6)]
    thin = thin_parts(row_chunk, dim)
    thin_orders = [turns(6, p) for p in (0, 2, 3, 5)]
    return row_chunk, kv_parts, kv_orders, wide, wide_orders, thin, thin_orders


def reduce_kernel(plan, scale, dkv_ref, dq_ref, xt_ref, qg_ref, kvg_ref, wg_ref, *scratch):
    row_chunk, kv_parts, kv_orders, wide, wide_orders, thin, thin_orders = plan
    (kv_acc, kv_in, kv_mine, w_acc, t_acc, xt, dq, fin, kv_send, kv_recv, w_send, w_recv, t_send, t_recv,
     side_send, side_recv, local_sem) = scratch[:17]
    landing = scratch[17:]
    tok, dim = dkv_ref.shape[-2:]
    half = dq_ref.shape[2]
    here_w = Place(True)
    here = Place(False)
    c = here.core
    n_kv, n_w = 16, 36
    kv = Halving(here, kv_acc, kv_parts, kv_orders, landing[:n_kv], kv_send, kv_recv)
    w = Halving(here_w, w_acc, wide, wide_orders, landing[n_kv:n_kv + n_w], w_send, w_recv)
    t = Halving(here_w, t_acc, thin, thin_orders, landing[n_kv + n_w:], t_send, t_recv)

    own_q = pltpu.make_async_copy(dq_ref.at[c], qg_ref.at[:, pl.ds(c * half, half)], local_sem.at[3])
    own_q.start()
    load_x = pltpu.make_async_copy(xt_ref, xt, local_sem.at[1])
    load_x.start()
    load_q = pltpu.make_async_copy(dq_ref, dq, local_sem.at[0])
    load_q.start()
    load_kv = pltpu.make_async_copy(dkv_ref.at[c], kv_acc, local_sem.at[2])
    load_kv.start()
    here_w.greet()
    sides = []

    def aside(src, dst):
        n = len(sides)
        sides.append(remote(src, dst, side_send.at[n], side_recv.at[n], here.sibling))
        sides[-1].start()

    rest = (slice(None),) * 5
    for p in range(4):
        r0, nr, _, _ = kv_parts[p]
        aside(dkv_ref.at[(1 - c,) + rest + (pl.ds(r0, nr),)], kv_in.at[rest + (pl.ds(r0, nr),)])
    aside(dq_ref.at[1 - c], qg_ref.at[:, pl.ds(c * half, half)])

    load_kv.wait()
    for p in range(4):
        r0, nr, _, _ = kv_parts[p]
        sides[p].wait_recv()

        def join(i, carry, r0=r0, nr=nr):
            at = (i // 8, lax.rem(i // 4, 2), lax.rem(i // 2, 2), lax.rem(i, 2), slice(None), pl.ds(r0, nr))
            kv_acc[at] = (kv_acc[at].astype(F32) + kv_in[at].astype(F32)).astype(BF16)
            return carry

        lax.fori_loop(0, 16, join, 0)
        kv.send(p, 0)

    def products(i, right, acc):
        block = dot(xt[pl.ds(i * 8 * row_chunk, 8 * row_chunk), :], right).astype(BF16)
        y = i // 2
        for j in range(8):
            z = 2 * lax.rem(i, 2) + j // 4
            x = j % 4
            at = split_axis(y) + split_axis(z) + (x // 2, (x + x // 2) % 2)
            acc[at] = block[j * row_chunk:(j + 1) * row_chunk]

    load_x.wait()
    load_q.wait()
    both = dq[...].reshape(2 * tok, half)

    def wide_products(i, carry):
        products(i, both, w_acc)
        return carry

    lax.fori_loop(0, 8, wide_products, 0)
    for p in range(6):
        w.send(p, 0)
    for s in range(1, 4):
        for p in range(4):
            kv.add(p, s - 1)
            kv.send(p, s)
    kv_scale = jnp.where(c == 0, scale, 1.0).astype(F32)
    for p in range(4):
        r0, nr, _, _ = kv_parts[p]
        kv_mine[:, pl.ds(r0, nr), :] = (kv.total(p, 3) * kv_scale).astype(BF16)
    own_kv = pltpu.make_async_copy(kv_mine.at[c], kvg_ref.at[c], local_sem.at[4])
    own_kv.start()
    aside(kv_mine.at[1 - c], kvg_ref.at[c])
    mine = kv_mine[...].reshape(2 * tok, dim)

    def thin_products(i, carry):
        products(i, mine, t_acc)
        return carry

    lax.fori_loop(0, 8, thin_products, 0)
    for p in range(4):
        t.send(p, 0)
    for s in range(1, 6):
        for p in range(6):
            w.add(p, s - 1)
            w.send(p, s)
        for p in range(4):
            t.add(p, s - 1)
            t.send(p, s)
    for p, (r0, nr, c0, nc) in enumerate(wide):
        fin[pl.ds(r0, nr), pl.ds(c0, nc)] = w.total(p, 5)
    for p, (r0, nr, c0, nc) in enumerate(thin):
        fin[pl.ds(r0, nr), pl.ds(half, nc)] = t.total(p, 5)
    rows_out = row_chunk // 2
    pieces = [(0, c * half, half), (half, 2 * half + c * dim, dim)]
    own_w = []
    for n, (src, dst, width) in enumerate(pieces):
        own_w.append(pltpu.make_async_copy(
            fin.at[pl.ds(c * rows_out, rows_out), pl.ds(src, width)],
            wg_ref.at[:, pl.ds(dst, width)], local_sem.at[5 + n]))
        own_w[-1].start()
        aside(fin.at[pl.ds((1 - c) * rows_out, rows_out), pl.ds(src, width)],
              wg_ref.at[:, pl.ds(dst, width)])
    own_q.wait()
    own_kv.wait()
    for copy in own_w:
        copy.wait()
    for n, copy in enumerate(sides):
        copy.wait_send()
        if n >= 4:
            copy.wait_recv()
    kv.finish()
    w.finish()
    t.finish()


def reduce(dkv, dq, xt, scale):
    tok, dim = dkv.shape[-2:]
    half = dq.shape[2]
    features = xt.shape[0]
    plan = layout(tok, dim, half, features)
    row_chunk, kv_parts, kv_orders, wide, wide_orders, thin, thin_orders = plan
    dma = pltpu.SemaphoreType.DMA
    shapes = (landing_shapes(kv_parts, kv_orders, (2,)) + landing_shapes(wide, wide_orders, ())
              + landing_shapes(thin, thin_orders, ()))
    return pl.pallas_call(
        functools.partial(reduce_kernel, plan, scale),
        out_shape=(
            jax.ShapeDtypeStruct((tok, 2 * half), BF16),
            jax.ShapeDtypeStruct((2, tok, dim), BF16),
            jax.ShapeDtypeStruct((row_chunk // 2, 2 * half + 2 * dim), F32),
        ),
        in_specs=[pl.BlockSpec(memory_space=pltpu.HBM)] * 3,
        out_specs=(pl.BlockSpec(memory_space=pltpu.HBM),) * 3,
        scratch_shapes=[
            pltpu.VMEM(dkv.shape[1:], BF16),
            pltpu.VMEM(dkv.shape[1:], BF16),
            pltpu.VMEM((2, tok, dim), BF16),
            pltpu.VMEM((2,) * 6 + (row_chunk, half), BF16),
            pltpu.VMEM((2,) * 6 + (row_chunk, dim), BF16),
            pltpu.VMEM(xt.shape, BF16),
            pltpu.VMEM(dq.shape, BF16),
            pltpu.VMEM((row_chunk, half + dim), F32),
            dma((16,)), dma((16,)), dma((36,)), dma((36,)), dma((24,)), dma((24,)),
            dma((8,)), dma((8,)), dma((8,)),
        ] + [pltpu.VMEM(shape, BF16) for shape in shapes],
        compiler_params=pltpu.CompilerParams(
            collective_id=2, has_side_effects=True, vmem_limit_bytes=58 * 2**20
        ),
        name="reduce",
    )(dkv, dq, xt)


def finish_kernel(qg_ref, kvg_ref, wg_ref, q_out, k_out, v_out, w_out, sems):
    pairs = ((qg_ref, q_out.at[0]), (kvg_ref.at[0], k_out.at[0]), (kvg_ref.at[1], v_out.at[0]), (wg_ref, w_out))
    copies = [pltpu.make_async_copy(src, dst, sems.at[n]) for n, (src, dst) in enumerate(pairs)]
    for copy in copies:
        copy.start()
    for copy in copies:
        copy.wait()


def finish(qg, kvg, wg):
    hbm = pl.BlockSpec(memory_space=pltpu.HBM)
    one = jax.ShapeDtypeStruct((1,) + kvg.shape[1:], BF16)
    return pl.pallas_call(
        finish_kernel,
        out_shape=(jax.ShapeDtypeStruct((1,) + qg.shape, BF16), one, one, jax.ShapeDtypeStruct(wg.shape, F32)),
        in_specs=[hbm] * 3,
        out_specs=(hbm,) * 4,
        scratch_shapes=[pltpu.SemaphoreType.DMA((4,))],
        compiler_params=pltpu.CompilerParams(vmem_limit_bytes=60 * 2**20),
        name="finish",
    )(qg, kvg, wg)


def local(
    queries, key_rows, value_rows, forward_out, out_grad, layer_input, doc_lengths, held_span
):
    tok = queries.shape[1]
    dim = key_rows.shape[2]
    k, v, q, do, delta, xt = gather(
        key_rows[0], value_rows[0], queries[0], out_grad[0], forward_out[0], layer_input[0]
    )
    dq, dkv = attention(
        doc_lengths, held_span, q, do, delta, k.reshape(-1, tok, dim), v.reshape(-1, tok, dim)
    )
    dkv = dkv.reshape(2, 2, 2, 2, 2, 2, tok, dim)
    return finish(*reduce(dkv, dq, xt, 1.0 / math.sqrt(dim)))


def solution(mesh):
    row = P("dp", "ctx", None)
    flat = P("dp", None)
    return jax.shard_map(
        local, mesh=mesh, in_specs=(row,) * 6 + (flat,) * 2,
        out_specs=(row, row, row, P(("dp", "ctx"), None)), check_vma=False,
    )
```

```python
import functools, math
import jax, jax.numpy as jnp
from jax import lax
from jax.experimental import pallas as pl
from jax.experimental.pallas import tpu as pltpu
from jax.sharding import PartitionSpec as P

F32 = jnp.float32
BF16 = jnp.bfloat16
MESH = pl.DeviceIdType.MESH
NEG = -1e30


def dot(a, b):
    return jnp.dot(a, b, preferred_element_type=F32)


def split_axis(t):
    return t // 2, lax.rem(t + t // 2, 2)


def join_bits(bits):
    return ((bits[0] * 2 + bits[1]) * 2 + bits[2]) * 2 + bits[3]


def attention_kernel(sets, heads, tok, dim, blocks,
                     lengths_ref, span_ref,
                     q_in, do_in, delta_in, k_in, v_in,
                     dq_out, dkv_out,
                     qt, dot_, kt, dqt, dka, dva, stat_m, stat_l, bias, seen,
                     ends_ref, held_ref, q_ref, do_ref, delta_ref, k_ref, v_ref, loads,
                     dq_ref, dkv_ref, q_stores, kv_stores):
    logit_scale = 1.0 / math.sqrt(dim)
    log2_scale = logit_scale * math.log2(math.e)

    pairs = ((q_in, q_ref), (do_in, do_ref), (delta_in, delta_ref), (k_in, k_ref), (v_in, v_ref))
    copies = [pltpu.make_async_copy(src, dst, loads.at[n]) for n, (src, dst) in enumerate(pairs)]
    for copy in copies:
        copy.start()
    me = lax.axis_index("ctx")
    own_chip = join_bits(split_axis(me // 8) + split_axis(lax.rem(me // 2, 4)))
    doc_count = lengths_ref.shape[1]
    end = jnp.int32(0)
    for d in range(doc_count):
        end = end + lengths_ref[0, d]
        ends_ref[d] = end

    def place(i, carry):
        chip = join_bits(split_axis(i // 8) + split_axis(lax.rem(i // 2, 4)))
        held_ref[2 * chip + lax.rem(i, 2)] = span_ref[0, i]
        return carry

    lax.fori_loop(0, blocks, place, 0)
    dka[...] = jnp.zeros_like(dka)
    dva[...] = jnp.zeros_like(dva)
    for copy in copies:
        copy.wait()

    for rs in range(sets):
        own = 2 * own_chip + rs
        span = held_ref[own]
        first = span * tok

        def count(d, lo):
            end = ends_ref[d]
            return jnp.where(end <= first, jnp.maximum(lo, end), lo)

        lo_first = lax.fori_loop(0, doc_count, count, jnp.int32(0))
        seen[0] = own

        def collect(b, n):
            h = held_ref[b]
            take = (h < span) & (h * tok + (tok - 1) >= lo_first)

            @pl.when(take)
            def _():
                seen[n] = b

            return n + take.astype(jnp.int32)

        total = lax.fori_loop(0, blocks, collect, jnp.int32(1))
        for h in range(heads):
            rows = pl.ds(h * dim, dim)
            qt[rows, :] = q_ref[rs, :, rows].T
            dot_[rows, :] = do_ref[rs, :, rows].T
        pos = first + lax.broadcasted_iota(jnp.int32, (1, tok), 1)
        low = jnp.zeros((1, tok), jnp.int32)
        for d in range(doc_count):
            end = ends_ref[d]
            low = jnp.where(pos >= end, jnp.maximum(low, end), low)

        stat_m[...] = jnp.full_like(stat_m, NEG)
        stat_l[...] = jnp.zeros_like(stat_l)
        dqt[...] = jnp.zeros_like(dqt)

        def set_bias(b):
            kp = held_ref[b] * tok + lax.broadcasted_iota(jnp.int32, (tok, tok), 0)
            bias[...] = jnp.where((kp >= low) & (kp <= pos), 0.0, NEG)

        def pass_one(i, carry):
            b = seen[i]
            set_bias(b)
            k = k_ref[b]
            kt[b] = k.T
            for h in range(heads):
                s = dot(k, qt[pl.ds(h * dim, dim), :]) * log2_scale + bias[...]
                m_old = stat_m[pl.ds(h, 1), :]
                m_new = jnp.maximum(m_old, jnp.max(s, axis=0, keepdims=True))
                add = jnp.sum(jnp.exp2(s - m_new), axis=0, keepdims=True)
                stat_l[pl.ds(h, 1), :] = stat_l[pl.ds(h, 1), :] * jnp.exp2(m_old - m_new) + add
                stat_m[pl.ds(h, 1), :] = m_new
            return carry

        lax.fori_loop(0, total, pass_one, 0)
        stat_m[...] = stat_m[...] + jnp.log2(stat_l[...])

        def pass_two(i, carry):
            b = seen[i]
            set_bias(b)
            k = k_ref[b]
            v = v_ref[b]
            ktb = kt[b]
            dk = dka[b]
            dv = dva[b]
            for h in range(heads):
                rows = pl.ds(h * dim, dim)
                s = dot(k, qt[rows, :]) * log2_scale + bias[...]
                p = jnp.exp2(s - stat_m[pl.ds(h, 1), :])
                dp = dot(v, dot_[rows, :])
                ds = (p * (dp - delta_ref[rs, pl.ds(h, 1), :])).astype(BF16)
                dv = dv + dot(p.astype(BF16), do_ref[rs, :, rows])
                dk = dk + dot(ds, q_ref[rs, :, rows])
                dqt[rows, :] += dot(ktb, ds)
            dka[b] = dk
            dva[b] = dv
            return carry

        lax.fori_loop(0, total, pass_two, 0)
        for h in range(heads):
            rows = pl.ds(h * dim, dim)
            dq_ref[rs, :, rows] = (logit_scale * dqt[rows, :]).T.astype(BF16)
        pltpu.make_async_copy(dq_ref.at[rs], dq_out.at[rs], q_stores.at[rs]).start()

    def write(b, carry):
        for kind, acc in enumerate((dka, dva)):
            dkv_ref[kind, b] = acc[b].astype(BF16)
            store(kind, b).start()
        return carry

    def store(kind, b):
        return pltpu.make_async_copy(dkv_ref.at[kind, b], dkv_out.at[kind, b], kv_stores.at[kind, b])

    def stored(b, carry):
        store(0, b).wait()
        store(1, b).wait()
        return carry

    lax.fori_loop(0, blocks, write, 0)
    lax.fori_loop(0, blocks, stored, 0)
    for rs in range(sets):
        pltpu.make_async_copy(dq_ref.at[rs], dq_out.at[rs], q_stores.at[rs]).wait()


def attention(lengths, spans, q, do, delta, k, v):
    sets, tok, width = q.shape
    blocks, _, dim = k.shape
    heads = width // dim
    smem = pl.BlockSpec(memory_space=pltpu.SMEM)
    return pl.pallas_call(
        functools.partial(attention_kernel, sets, heads, tok, dim, blocks),
        out_shape=(
            jax.ShapeDtypeStruct(q.shape, BF16),
            jax.ShapeDtypeStruct((2,) + k.shape, BF16),
        ),
        in_specs=[smem, smem] + [pl.BlockSpec(memory_space=pltpu.HBM)] * 5,
        out_specs=(pl.BlockSpec(memory_space=pltpu.HBM),) * 2,
        scratch_shapes=[
            pltpu.VMEM((width, tok), BF16),
            pltpu.VMEM((width, tok), BF16),
            pltpu.VMEM((blocks, dim, tok), BF16),
            pltpu.VMEM((width, tok), F32),
            pltpu.VMEM((blocks, tok, dim), F32),
            pltpu.VMEM((blocks, tok, dim), F32),
            pltpu.VMEM((heads, tok), F32),
            pltpu.VMEM((heads, tok), F32),
            pltpu.VMEM((tok, tok), F32),
            pltpu.SMEM((blocks + 1,), jnp.int32),
            pltpu.SMEM((8,), jnp.int32),
            pltpu.SMEM((blocks,), jnp.int32),
            pltpu.VMEM(q.shape, BF16),
            pltpu.VMEM(do.shape, BF16),
            pltpu.VMEM(delta.shape, F32),
            pltpu.VMEM(k.shape, BF16),
            pltpu.VMEM(v.shape, BF16),
            pltpu.SemaphoreType.DMA((5,)),
            pltpu.VMEM(q.shape, BF16),
            pltpu.VMEM((2,) + k.shape, BF16),
            pltpu.SemaphoreType.DMA((sets,)),
            pltpu.SemaphoreType.DMA((2, blocks)),
        ],
        compiler_params=pltpu.CompilerParams(vmem_limit_bytes=59 * 2**20),
        name="attention",
    )(lengths, spans, q, do, delta, k, v)


class Place:
    def __init__(self, with_dp):
        y = lax.axis_index("dp")
        me = lax.axis_index("ctx")
        z, x, c = me // 8, lax.rem(me // 2, 4), lax.rem(me, 2)
        self.core = c
        self.sibling = {"dp": y, "ctx": me + 1 - 2 * c}

        def at(y, z, x):
            return {"dp": y, "ctx": z * 8 + x * 2 + c}

        def low(t):
            return t + 1 - 2 * lax.rem(t, 2)

        self.bits = split_axis(z) + split_axis(x)
        self.partners = (at(y, 3 - z, x), at(y, low(z), x), at(y, z, 3 - x), at(y, z, low(x)))
        if with_dp:
            self.bits = split_axis(y) + self.bits
            self.partners = (at(3 - y, z, x), at(low(y), z, x)) + self.partners
        self.dims = len(self.bits)

    def greet(self):
        barrier = pltpu.get_barrier_semaphore()
        everyone = (self.sibling,) + self.partners
        for other in everyone:
            pl.semaphore_signal(barrier, inc=1, device_id=other, device_id_type=MESH)
        pl.semaphore_wait(barrier, len(everyone))

    def spot(self, free, flipped=None):
        found = []
        for d in range(self.dims):
            if d in free:
                found.append(slice(None))
            elif d == flipped:
                found.append(1 - self.bits[d])
            else:
                found.append(self.bits[d])
        return tuple(found)


def remote(src, dst, send, recv, to):
    return pltpu.make_async_remote_copy(
        src_ref=src, dst_ref=dst, send_sem=send, recv_sem=recv, device_id=to, device_id_type=MESH
    )


def turns(dims, start):
    return [(start + s) % dims for s in range(dims)]


def gather_kernel(k_ref, v_ref, q_ref, do_ref, o_ref, x_ref,
                  k_out, v_out, q_two, do_two, delta_two, xt_two,
                  k_all, v_all, q_buf, x_buf, do_buf, o_buf, xt_buf, delta_buf,
                  hop_send, hop_recv, pass_send, pass_recv, side_send, side_recv, local_sem):
    tok, dim = k_ref.shape
    half = q_two.shape[2]
    here = Place(False)
    c = here.core
    dims = here.dims
    quarter = tok // dims
    sources, targets = (k_ref, v_ref), (k_all, v_all)

    own_k, own_v = k_all.at[here.bits + (c,)], v_all.at[here.bits + (c,)]
    loads = [
        pltpu.make_async_copy(src, dst, local_sem.at[n])
        for n, (src, dst) in enumerate((
            (k_ref, own_k), (v_ref, own_v), (q_ref, q_buf), (do_ref, do_buf), (o_ref, o_buf), (x_ref, x_buf)))
    ]
    for copy in loads:
        copy.start()
    here.greet()

    def rows(p):
        return (pl.ds(p * quarter, quarter), slice(None))

    hops = {}
    for p in range(dims):
        for kind in range(2):
            n = (p * dims) * 2 + kind
            hops[p, 0, kind] = remote(
                sources[kind].at[rows(p)],
                targets[kind].at[here.bits + (c,) + rows(p)],
                hop_send.at[n], hop_recv.at[n], here.partners[turns(dims, p)[0]],
            )
            hops[p, 0, kind].start()
    sides = []
    def aside(src, dst):
        n = len(sides)
        sides.append(remote(src, dst, side_send.at[n], side_recv.at[n], here.sibling))
        sides[-1].start()

    for copy in loads[:5]:
        copy.wait()
    theirs, mine = pl.ds((1 - c) * half, half), pl.ds(c * half, half)
    aside(own_k, own_k)
    aside(own_v, own_v)
    aside(q_buf.at[:, theirs], q_two.at[c])
    aside(do_buf.at[:, theirs], do_two.at[c])
    keeps = []

    def keep(src, dst):
        keeps.append(pltpu.make_async_copy(src, dst, local_sem.at[6 + len(keeps)]))
        keeps[-1].start()

    keep(q_buf.at[:, mine], q_two.at[c])
    keep(do_buf.at[:, mine], do_two.at[c])

    passes = []

    def hand_on(p, s):
        order = turns(dims, p)
        for kind in range(2):
            n = (p * dims + s) * 2 + kind
            hops[p, s, kind].wait_recv()
            part = targets[kind].at[here.spot(order[:s], order[s]) + (c,) + rows(p)]
            copy = remote(part, part, pass_send.at[n], pass_recv.at[n], here.sibling)
            copy.start()
            passes.append(copy)

    def hop(p, s):
        order = turns(dims, p)
        for kind in range(2):
            n = (p * dims + s) * 2 + kind
            part = targets[kind].at[here.spot(order[:s]) + (c,) + rows(p)]
            hops[p, s, kind] = remote(
                part, part, hop_send.at[n], hop_recv.at[n], here.partners[order[s]]
            )
            hops[p, s, kind].start()

    heads = half // dim
    for h in range(2 * heads):
        cols = pl.ds(h * dim, dim)
        products = do_buf[:, cols].astype(F32) * o_buf[:, cols].astype(F32)
        delta_buf[h // heads, pl.ds(h % heads, 1), :] = jnp.sum(products.T, axis=0, keepdims=True)
    for h in range(heads, delta_buf.shape[1]):
        delta_buf[:, pl.ds(h, 1), :] = jnp.zeros((2, 1, tok), F32)
    keep(delta_buf.at[c], delta_two.at[c])
    aside(delta_buf.at[1 - c], delta_two.at[c])

    for p in range(dims):
        hand_on(p, 0)
        hop(p, 1)
    loads[5].wait()

    def turn(i, carry):
        xt_buf[pl.ds(i * 128, 128), :] = x_buf[:, pl.ds(i * 128, 128)].T
        return carry

    steps = x_ref.shape[1] // 128
    lax.fori_loop(0, steps // 2, turn, 0)
    for p in range(dims):
        hand_on(p, 1)
        hop(p, 2)
    lax.fori_loop(steps // 2, steps, turn, 0)
    mine = xt_two.at[:, pl.ds(c * tok, tok)]
    keep(xt_buf, mine)
    for p in range(dims):
        hand_on(p, 2)
        hop(p, 3)
    aside(xt_buf, mine)
    for p in range(dims):
        hand_on(p, 3)
    everywhere = (slice(None),) * dims
    keep(k_all.at[everywhere + (c,)], k_out.at[everywhere + (c,)])
    keep(v_all.at[everywhere + (c,)], v_out.at[everywhere + (c,)])
    for copy in passes:
        copy.wait()
    for copy in sides:
        copy.wait()
    keep(k_all.at[everywhere + (1 - c,)], k_out.at[everywhere + (1 - c,)])
    keep(v_all.at[everywhere + (1 - c,)], v_out.at[everywhere + (1 - c,)])
    for copy in hops.values():
        copy.wait_send()
    for copy in keeps:
        copy.wait()


def gather(k, v, q, do, o, x):
    tok, dim = k.shape
    half = q.shape[1] // 2
    anywhere = pl.BlockSpec(memory_space=pltpu.HBM)
    dma = pltpu.SemaphoreType.DMA
    full = jax.ShapeDtypeStruct((2, 2, 2, 2, 2, tok, dim), BF16)
    return pl.pallas_call(
        gather_kernel,
        out_shape=(
            full, full,
            jax.ShapeDtypeStruct((2, tok, half), BF16),
            jax.ShapeDtypeStruct((2, tok, half), BF16),
            jax.ShapeDtypeStruct((2, 8, tok), F32),
            jax.ShapeDtypeStruct((x.shape[1], 2 * tok), BF16),
        ),
        in_specs=[anywhere] * 6,
        out_specs=(anywhere,) * 6,
        scratch_shapes=[
            pltpu.VMEM(full.shape, BF16),
            pltpu.VMEM(full.shape, BF16),
            pltpu.VMEM(q.shape, BF16),
            pltpu.VMEM(x.shape, BF16),
            pltpu.VMEM(q.shape, BF16),
            pltpu.VMEM(q.shape, BF16),
            pltpu.VMEM((x.shape[1], tok), BF16),
            pltpu.VMEM((2, 8, tok), F32),
            dma((32,)), dma((32,)), dma((32,)), dma((32,)), dma((6,)), dma((6,)), dma((14,)),
        ],
        compiler_params=pltpu.CompilerParams(
            collective_id=1, has_side_effects=True, vmem_limit_bytes=59 * 2**20
        ),
        name="gather",
    )(k, v, q, do, o, x)


def wide_parts(rows, cols):
    cut = cols // 4 * 3
    quarter, half = rows // 4, rows // 2
    return [(i * quarter, quarter, 0, cut) for i in range(4)] + [
        (i * half, half, cut, cols - cut) for i in range(2)
    ]


def thin_parts(rows, cols):
    return [(i * (rows // 4), rows // 4, 0, cols) for i in range(4)]


class Halving:
    def __init__(self, here, acc, parts, orders, landing, send, recv):
        self.here, self.acc, self.parts, self.orders = here, acc, parts, orders
        self.landing, self.send_sem, self.recv_sem = landing, send, recv
        self.copies = {}

    def index(self, p, s, flip):
        r0, nr, c0, nc = self.parts[p]
        order = self.orders[p]
        free = order[s + 1:]
        d = order[s]
        return self.here.spot(free, d if flip else None) + self.cut(r0, nr, c0, nc)

    def cut(self, r0, nr, c0, nc):
        return (slice(None),) * (len(self.acc.shape) - self.here.dims - 2) + (
            pl.ds(r0, nr), pl.ds(c0, nc))

    def send(self, p, s):
        dims = self.here.dims
        n = p * dims + s
        copy = remote(
            self.acc.at[self.index(p, s, True)], self.landing[n],
            self.send_sem.at[n], self.recv_sem.at[n], self.here.partners[self.orders[p][s]],
        )
        copy.start()
        self.copies[p, s] = copy

    def total(self, p, s):
        self.copies[p, s].wait_recv()
        n = p * self.here.dims + s
        return self.acc[self.index(p, s, False)].astype(F32) + self.landing[n][...].astype(F32)

    def add(self, p, s):
        self.acc[self.index(p, s, False)] = self.total(p, s).astype(self.acc.dtype)

    def finish(self):
        for copy in self.copies.values():
            copy.wait_send()


def landing_shapes(parts, orders, extra):
    shapes = []
    for (_, nr, _, nc), order in zip(parts, orders):
        for s in range(len(order)):
            shapes.append((2,) * (len(order) - 1 - s) + extra + (nr, nc))
    return shapes


def layout(tok, dim, half, features):
    row_chunk = features // 64
    kv_parts = thin_parts(tok, dim)
    kv_orders = [turns(4, p) for p in range(4)]
    wide = wide_parts(row_chunk, half)
    wide_orders = [turns(6, p) for p in range(6)]
    thin = thin_parts(row_chunk, dim)
    thin_orders = [turns(6, p) for p in (0, 2, 3, 5)]
    return row_chunk, kv_parts, kv_orders, wide, wide_orders, thin, thin_orders


def reduce_kernel(plan, scale, dkv_ref, dq_ref, xt_ref, qg_ref, kvg_ref, wg_ref, *scratch):
    row_chunk, kv_parts, kv_orders, wide, wide_orders, thin, thin_orders = plan
    (kv_acc, kv_in, kv_mine, w_acc, t_acc, xt, dq, fin, kv_send, kv_recv, w_send, w_recv, t_send, t_recv,
     side_send, side_recv, local_sem) = scratch[:17]
    landing = scratch[17:]
    tok, dim = dkv_ref.shape[-2:]
    half = dq_ref.shape[2]
    here_w = Place(True)
    here = Place(False)
    c = here.core
    n_kv, n_w = 16, 36
    kv = Halving(here, kv_acc, kv_parts, kv_orders, landing[:n_kv], kv_send, kv_recv)
    w = Halving(here_w, w_acc, wide, wide_orders, landing[n_kv:n_kv + n_w], w_send, w_recv)
    t = Halving(here_w, t_acc, thin, thin_orders, landing[n_kv + n_w:], t_send, t_recv)

    load_x = pltpu.make_async_copy(xt_ref, xt, local_sem.at[1])
    load_x.start()
    load_q = pltpu.make_async_copy(dq_ref, dq, local_sem.at[0])
    load_q.start()
    load_kv = pltpu.make_async_copy(dkv_ref.at[c], kv_acc, local_sem.at[2])
    load_kv.start()
    here_w.greet()
    sides = []

    def aside(src, dst):
        n = len(sides)
        sides.append(remote(src, dst, side_send.at[n], side_recv.at[n], here.sibling))
        sides[-1].start()

    rest = (slice(None),) * 5
    for p in range(4):
        r0, nr, _, _ = kv_parts[p]
        aside(dkv_ref.at[(1 - c,) + rest + (pl.ds(r0, nr),)], kv_in.at[rest + (pl.ds(r0, nr),)])
    aside(dq_ref.at[1 - c], qg_ref.at[:, pl.ds(c * half, half)])

    load_kv.wait()
    for p in range(4):
        r0, nr, _, _ = kv_parts[p]
        sides[p].wait_recv()

        def join(i, carry, r0=r0, nr=nr):
            at = (i // 8, lax.rem(i // 4, 2), lax.rem(i // 2, 2), lax.rem(i, 2), slice(None), pl.ds(r0, nr))
            kv_acc[at] = (kv_acc[at].astype(F32) + kv_in[at].astype(F32)).astype(BF16)
            return carry

        lax.fori_loop(0, 16, join, 0)
        kv.send(p, 0)

    def products(i, right, acc):
        block = dot(xt[pl.ds(i * 8 * row_chunk, 8 * row_chunk), :], right).astype(BF16)
        y = i // 2
        for j in range(8):
            z = 2 * lax.rem(i, 2) + j // 4
            x = j % 4
            at = split_axis(y) + split_axis(z) + (x // 2, (x + x // 2) % 2)
            acc[at] = block[j * row_chunk:(j + 1) * row_chunk]

    load_x.wait()
    load_q.wait()
    own_q = pltpu.make_async_copy(dq.at[c], qg_ref.at[:, pl.ds(c * half, half)], local_sem.at[3])
    own_q.start()
    both = dq[...].reshape(2 * tok, half)

    def wide_products(i, carry):
        products(i, both, w_acc)
        return carry

    lax.fori_loop(0, 8, wide_products, 0)
    for p in range(6):
        w.send(p, 0)
    for s in range(1, 4):
        for p in range(4):
            kv.add(p, s - 1)
            kv.send(p, s)
    kv_scale = jnp.where(c == 0, scale, 1.0).astype(F32)
    for p in range(4):
        r0, nr, _, _ = kv_parts[p]
        kv_mine[:, pl.ds(r0, nr), :] = (kv.total(p, 3) * kv_scale).astype(BF16)
    own_kv = pltpu.make_async_copy(kv_mine.at[c], kvg_ref.at[c], local_sem.at[4])
    own_kv.start()
    aside(kv_mine.at[1 - c], kvg_ref.at[c])
    mine = kv_mine[...].reshape(2 * tok, dim)

    def thin_products(i, carry):
        products(i, mine, t_acc)
        return carry

    lax.fori_loop(0, 8, thin_products, 0)
    for p in range(4):
        t.send(p, 0)
    for s in range(1, 6):
        for p in range(6):
            w.add(p, s - 1)
            w.send(p, s)
        for p in range(4):
            t.add(p, s - 1)
            t.send(p, s)
    for p, (r0, nr, c0, nc) in enumerate(wide):
        fin[pl.ds(r0, nr), pl.ds(c0, nc)] = w.total(p, 5)
    for p, (r0, nr, c0, nc) in enumerate(thin):
        fin[pl.ds(r0, nr), pl.ds(half, nc)] = t.total(p, 5)
    rows_out = row_chunk // 2
    pieces = [(0, c * half, half), (half, 2 * half + c * dim, dim)]
    own_w = []
    for n, (src, dst, width) in enumerate(pieces):
        own_w.append(pltpu.make_async_copy(
            fin.at[pl.ds(c * rows_out, rows_out), pl.ds(src, width)],
            wg_ref.at[:, pl.ds(dst, width)], local_sem.at[5 + n]))
        own_w[-1].start()
        aside(fin.at[pl.ds((1 - c) * rows_out, rows_out), pl.ds(src, width)],
              wg_ref.at[:, pl.ds(dst, width)])
    own_q.wait()
    own_kv.wait()
    for copy in own_w:
        copy.wait()
    for n, copy in enumerate(sides):
        copy.wait_send()
        if n >= 4:
            copy.wait_recv()
    kv.finish()
    w.finish()
    t.finish()


def reduce(dkv, dq, xt, scale):
    tok, dim = dkv.shape[-2:]
    half = dq.shape[2]
    features = xt.shape[0]
    plan = layout(tok, dim, half, features)
    row_chunk, kv_parts, kv_orders, wide, wide_orders, thin, thin_orders = plan
    dma = pltpu.SemaphoreType.DMA
    shapes = (landing_shapes(kv_parts, kv_orders, (2,)) + landing_shapes(wide, wide_orders, ())
              + landing_shapes(thin, thin_orders, ()))
    return pl.pallas_call(
        functools.partial(reduce_kernel, plan, scale),
        out_shape=(
            jax.ShapeDtypeStruct((tok, 2 * half), BF16),
            jax.ShapeDtypeStruct((2, tok, dim), BF16),
            jax.ShapeDtypeStruct((row_chunk // 2, 2 * half + 2 * dim), F32),
        ),
        in_specs=[pl.BlockSpec(memory_space=pltpu.HBM)] * 3,
        out_specs=(pl.BlockSpec(memory_space=pltpu.HBM),) * 3,
        scratch_shapes=[
            pltpu.VMEM(dkv.shape[1:], BF16),
            pltpu.VMEM(dkv.shape[1:], BF16),
            pltpu.VMEM((2, tok, dim), BF16),
            pltpu.VMEM((2,) * 6 + (row_chunk, half), BF16),
            pltpu.VMEM((2,) * 6 + (row_chunk, dim), BF16),
            pltpu.VMEM(xt.shape, BF16),
            pltpu.VMEM(dq.shape, BF16),
            pltpu.VMEM((row_chunk, half + dim), F32),
            dma((16,)), dma((16,)), dma((36,)), dma((36,)), dma((24,)), dma((24,)),
            dma((8,)), dma((8,)), dma((8,)),
        ] + [pltpu.VMEM(shape, BF16) for shape in shapes],
        compiler_params=pltpu.CompilerParams(
            collective_id=2, has_side_effects=True, vmem_limit_bytes=58 * 2**20
        ),
        name="reduce",
    )(dkv, dq, xt)


def finish_kernel(qg_ref, kvg_ref, wg_ref, q_out, k_out, v_out, w_out, sems):
    pairs = ((qg_ref, q_out.at[0]), (kvg_ref.at[0], k_out.at[0]), (kvg_ref.at[1], v_out.at[0]), (wg_ref, w_out))
    copies = [pltpu.make_async_copy(src, dst, sems.at[n]) for n, (src, dst) in enumerate(pairs)]
    for copy in copies:
        copy.start()
    for copy in copies:
        copy.wait()


def finish(qg, kvg, wg):
    hbm = pl.BlockSpec(memory_space=pltpu.HBM)
    one = jax.ShapeDtypeStruct((1,) + kvg.shape[1:], BF16)
    return pl.pallas_call(
        finish_kernel,
        out_shape=(jax.ShapeDtypeStruct((1,) + qg.shape, BF16), one, one, jax.ShapeDtypeStruct(wg.shape, F32)),
        in_specs=[pl.BlockSpec(memory_space=pltpu.VMEM)] * 3,
        out_specs=(hbm,) * 4,
        scratch_shapes=[pltpu.SemaphoreType.DMA((4,))],
        compiler_params=pltpu.CompilerParams(vmem_limit_bytes=59 * 2**20),
        name="finish",
    )(qg, kvg, wg)


def local(
    queries, key_rows, value_rows, forward_out, out_grad, layer_input, doc_lengths, held_span
):
    tok = queries.shape[1]
    dim = key_rows.shape[2]
    k, v, q, do, delta, xt = gather(
        key_rows[0], value_rows[0], queries[0], out_grad[0], forward_out[0], layer_input[0]
    )
    dq, dkv = attention(
        doc_lengths, held_span, q, do, delta, k.reshape(-1, tok, dim), v.reshape(-1, tok, dim)
    )
    dkv = dkv.reshape(2, 2, 2, 2, 2, 2, tok, dim)
    return finish(*reduce(dkv, dq, xt, 1.0 / math.sqrt(dim)))


def solution(mesh):
    row = P("dp", "ctx", None)
    flat = P("dp", None)
    return jax.shard_map(
        local, mesh=mesh, in_specs=(row,) * 6 + (flat,) * 2,
        out_specs=(row, row, row, P(("dp", "ctx"), None)), check_vma=False,
    )
```

```python
import functools, math
import jax, jax.numpy as jnp
from jax import lax
from jax.experimental import pallas as pl
from jax.experimental.pallas import tpu as pltpu
from jax.sharding import PartitionSpec as P

F32 = jnp.float32
BF16 = jnp.bfloat16
MESH = pl.DeviceIdType.MESH
NEG = -1e30
LONGEST = 4096


def dot(a, b):
    return jnp.dot(a, b, preferred_element_type=F32)


def split_axis(t):
    return t // 2, lax.rem(t + t // 2, 2)


def join_bits(bits):
    return ((bits[0] * 2 + bits[1]) * 2 + bits[2]) * 2 + bits[3]


def attention_kernel(sets, heads, tok, dim, blocks,
                     lengths_ref, span_ref,
                     q_in, do_in, delta_in, k_in, v_in,
                     dq_out, dkv_out,
                     qt, dot_, kt, dqt, dka, dva, stat_m, stat_l, bias, seen,
                     ends_ref, held_ref, q_ref, do_ref, delta_ref, k_ref, v_ref, loads,
                     dq_ref, dkv_ref, q_stores, kv_stores,
                     q_flat, do_flat, kept, kept_m, p_all, ds_all, marked):
    logit_scale = 1.0 / math.sqrt(dim)
    log2_scale = logit_scale * math.log2(math.e)

    pairs = ((q_in, q_ref), (do_in, do_ref), (delta_in, delta_ref), (k_in, k_ref), (v_in, v_ref))
    copies = [pltpu.make_async_copy(src, dst, loads.at[n]) for n, (src, dst) in enumerate(pairs)]
    for copy in copies:
        copy.start()
    me = lax.axis_index("ctx")
    own_chip = join_bits(split_axis(me // 8) + split_axis(lax.rem(me // 2, 4)))
    doc_count = lengths_ref.shape[1]
    end = jnp.int32(0)
    for d in range(doc_count):
        end = end + lengths_ref[0, d]
        ends_ref[d] = end

    def place(i, carry):
        chip = join_bits(split_axis(i // 8) + split_axis(lax.rem(i // 2, 4)))
        held_ref[2 * chip + lax.rem(i, 2)] = span_ref[0, i]
        return carry

    lax.fori_loop(0, blocks, place, 0)
    dka[...] = jnp.zeros_like(dka)
    dva[...] = jnp.zeros_like(dva)
    def store(kind, b):
        return pltpu.make_async_copy(dkv_ref.at[kind, b], dkv_out.at[kind, b], kv_stores.at[kind, b])

    def write(b):
        for kind, acc in enumerate((dka, dva)):
            dkv_ref[kind, b] = acc[b].astype(BF16)
            store(kind, b).start()

    for copy in copies:
        copy.wait()

    for rs in range(sets):
        own = 2 * own_chip + rs
        span = held_ref[own]
        first = span * tok

        def count(d, lo):
            end = ends_ref[d]
            return jnp.where(end <= first, jnp.maximum(lo, end), lo)

        lo_first = lax.fori_loop(0, doc_count, count, jnp.int32(0))
        seen[0] = own

        def collect(b, n):
            h = held_ref[b]
            take = (h < span) & (h * tok + (tok - 1) >= lo_first)

            @pl.when(take)
            def _():
                seen[n] = b

            return n + take.astype(jnp.int32)

        total = lax.fori_loop(0, blocks, collect, jnp.int32(1))
        last = rs == sets - 1
        if last:
            def unmark(b, carry):
                marked[b] = 0
                return carry

            def mark(i, carry):
                marked[seen[i]] = 1
                return carry

            def write_other(b, carry):
                @pl.when(marked[b] == 0)
                def _():
                    write(b)

                return carry

            lax.fori_loop(0, blocks, unmark, 0)
            lax.fori_loop(0, total, mark, 0)
            lax.fori_loop(0, blocks, write_other, 0)
        for h in range(heads):
            rows = pl.ds(h * dim, dim)
            flat = pl.ds(h * tok, tok)
            q_flat[flat, :] = q_ref[rs, :, rows]
            do_flat[flat, :] = do_ref[rs, :, rows]
            qt[:, flat] = q_flat[flat, :].T
            dot_[:, flat] = do_flat[flat, :].T
        pos = first + lax.broadcasted_iota(jnp.int32, (1, tok), 1)
        low = jnp.zeros((1, tok), jnp.int32)
        for d in range(doc_count):
            end = ends_ref[d]
            low = jnp.where(pos >= end, jnp.maximum(low, end), low)

        stat_m[...] = jnp.full_like(stat_m, NEG)
        stat_l[...] = jnp.zeros_like(stat_l)
        dqt[...] = jnp.zeros_like(dqt)

        def set_bias(b):
            kp = held_ref[b] * tok + lax.broadcasted_iota(jnp.int32, (tok, tok), 0)
            bias[...] = jnp.where((kp >= low) & (kp <= pos), 0.0, NEG)

        def pass_one(i, carry):
            b = seen[i]
            set_bias(b)
            k = k_ref[b]
            kt[b] = k.T
            for h in range(heads):
                row, cols = pl.ds(h, 1), pl.ds(h * tok, tok)
                s = dot(k, qt[:, cols]) * log2_scale + bias[...]
                m_old = stat_m[row, :]
                m_new = jnp.maximum(m_old, jnp.max(s, axis=0, keepdims=True))
                p = jnp.exp2(s - m_new)
                kept[i, :, cols] = p.astype(BF16)
                add = jnp.sum(p, axis=0, keepdims=True)
                stat_l[row, :] = stat_l[row, :] * jnp.exp2(m_old - m_new) + add
                stat_m[row, :] = m_new
                kept_m[i, row, :] = m_new
            return carry

        lax.fori_loop(0, total, pass_one, 0)
        stat_m[...] = stat_m[...] + jnp.log2(stat_l[...])

        def pass_two(i, carry):
            b = seen[i]
            v = v_ref[b]
            for h in range(heads):
                row, cols = pl.ds(h, 1), pl.ds(h * tok, tok)
                scaled = jnp.exp2(kept_m[i, row, :] - stat_m[row, :])
                p = kept[i, :, cols].astype(F32) * scaled
                dp = dot(v, dot_[:, cols])
                p_all[:, cols] = p.astype(BF16)
                ds_all[:, cols] = (p * (dp - delta_ref[rs, row, :])).astype(BF16)
            dva[b] += dot(p_all[...], do_flat[...])
            dka[b] += dot(ds_all[...], q_flat[...])
            dqt[...] += dot(kt[b], ds_all[...])
            if last:
                write(b)
            return carry

        lax.fori_loop(0, total, pass_two, 0)
        for h in range(heads):
            rows = pl.ds(h * dim, dim)
            dq_ref[rs, :, rows] = (logit_scale * dqt[:, pl.ds(h * tok, tok)]).T.astype(BF16)
        pltpu.make_async_copy(dq_ref.at[rs], dq_out.at[rs], q_stores.at[rs]).start()

    def stored(b, carry):
        store(0, b).wait()
        store(1, b).wait()
        return carry

    lax.fori_loop(0, blocks, stored, 0)
    for rs in range(sets):
        pltpu.make_async_copy(dq_ref.at[rs], dq_out.at[rs], q_stores.at[rs]).wait()


def attention(lengths, spans, q, do, delta, k, v):
    sets, tok, width = q.shape
    blocks, _, dim = k.shape
    heads = width // dim
    smem = pl.BlockSpec(memory_space=pltpu.SMEM)
    return pl.pallas_call(
        functools.partial(attention_kernel, sets, heads, tok, dim, blocks),
        out_shape=(
            jax.ShapeDtypeStruct(q.shape, BF16),
            jax.ShapeDtypeStruct((2,) + k.shape, BF16),
        ),
        in_specs=[smem, smem] + [pl.BlockSpec(memory_space=pltpu.HBM)] * 5,
        out_specs=(pl.BlockSpec(memory_space=pltpu.HBM),) * 2,
        scratch_shapes=[
            pltpu.VMEM((dim, heads * tok), BF16),
            pltpu.VMEM((dim, heads * tok), BF16),
            pltpu.VMEM((blocks, dim, tok), BF16),
            pltpu.VMEM((dim, heads * tok), F32),
            pltpu.VMEM((blocks, tok, dim), F32),
            pltpu.VMEM((blocks, tok, dim), F32),
            pltpu.VMEM((heads, tok), F32),
            pltpu.VMEM((heads, tok), F32),
            pltpu.VMEM((tok, tok), F32),
            pltpu.SMEM((blocks + 1,), jnp.int32),
            pltpu.SMEM((8,), jnp.int32),
            pltpu.SMEM((blocks,), jnp.int32),
            pltpu.VMEM(q.shape, BF16),
            pltpu.VMEM(do.shape, BF16),
            pltpu.VMEM(delta.shape, F32),
            pltpu.VMEM(k.shape, BF16),
            pltpu.VMEM(v.shape, BF16),
            pltpu.SemaphoreType.DMA((5,)),
            pltpu.VMEM(q.shape, BF16),
            pltpu.VMEM((2,) + k.shape, BF16),
            pltpu.SemaphoreType.DMA((sets,)),
            pltpu.SemaphoreType.DMA((2, blocks)),
            pltpu.VMEM((heads * tok, dim), BF16),
            pltpu.VMEM((heads * tok, dim), BF16),
            pltpu.VMEM((LONGEST // tok + 1, tok, heads * tok), BF16),
            pltpu.VMEM((LONGEST // tok + 1, heads, tok), F32),
            pltpu.VMEM((tok, heads * tok), BF16),
            pltpu.VMEM((tok, heads * tok), BF16),
            pltpu.SMEM((blocks,), jnp.int32),
        ],
        compiler_params=pltpu.CompilerParams(vmem_limit_bytes=59 * 2**20),
        name="attention",
    )(lengths, spans, q, do, delta, k, v)


class Place:
    def __init__(self, with_dp):
        y = lax.axis_index("dp")
        me = lax.axis_index("ctx")
        z, x, c = me // 8, lax.rem(me // 2, 4), lax.rem(me, 2)
        self.core = c
        self.sibling = {"dp": y, "ctx": me + 1 - 2 * c}

        def at(y, z, x):
            return {"dp": y, "ctx": z * 8 + x * 2 + c}

        def low(t):
            return t + 1 - 2 * lax.rem(t, 2)

        def far(t):
            return lax.rem(t + 2, 4)

        self.opposite = ()
        self.bits = split_axis(z) + split_axis(x)
        self.partners = (at(y, 3 - z, x), at(y, low(z), x), at(y, z, 3 - x), at(y, z, low(x)))
        if with_dp:
            self.bits = split_axis(y) + self.bits
            self.partners = (at(3 - y, z, x), at(low(y), z, x)) + self.partners
            self.opposite = tuple(
                at(*t) for t in ((far(y), z, x), (y, far(z), x), (y, z, far(x))))
        self.dims = len(self.bits)

    def greet(self):
        barrier = pltpu.get_barrier_semaphore()
        everyone = (self.sibling,) + self.partners + self.opposite
        for other in everyone:
            pl.semaphore_signal(barrier, inc=1, device_id=other, device_id_type=MESH)
        pl.semaphore_wait(barrier, len(everyone))

    def spot(self, free, flipped=()):
        found = []
        for d in range(self.dims):
            if d in free:
                found.append(slice(None))
            elif d in flipped:
                found.append(1 - self.bits[d])
            else:
                found.append(self.bits[d])
        return tuple(found)


def remote(src, dst, send, recv, to):
    return pltpu.make_async_remote_copy(
        src_ref=src, dst_ref=dst, send_sem=send, recv_sem=recv, device_id=to, device_id_type=MESH
    )


def turns(dims, start):
    return [(start + s) % dims for s in range(dims)]


def gather_kernel(k_ref, v_ref, q_ref, do_ref, o_ref, x_ref,
                  k_out, v_out, q_two, do_two, delta_two, xt_two,
                  k_all, v_all, q_buf, x_buf, do_buf, o_buf, xt_buf, delta_buf,
                  hop_send, hop_recv, pass_send, pass_recv, side_send, side_recv, local_sem):
    tok, dim = k_ref.shape
    half = q_two.shape[2]
    here = Place(False)
    c = here.core
    dims = here.dims
    quarter = tok // dims
    sources, targets = (k_ref, v_ref), (k_all, v_all)

    own_k, own_v = k_all.at[here.bits + (c,)], v_all.at[here.bits + (c,)]
    loads = [
        pltpu.make_async_copy(src, dst, local_sem.at[n])
        for n, (src, dst) in enumerate((
            (k_ref, own_k), (v_ref, own_v), (q_ref, q_buf), (do_ref, do_buf), (o_ref, o_buf), (x_ref, x_buf)))
    ]
    for copy in loads:
        copy.start()
    here.greet()

    def rows(p):
        return (pl.ds(p * quarter, quarter), slice(None))

    hops = {}
    for p in range(dims):
        for kind in range(2):
            n = (p * dims) * 2 + kind
            hops[p, 0, kind] = remote(
                sources[kind].at[rows(p)],
                targets[kind].at[here.bits + (c,) + rows(p)],
                hop_send.at[n], hop_recv.at[n], here.partners[turns(dims, p)[0]],
            )
            hops[p, 0, kind].start()
    sides = []
    def aside(src, dst):
        n = len(sides)
        sides.append(remote(src, dst, side_send.at[n], side_recv.at[n], here.sibling))
        sides[-1].start()

    for copy in loads[:5]:
        copy.wait()
    theirs, mine = pl.ds((1 - c) * half, half), pl.ds(c * half, half)
    aside(own_k, own_k)
    aside(own_v, own_v)
    aside(q_buf.at[:, theirs], q_two.at[c])
    aside(do_buf.at[:, theirs], do_two.at[c])
    keeps = []

    def keep(src, dst):
        keeps.append(pltpu.make_async_copy(src, dst, local_sem.at[6 + len(keeps)]))
        keeps[-1].start()

    keep(q_buf.at[:, mine], q_two.at[c])
    keep(do_buf.at[:, mine], do_two.at[c])

    passes = []

    def hand_on(p, s):
        order = turns(dims, p)
        for kind in range(2):
            n = (p * dims + s) * 2 + kind
            hops[p, s, kind].wait_recv()
            part = targets[kind].at[here.spot(order[:s], (order[s],)) + (c,) + rows(p)]
            copy = remote(part, part, pass_send.at[n], pass_recv.at[n], here.sibling)
            copy.start()
            passes.append(copy)

    def hop(p, s):
        order = turns(dims, p)
        for kind in range(2):
            n = (p * dims + s) * 2 + kind
            part = targets[kind].at[here.spot(order[:s]) + (c,) + rows(p)]
            hops[p, s, kind] = remote(
                part, part, hop_send.at[n], hop_recv.at[n], here.partners[order[s]]
            )
            hops[p, s, kind].start()

    for p in range(dims):
        hand_on(p, 0)
        hop(p, 1)
    heads = half // dim
    for h in range(2 * heads):
        cols = pl.ds(h * dim, dim)
        products = do_buf[:, cols].astype(F32) * o_buf[:, cols].astype(F32)
        delta_buf[h // heads, pl.ds(h % heads, 1), :] = jnp.sum(products.T, axis=0, keepdims=True)
    for h in range(heads, delta_buf.shape[1]):
        delta_buf[:, pl.ds(h, 1), :] = jnp.zeros((2, 1, tok), F32)
    keep(delta_buf.at[c], delta_two.at[c])
    aside(delta_buf.at[1 - c], delta_two.at[c])
    loads[5].wait()

    def turn(i, carry):
        xt_buf[pl.ds(i * 128, 128), :] = x_buf[:, pl.ds(i * 128, 128)].T
        return carry

    steps = x_ref.shape[1] // 128
    for p in range(dims):
        hand_on(p, 1)
        hop(p, 2)
    lax.fori_loop(0, steps // 2, turn, 0)
    mine = xt_two.at[:, pl.ds(c * tok, tok)]
    for p in range(dims):
        hand_on(p, 2)
        hop(p, 3)
    lax.fori_loop(steps // 2, steps, turn, 0)
    keep(xt_buf, mine)
    aside(xt_buf, mine)
    for p in range(dims):
        hand_on(p, 3)
    everywhere = (slice(None),) * dims
    keep(k_all.at[everywhere + (c,)], k_out.at[everywhere + (c,)])
    keep(v_all.at[everywhere + (c,)], v_out.at[everywhere + (c,)])
    for copy in passes:
        copy.wait()
    for copy in sides:
        copy.wait()
    keep(k_all.at[everywhere + (1 - c,)], k_out.at[everywhere + (1 - c,)])
    keep(v_all.at[everywhere + (1 - c,)], v_out.at[everywhere + (1 - c,)])
    for copy in hops.values():
        copy.wait_send()
    for copy in keeps:
        copy.wait()


def gather(k, v, q, do, o, x):
    tok, dim = k.shape
    half = q.shape[1] // 2
    anywhere = pl.BlockSpec(memory_space=pltpu.HBM)
    dma = pltpu.SemaphoreType.DMA
    full = jax.ShapeDtypeStruct((2, 2, 2, 2, 2, tok, dim), BF16)
    return pl.pallas_call(
        gather_kernel,
        out_shape=(
            full, full,
            jax.ShapeDtypeStruct((2, tok, half), BF16),
            jax.ShapeDtypeStruct((2, tok, half), BF16),
            jax.ShapeDtypeStruct((2, 8, tok), F32),
            jax.ShapeDtypeStruct((x.shape[1], 2 * tok), BF16),
        ),
        in_specs=[anywhere] * 6,
        out_specs=(anywhere,) * 6,
        scratch_shapes=[
            pltpu.VMEM(full.shape, BF16),
            pltpu.VMEM(full.shape, BF16),
            pltpu.VMEM(q.shape, BF16),
            pltpu.VMEM(x.shape, BF16),
            pltpu.VMEM(q.shape, BF16),
            pltpu.VMEM(q.shape, BF16),
            pltpu.VMEM((x.shape[1], tok), BF16),
            pltpu.VMEM((2, 8, tok), F32),
            dma((32,)), dma((32,)), dma((32,)), dma((32,)), dma((6,)), dma((6,)), dma((14,)),
        ],
        compiler_params=pltpu.CompilerParams(
            collective_id=1, has_side_effects=True, vmem_limit_bytes=59 * 2**20
        ),
        name="gather",
    )(k, v, q, do, o, x)


def wide_parts(rows, cols):
    cut = cols // 4 * 3
    quarter, half = rows // 4, rows // 2
    return [(i * quarter, quarter, 0, cut) for i in range(4)] + [
        (i * half, half, cut, cols - cut) for i in range(2)
    ]


def thin_parts(rows, cols):
    return [(i * (rows // 4), rows // 4, 0, cols) for i in range(4)]


def ring_parts(rows, cols):
    half, quarter = rows // 2, rows // 4
    return [(0, half, 0, cols), (half, quarter, 0, cols), (half + quarter, quarter, 0, cols)]


class Halving:
    def __init__(self, here, acc, parts, orders, landing, send, recv):
        self.here, self.acc, self.parts, self.orders = here, acc, parts, orders
        self.landing, self.send_sem, self.recv_sem = landing, send, recv
        self.copies = {}

    def index(self, p, s, flip):
        r0, nr, c0, nc = self.parts[p]
        order = self.orders[p]
        free = order[s + 1:]
        d = order[s]
        return self.here.spot(free, (d,) if flip else ()) + self.cut(r0, nr, c0, nc)

    def cut(self, r0, nr, c0, nc):
        return (slice(None),) * (len(self.acc.shape) - self.here.dims - 2) + (
            pl.ds(r0, nr), pl.ds(c0, nc))

    def send(self, p, s):
        dims = self.here.dims
        n = p * dims + s
        copy = remote(
            self.acc.at[self.index(p, s, True)], self.landing[n],
            self.send_sem.at[n], self.recv_sem.at[n], self.here.partners[self.orders[p][s]],
        )
        copy.start()
        self.copies[p, s] = copy

    def total(self, p, s):
        self.copies[p, s].wait_recv()
        n = p * self.here.dims + s
        return self.acc[self.index(p, s, False)].astype(F32) + self.landing[n][...].astype(F32)

    def add(self, p, s):
        self.acc[self.index(p, s, False)] = self.total(p, s).astype(self.acc.dtype)

    def finish(self):
        for copy in self.copies.values():
            copy.wait_send()


class Rings:
    def __init__(self, here, acc, parts, orders, landing, send, recv):
        self.here, self.acc, self.parts, self.orders = here, acc, parts, orders
        self.landing, self.send_sem, self.recv_sem = landing, send, recv
        self.copies = {}

    def index(self, p, s, flipped):
        r0, nr, c0, nc = self.parts[p]
        free = [d for a in self.orders[p][s + 1:] for d in (2 * a, 2 * a + 1)]
        return self.here.spot(free, flipped) + (pl.ds(r0, nr), pl.ds(c0, nc))

    def send(self, p, s):
        a = self.orders[p][s]
        high, low = 2 * a, 2 * a + 1
        ways = (((low,), self.here.partners[low]), ((high,), self.here.partners[high]),
                ((high, low), self.here.opposite[a]))
        for m in (2, 0, 1):
            flipped, partner = ways[m]
            n = (p * 3 + s) * 3 + m
            copy = remote(
                self.acc.at[self.index(p, s, flipped)], self.landing[n],
                self.send_sem.at[n], self.recv_sem.at[n], partner,
            )
            copy.start()
            self.copies[p, s, m] = copy

    def total(self, p, s):
        found = self.acc[self.index(p, s, ())].astype(F32)
        for m in range(3):
            self.copies[p, s, m].wait_recv()
            found = found + self.landing[(p * 3 + s) * 3 + m][...].astype(F32)
        return found

    def add(self, p, s):
        self.acc[self.index(p, s, ())] = self.total(p, s).astype(self.acc.dtype)

    def finish(self):
        for copy in self.copies.values():
            copy.wait_send()


def ring_shapes(parts):
    return [(2,) * (2 * (2 - s)) + (nr, nc) for (_, nr, _, nc) in parts for s in range(3) for _ in range(3)]


def landing_shapes(parts, orders, extra):
    shapes = []
    for (_, nr, _, nc), order in zip(parts, orders):
        for s in range(len(order)):
            shapes.append((2,) * (len(order) - 1 - s) + extra + (nr, nc))
    return shapes


def layout(tok, dim, half, features):
    row_chunk = features // 64
    kv_parts = thin_parts(tok, dim)
    kv_orders = [turns(4, p) for p in range(4)]
    wide = wide_parts(row_chunk, half)
    wide_orders = [turns(6, p) for p in range(6)]
    thin = ring_parts(row_chunk, dim)
    thin_orders = [turns(3, p) for p in range(3)]
    return row_chunk, kv_parts, kv_orders, wide, wide_orders, thin, thin_orders


def reduce_kernel(plan, scale, dkv_ref, dq_ref, xt_ref, qg_ref, kvg_ref, wg_ref, *scratch):
    row_chunk, kv_parts, kv_orders, wide, wide_orders, thin, thin_orders = plan
    (kv_acc, kv_in, kv_mine, w_acc, t_acc, xt, dq, fin, kv_send, kv_recv, w_send, w_recv, t_send, t_recv,
     side_send, side_recv, local_sem) = scratch[:17]
    landing = scratch[17:]
    tok, dim = dkv_ref.shape[-2:]
    half = dq_ref.shape[2]
    here_w = Place(True)
    here = Place(False)
    c = here.core
    n_kv, n_w = 16, 36
    kv = Halving(here, kv_acc, kv_parts, kv_orders, landing[:n_kv], kv_send, kv_recv)
    w = Halving(here_w, w_acc, wide, wide_orders, landing[n_kv:n_kv + n_w], w_send, w_recv)
    t = Rings(here_w, t_acc, thin, thin_orders, landing[n_kv + n_w:], t_send, t_recv)

    load_x = pltpu.make_async_copy(xt_ref, xt, local_sem.at[1])
    load_x.start()
    load_q = pltpu.make_async_copy(dq_ref, dq, local_sem.at[0])
    load_q.start()
    load_kv = pltpu.make_async_copy(dkv_ref.at[c], kv_acc, local_sem.at[2])
    load_kv.start()
    here_w.greet()
    sides = []

    def aside(src, dst):
        n = len(sides)
        sides.append(remote(src, dst, side_send.at[n], side_recv.at[n], here.sibling))
        sides[-1].start()

    rest = (slice(None),) * 5
    for p in range(4):
        r0, nr, _, _ = kv_parts[p]
        aside(dkv_ref.at[(1 - c,) + rest + (pl.ds(r0, nr),)], kv_in.at[rest + (pl.ds(r0, nr),)])
    aside(dq_ref.at[1 - c], qg_ref.at[:, pl.ds(c * half, half)])

    load_kv.wait()
    for p in range(4):
        r0, nr, _, _ = kv_parts[p]
        sides[p].wait_recv()

        def join(i, carry, r0=r0, nr=nr):
            at = (i // 8, lax.rem(i // 4, 2), lax.rem(i // 2, 2), lax.rem(i, 2), slice(None), pl.ds(r0, nr))
            kv_acc[at] = (kv_acc[at].astype(F32) + kv_in[at].astype(F32)).astype(BF16)
            return carry

        lax.fori_loop(0, 16, join, 0)
        kv.send(p, 0)

    def products(i, right, acc):
        block = dot(xt[pl.ds(i * 8 * row_chunk, 8 * row_chunk), :], right).astype(BF16)
        y = i // 2
        for j in range(8):
            z = 2 * lax.rem(i, 2) + j // 4
            x = j % 4
            at = split_axis(y) + split_axis(z) + (x // 2, (x + x // 2) % 2)
            acc[at] = block[j * row_chunk:(j + 1) * row_chunk]

    load_x.wait()
    load_q.wait()
    own_q = pltpu.make_async_copy(dq.at[c], qg_ref.at[:, pl.ds(c * half, half)], local_sem.at[3])
    own_q.start()
    both = dq[...].reshape(2 * tok, half)

    def wide_products(i, carry):
        products(i, both, w_acc)
        return carry

    lax.fori_loop(0, 8, wide_products, 0)
    for p in range(6):
        w.send(p, 0)
    def wide_step(s):
        for p in range(6):
            w.add(p, s - 1)
            w.send(p, s)

    for s in range(1, 4):
        for p in range(4):
            kv.add(p, s - 1)
            kv.send(p, s)
        if s > 1:
            wide_step(s - 1)
    kv_scale = jnp.where(c == 0, scale, 1.0).astype(F32)
    for p in range(4):
        r0, nr, _, _ = kv_parts[p]
        kv_mine[:, pl.ds(r0, nr), :] = (kv.total(p, 3) * kv_scale).astype(BF16)
    own_kv = pltpu.make_async_copy(kv_mine.at[c], kvg_ref.at[c], local_sem.at[4])
    own_kv.start()
    aside(kv_mine.at[1 - c], kvg_ref.at[c])
    mine = kv_mine[...].reshape(2 * tok, dim)

    def thin_products(i, carry):
        products(i, mine, t_acc)
        return carry

    lax.fori_loop(0, 8, thin_products, 0)
    for p in range(3):
        t.send(p, 0)
    wide_step(3)
    for s in range(1, 3):
        for p in range(3):
            t.add(p, s - 1)
            t.send(p, s)
        wide_step(s + 3)
    for p, (r0, nr, c0, nc) in enumerate(wide):
        fin[pl.ds(r0, nr), pl.ds(c0, nc)] = w.total(p, 5)
    for p, (r0, nr, c0, nc) in enumerate(thin):
        fin[pl.ds(r0, nr), pl.ds(half, nc)] = t.total(p, 2)
    rows_out = row_chunk // 2
    pieces = [(0, c * half, half), (half, 2 * half + c * dim, dim)]
    own_w = []
    for n, (src, dst, width) in enumerate(pieces):
        own_w.append(pltpu.make_async_copy(
            fin.at[pl.ds(c * rows_out, rows_out), pl.ds(src, width)],
            wg_ref.at[:, pl.ds(dst, width)], local_sem.at[5 + n]))
        own_w[-1].start()
        aside(fin.at[pl.ds((1 - c) * rows_out, rows_out), pl.ds(src, width)],
              wg_ref.at[:, pl.ds(dst, width)])
    own_q.wait()
    own_kv.wait()
    for copy in own_w:
        copy.wait()
    for n, copy in enumerate(sides):
        copy.wait_send()
        if n >= 4:
            copy.wait_recv()
    kv.finish()
    w.finish()
    t.finish()


def reduce(dkv, dq, xt, scale):
    tok, dim = dkv.shape[-2:]
    half = dq.shape[2]
    features = xt.shape[0]
    plan = layout(tok, dim, half, features)
    row_chunk, kv_parts, kv_orders, wide, wide_orders, thin, thin_orders = plan
    dma = pltpu.SemaphoreType.DMA
    shapes = (landing_shapes(kv_parts, kv_orders, (2,)) + landing_shapes(wide, wide_orders, ())
              + ring_shapes(thin))
    return pl.pallas_call(
        functools.partial(reduce_kernel, plan, scale),
        out_shape=(
            jax.ShapeDtypeStruct((tok, 2 * half), BF16),
            jax.ShapeDtypeStruct((2, tok, dim), BF16),
            jax.ShapeDtypeStruct((row_chunk // 2, 2 * half + 2 * dim), F32),
        ),
        in_specs=[pl.BlockSpec(memory_space=pltpu.HBM)] * 3,
        out_specs=(pl.BlockSpec(memory_space=pltpu.HBM),) * 3,
        scratch_shapes=[
            pltpu.VMEM(dkv.shape[1:], BF16),
            pltpu.VMEM(dkv.shape[1:], BF16),
            pltpu.VMEM((2, tok, dim), BF16),
            pltpu.VMEM((2,) * 6 + (row_chunk, half), BF16),
            pltpu.VMEM((2,) * 6 + (row_chunk, dim), BF16),
            pltpu.VMEM(xt.shape, BF16),
            pltpu.VMEM(dq.shape, BF16),
            pltpu.VMEM((row_chunk, half + dim), F32),
            dma((16,)), dma((16,)), dma((36,)), dma((36,)), dma((27,)), dma((27,)),
            dma((8,)), dma((8,)), dma((8,)),
        ] + [pltpu.VMEM(shape, BF16) for shape in shapes],
        compiler_params=pltpu.CompilerParams(
            collective_id=2, has_side_effects=True, vmem_limit_bytes=58 * 2**20
        ),
        name="reduce",
    )(dkv, dq, xt)


def finish_kernel(qg_ref, kvg_ref, wg_ref, q_out, k_out, v_out, w_out, sems):
    pairs = ((qg_ref, q_out.at[0]), (kvg_ref.at[0], k_out.at[0]), (kvg_ref.at[1], v_out.at[0]), (wg_ref, w_out))
    copies = [pltpu.make_async_copy(src, dst, sems.at[n]) for n, (src, dst) in enumerate(pairs)]
    for copy in copies:
        copy.start()
    for copy in copies:
        copy.wait()


def finish(qg, kvg, wg):
    hbm = pl.BlockSpec(memory_space=pltpu.HBM)
    one = jax.ShapeDtypeStruct((1,) + kvg.shape[1:], BF16)
    return pl.pallas_call(
        finish_kernel,
        out_shape=(jax.ShapeDtypeStruct((1,) + qg.shape, BF16), one, one, jax.ShapeDtypeStruct(wg.shape, F32)),
        in_specs=[pl.BlockSpec(memory_space=pltpu.VMEM)] * 3,
        out_specs=(hbm,) * 4,
        scratch_shapes=[pltpu.SemaphoreType.DMA((4,))],
        compiler_params=pltpu.CompilerParams(vmem_limit_bytes=59 * 2**20),
        name="finish",
    )(qg, kvg, wg)


def local(
    queries, key_rows, value_rows, forward_out, out_grad, layer_input, doc_lengths, held_span
):
    tok = queries.shape[1]
    dim = key_rows.shape[2]
    k, v, q, do, delta, xt = gather(
        key_rows[0], value_rows[0], queries[0], out_grad[0], forward_out[0], layer_input[0]
    )
    dq, dkv = attention(
        doc_lengths, held_span, q, do, delta, k.reshape(-1, tok, dim), v.reshape(-1, tok, dim)
    )
    dkv = dkv.reshape(2, 2, 2, 2, 2, 2, tok, dim)
    return finish(*reduce(dkv, dq, xt, 1.0 / math.sqrt(dim)))


def solution(mesh):
    row = P("dp", "ctx", None)
    flat = P("dp", None)
    return jax.shard_map(
        local, mesh=mesh, in_specs=(row,) * 6 + (flat,) * 2,
        out_specs=(row, row, row, P(("dp", "ctx"), None)), check_vma=False,
    )
```

```python
import functools, math
import jax, jax.numpy as jnp
from jax import lax
from jax.experimental import pallas as pl
from jax.experimental.pallas import tpu as pltpu
from jax.sharding import PartitionSpec as P

F32 = jnp.float32
BF16 = jnp.bfloat16
MESH = pl.DeviceIdType.MESH
NEG = -1e30
LONGEST = 4096


def dot(a, b):
    return jnp.dot(a, b, preferred_element_type=F32)


def split_axis(t):
    return t // 2, lax.rem(t + t // 2, 2)


def join_bits(bits):
    return ((bits[0] * 2 + bits[1]) * 2 + bits[2]) * 2 + bits[3]


def attention_kernel(sets, heads, tok, dim, blocks,
                     lengths_ref, span_ref,
                     q_in, do_in, delta_in, k_in, v_in,
                     dq_out, dkv_out,
                     qt, dot_, kt, dqt, dka, dva, stat_m, stat_l, bias, seen,
                     ends_ref, held_ref, q_ref, do_ref, delta_ref, k_ref, v_ref, loads,
                     dq_ref, dkv_ref, q_stores, kv_stores,
                     q_flat, do_flat, kept, kept_m, p_all, ds_all, marked):
    logit_scale = 1.0 / math.sqrt(dim)
    log2_scale = logit_scale * math.log2(math.e)

    pairs = ((q_in, q_ref), (do_in, do_ref), (delta_in, delta_ref), (k_in, k_ref), (v_in, v_ref))
    copies = [pltpu.make_async_copy(src, dst, loads.at[n]) for n, (src, dst) in enumerate(pairs)]
    for copy in copies:
        copy.start()
    me = lax.axis_index("ctx")
    own_chip = join_bits(split_axis(me // 8) + split_axis(lax.rem(me // 2, 4)))
    doc_count = lengths_ref.shape[1]
    end = jnp.int32(0)
    for d in range(doc_count):
        end = end + lengths_ref[0, d]
        ends_ref[d] = end

    def place(i, carry):
        chip = join_bits(split_axis(i // 8) + split_axis(lax.rem(i // 2, 4)))
        held_ref[2 * chip + lax.rem(i, 2)] = span_ref[0, i]
        return carry

    lax.fori_loop(0, blocks, place, 0)
    dka[...] = jnp.zeros_like(dka)
    dva[...] = jnp.zeros_like(dva)
    def store(kind, b):
        return pltpu.make_async_copy(dkv_ref.at[kind, b], dkv_out.at[kind, b], kv_stores.at[kind, b])

    def write(b):
        for kind, acc in enumerate((dka, dva)):
            dkv_ref[kind, b] = acc[b].astype(BF16)
            store(kind, b).start()

    for copy in copies:
        copy.wait()

    for rs in range(sets):
        own = 2 * own_chip + rs
        span = held_ref[own]
        first = span * tok

        def count(d, lo):
            end = ends_ref[d]
            return jnp.where(end <= first, jnp.maximum(lo, end), lo)

        lo_first = lax.fori_loop(0, doc_count, count, jnp.int32(0))
        seen[0] = own

        def collect(b, n):
            h = held_ref[b]
            take = (h < span) & (h * tok + (tok - 1) >= lo_first)

            @pl.when(take)
            def _():
                seen[n] = b

            return n + take.astype(jnp.int32)

        total = lax.fori_loop(0, blocks, collect, jnp.int32(1))
        last = rs == sets - 1
        if last:
            def unmark(b, carry):
                marked[b] = 0
                return carry

            def mark(i, carry):
                marked[seen[i]] = 1
                return carry

            def write_other(b, carry):
                @pl.when(marked[b] == 0)
                def _():
                    write(b)

                return carry

            lax.fori_loop(0, blocks, unmark, 0)
            lax.fori_loop(0, total, mark, 0)
            lax.fori_loop(0, blocks, write_other, 0)
        for h in range(heads):
            rows = pl.ds(h * dim, dim)
            flat = pl.ds(h * tok, tok)
            q_flat[flat, :] = q_ref[rs, :, rows]
            do_flat[flat, :] = do_ref[rs, :, rows]
            qt[:, flat] = q_flat[flat, :].T
            dot_[:, flat] = do_flat[flat, :].T
        pos = first + lax.broadcasted_iota(jnp.int32, (1, tok), 1)
        low = jnp.zeros((1, tok), jnp.int32)
        for d in range(doc_count):
            end = ends_ref[d]
            low = jnp.where(pos >= end, jnp.maximum(low, end), low)

        stat_m[...] = jnp.full_like(stat_m, NEG)
        stat_l[...] = jnp.zeros_like(stat_l)
        dqt[...] = jnp.zeros_like(dqt)

        def set_bias(b):
            kp = held_ref[b] * tok + lax.broadcasted_iota(jnp.int32, (tok, tok), 0)
            bias[...] = jnp.where((kp >= low) & (kp <= pos), 0.0, NEG)

        def pass_one(i, carry):
            b = seen[i]
            set_bias(b)
            k = k_ref[b]
            kt[b] = k.T
            for h in range(heads):
                row, cols = pl.ds(h, 1), pl.ds(h * tok, tok)
                s = dot(k, qt[:, cols]) * log2_scale + bias[...]
                m_old = stat_m[row, :]
                m_new = jnp.maximum(m_old, jnp.max(s, axis=0, keepdims=True))
                p = jnp.exp2(s - m_new)
                kept[i, :, cols] = p.astype(BF16)
                add = jnp.sum(p, axis=0, keepdims=True)
                stat_l[row, :] = stat_l[row, :] * jnp.exp2(m_old - m_new) + add
                stat_m[row, :] = m_new
                kept_m[i, row, :] = m_new
            return carry

        lax.fori_loop(0, total, pass_one, 0)
        stat_m[...] = stat_m[...] + jnp.log2(stat_l[...])

        def pass_two(i, carry):
            b = seen[i]
            v = v_ref[b]
            for h in range(heads):
                row, cols = pl.ds(h, 1), pl.ds(h * tok, tok)
                scaled = jnp.exp2(kept_m[i, row, :] - stat_m[row, :])
                p = kept[i, :, cols].astype(F32) * scaled
                dp = dot(v, dot_[:, cols])
                p_all[:, cols] = p.astype(BF16)
                ds_all[:, cols] = (p * (dp - delta_ref[rs, row, :])).astype(BF16)
            dva[b] += dot(p_all[...], do_flat[...])
            dka[b] += dot(ds_all[...], q_flat[...])
            dqt[...] += dot(kt[b], ds_all[...])
            if last:
                write(b)
            return carry

        lax.fori_loop(0, total, pass_two, 0)
        for h in range(heads):
            rows = pl.ds(h * dim, dim)
            dq_ref[rs, :, rows] = (logit_scale * dqt[:, pl.ds(h * tok, tok)]).T.astype(BF16)
        pltpu.make_async_copy(dq_ref.at[rs], dq_out.at[rs], q_stores.at[rs]).start()

    def stored(b, carry):
        store(0, b).wait()
        store(1, b).wait()
        return carry

    lax.fori_loop(0, blocks, stored, 0)
    for rs in range(sets):
        pltpu.make_async_copy(dq_ref.at[rs], dq_out.at[rs], q_stores.at[rs]).wait()


def attention(lengths, spans, q, do, delta, k, v):
    sets, tok, width = q.shape
    blocks, _, dim = k.shape
    heads = width // dim
    smem = pl.BlockSpec(memory_space=pltpu.SMEM)
    return pl.pallas_call(
        functools.partial(attention_kernel, sets, heads, tok, dim, blocks),
        out_shape=(
            jax.ShapeDtypeStruct(q.shape, BF16),
            jax.ShapeDtypeStruct((2,) + k.shape, BF16),
        ),
        in_specs=[smem, smem] + [pl.BlockSpec(memory_space=pltpu.HBM)] * 5,
        out_specs=(pl.BlockSpec(memory_space=pltpu.HBM),) * 2,
        scratch_shapes=[
            pltpu.VMEM((dim, heads * tok), BF16),
            pltpu.VMEM((dim, heads * tok), BF16),
            pltpu.VMEM((blocks, dim, tok), BF16),
            pltpu.VMEM((dim, heads * tok), F32),
            pltpu.VMEM((blocks, tok, dim), F32),
            pltpu.VMEM((blocks, tok, dim), F32),
            pltpu.VMEM((heads, tok), F32),
            pltpu.VMEM((heads, tok), F32),
            pltpu.VMEM((tok, tok), F32),
            pltpu.SMEM((blocks + 1,), jnp.int32),
            pltpu.SMEM((8,), jnp.int32),
            pltpu.SMEM((blocks,), jnp.int32),
            pltpu.VMEM(q.shape, BF16),
            pltpu.VMEM(do.shape, BF16),
            pltpu.VMEM(delta.shape, F32),
            pltpu.VMEM(k.shape, BF16),
            pltpu.VMEM(v.shape, BF16),
            pltpu.SemaphoreType.DMA((5,)),
            pltpu.VMEM(q.shape, BF16),
            pltpu.VMEM((2,) + k.shape, BF16),
            pltpu.SemaphoreType.DMA((sets,)),
            pltpu.SemaphoreType.DMA((2, blocks)),
            pltpu.VMEM((heads * tok, dim), BF16),
            pltpu.VMEM((heads * tok, dim), BF16),
            pltpu.VMEM((LONGEST // tok + 1, tok, heads * tok), BF16),
            pltpu.VMEM((LONGEST // tok + 1, heads, tok), F32),
            pltpu.VMEM((tok, heads * tok), BF16),
            pltpu.VMEM((tok, heads * tok), BF16),
            pltpu.SMEM((blocks,), jnp.int32),
        ],
        compiler_params=pltpu.CompilerParams(vmem_limit_bytes=59 * 2**20),
        name="attention",
    )(lengths, spans, q, do, delta, k, v)


class Place:
    def __init__(self, with_dp):
        y = lax.axis_index("dp")
        me = lax.axis_index("ctx")
        z, x, c = me // 8, lax.rem(me // 2, 4), lax.rem(me, 2)
        self.core = c
        self.sibling = {"dp": y, "ctx": me + 1 - 2 * c}

        def at(y, z, x):
            return {"dp": y, "ctx": z * 8 + x * 2 + c}

        def low(t):
            return t + 1 - 2 * lax.rem(t, 2)

        def far(t):
            return lax.rem(t + 2, 4)

        self.opposite = (at(y, far(z), x), at(y, z, far(x)))
        self.bits = split_axis(z) + split_axis(x)
        self.partners = (at(y, 3 - z, x), at(y, low(z), x), at(y, z, 3 - x), at(y, z, low(x)))
        if with_dp:
            self.bits = split_axis(y) + self.bits
            self.partners = (at(3 - y, z, x), at(low(y), z, x)) + self.partners
            self.opposite = (at(far(y), z, x),) + self.opposite
        self.dims = len(self.bits)

    def greet(self, others=()):
        barrier = pltpu.get_barrier_semaphore()
        everyone = (self.sibling,) + self.partners + others
        for other in everyone:
            pl.semaphore_signal(barrier, inc=1, device_id=other, device_id_type=MESH)
        pl.semaphore_wait(barrier, len(everyone))

    def spot(self, free, flipped=()):
        found = []
        for d in range(self.dims):
            if d in free:
                found.append(slice(None))
            elif d in flipped:
                found.append(1 - self.bits[d])
            else:
                found.append(self.bits[d])
        return tuple(found)


def remote(src, dst, send, recv, to):
    return pltpu.make_async_remote_copy(
        src_ref=src, dst_ref=dst, send_sem=send, recv_sem=recv, device_id=to, device_id_type=MESH
    )


def turns(dims, start):
    return [(start + s) % dims for s in range(dims)]


GATHER_PARTS = 8


def gather_kernel(k_ref, v_ref, q_ref, do_ref, o_ref, x_ref,
                  k_out, v_out, q_two, do_two, delta_two, xt_two,
                  kv_all, q_buf, x_buf, do_buf, o_buf, xt_buf, delta_buf,
                  hop_send, hop_recv, pass_send, pass_recv, side_send, side_recv, local_sem):
    tok, dim = k_ref.shape
    half = q_two.shape[2]
    here = Place(False)
    c = here.core
    dims = here.dims
    quarter = tok // GATHER_PARTS
    own = kv_all.at[here.bits + (c,)]
    loads = [
        pltpu.make_async_copy(src, dst, local_sem.at[n])
        for n, (src, dst) in enumerate((
            (k_ref, own.at[0]), (v_ref, own.at[1]), (q_ref, q_buf), (do_ref, do_buf), (o_ref, o_buf), (x_ref, x_buf)))
    ]
    for copy in loads:
        copy.start()
    here.greet()
    loads[0].wait()
    loads[1].wait()

    def rows(p):
        return (slice(None), pl.ds(p * quarter, quarter), slice(None))

    hops, passes = {}, []

    def hop(p, s):
        order = turns(dims, p % dims)
        n = p * dims + s
        part = kv_all.at[here.spot(order[:s]) + (c,) + rows(p)]
        hops[p, s] = remote(part, part, hop_send.at[n], hop_recv.at[n], here.partners[order[s]])
        hops[p, s].start()

    def hand_on(p, s):
        order = turns(dims, p % dims)
        n = p * dims + s
        hops[p, s].wait_recv()
        part = kv_all.at[here.spot(order[:s], (order[s],)) + (c,) + rows(p)]
        copy = remote(part, part, pass_send.at[n], pass_recv.at[n], here.sibling)
        passes.append(copy)
        return copy

    def next_hop(s):
        for p in range(GATHER_PARTS):
            copy = hand_on(p, s)
            if s < dims - 1:
                hop(p, s + 1)
            copy.start()

    for p in range(GATHER_PARTS):
        hop(p, 0)
    sides = []
    def aside(src, dst):
        n = len(sides)
        sides.append(remote(src, dst, side_send.at[n], side_recv.at[n], here.sibling))
        sides[-1].start()

    for copy in loads[2:5]:
        copy.wait()
    theirs, mine = pl.ds((1 - c) * half, half), pl.ds(c * half, half)
    aside(own, own)
    aside(q_buf.at[:, theirs], q_two.at[c])
    aside(do_buf.at[:, theirs], do_two.at[c])
    keeps = []

    def keep(src, dst):
        keeps.append(pltpu.make_async_copy(src, dst, local_sem.at[6 + len(keeps)]))
        keeps[-1].start()

    keep(q_buf.at[:, mine], q_two.at[c])
    keep(do_buf.at[:, mine], do_two.at[c])

    next_hop(0)
    heads = half // dim
    for h in range(2 * heads):
        cols = pl.ds(h * dim, dim)
        products = do_buf[:, cols].astype(F32) * o_buf[:, cols].astype(F32)
        delta_buf[h // heads, pl.ds(h % heads, 1), :] = jnp.sum(products.T, axis=0, keepdims=True)
    for h in range(heads, delta_buf.shape[1]):
        delta_buf[:, pl.ds(h, 1), :] = jnp.zeros((2, 1, tok), F32)
    keep(delta_buf.at[c], delta_two.at[c])
    aside(delta_buf.at[1 - c], delta_two.at[c])
    loads[5].wait()

    def turn(i, carry):
        xt_buf[pl.ds(i * 128, 128), :] = x_buf[:, pl.ds(i * 128, 128)].T
        return carry

    steps = x_ref.shape[1] // 128
    next_hop(1)
    lax.fori_loop(0, steps // 2, turn, 0)
    mine = xt_two.at[:, pl.ds(c * tok, tok)]
    next_hop(2)
    lax.fori_loop(steps // 2, steps, turn, 0)
    keep(xt_buf, mine)
    aside(xt_buf, mine)
    next_hop(3)
    everywhere = (slice(None),) * dims
    keep(kv_all.at[everywhere + (c, 0)], k_out.at[everywhere + (c,)])
    keep(kv_all.at[everywhere + (c, 1)], v_out.at[everywhere + (c,)])
    for copy in passes:
        copy.wait()
    for copy in sides:
        copy.wait()
    keep(kv_all.at[everywhere + (1 - c, 0)], k_out.at[everywhere + (1 - c,)])
    keep(kv_all.at[everywhere + (1 - c, 1)], v_out.at[everywhere + (1 - c,)])
    for copy in hops.values():
        copy.wait_send()
    for copy in keeps:
        copy.wait()


def gather(k, v, q, do, o, x):
    tok, dim = k.shape
    half = q.shape[1] // 2
    anywhere = pl.BlockSpec(memory_space=pltpu.HBM)
    dma = pltpu.SemaphoreType.DMA
    full = jax.ShapeDtypeStruct((2, 2, 2, 2, 2, tok, dim), BF16)
    return pl.pallas_call(
        gather_kernel,
        out_shape=(
            full, full,
            jax.ShapeDtypeStruct((2, tok, half), BF16),
            jax.ShapeDtypeStruct((2, tok, half), BF16),
            jax.ShapeDtypeStruct((2, 8, tok), F32),
            jax.ShapeDtypeStruct((x.shape[1], 2 * tok), BF16),
        ),
        in_specs=[anywhere] * 6,
        out_specs=(anywhere,) * 6,
        scratch_shapes=[
            pltpu.VMEM((2, 2, 2, 2, 2, 2, tok, dim), BF16),
            pltpu.VMEM(q.shape, BF16),
            pltpu.VMEM(x.shape, BF16),
            pltpu.VMEM(q.shape, BF16),
            pltpu.VMEM(q.shape, BF16),
            pltpu.VMEM((x.shape[1], tok), BF16),
            pltpu.VMEM((2, 8, tok), F32),
            *[dma((4 * GATHER_PARTS,))] * 4, dma((6,)), dma((6,)), dma((14,)),
        ],
        compiler_params=pltpu.CompilerParams(
            collective_id=1, has_side_effects=True, vmem_limit_bytes=59 * 2**20
        ),
        name="gather",
    )(k, v, q, do, o, x)


def wide_parts(rows, cols):
    cut = cols // 4 * 3
    quarter, half = rows // 4, rows // 2
    return [(i * quarter, quarter, 0, cut) for i in range(4)] + [
        (i * half, half, cut, cols - cut) for i in range(2)
    ]


def ring_parts(rows, cols):
    half, quarter = rows // 2, rows // 4
    return [(0, half, 0, cols), (half, quarter, 0, cols), (half + quarter, quarter, 0, cols)]


def flips(stage):
    return (stage,) if len(stage) == 1 else (stage, stage[:1], stage[1:])


class Sums:
    def __init__(self, here, acc, parts, orders, landing, sems):
        self.here, self.acc, self.parts, self.orders = here, acc, parts, orders
        self.send_sem, self.recv_sem = sems
        self.copies, self.landing = {}, {}
        for n, key in enumerate(keys(orders)):
            self.landing[key] = (n, landing[n])

    def index(self, p, s, flipped):
        r0, nr, c0, nc = self.parts[p]
        free = [d for stage in self.orders[p][s + 1:] for d in stage]
        if isinstance(self.acc, list):
            return self.here.spot(free, flipped)
        middle = (slice(None),) * (len(self.acc.shape) - self.here.dims - 2)
        return self.here.spot(free, flipped) + middle + (pl.ds(r0, nr), pl.ds(c0, nc))

    def buffer(self, p):
        return self.acc[p] if isinstance(self.acc, list) else self.acc

    def send(self, p, s):
        for m, flipped in enumerate(flips(self.orders[p][s])):
            n, landing = self.landing[p, s, m]
            partner = self.here.partners[flipped[0]] if len(flipped) == 1 else self.here.opposite[flipped[0] // 2]
            copy = remote(
                self.buffer(p).at[self.index(p, s, flipped)], landing, self.send_sem.at[n], self.recv_sem.at[n], partner)
            copy.start()
            self.copies[p, s, m] = copy

    def total(self, p, s):
        found = self.buffer(p)[self.index(p, s, ())].astype(F32)
        for m in range(len(flips(self.orders[p][s]))):
            self.copies[p, s, m].wait_recv()
            found = found + self.landing[p, s, m][1][...].astype(F32)
        return found

    def step(self, s):
        for p in range(len(self.parts)):
            self.buffer(p)[self.index(p, s - 1, ())] = self.total(p, s - 1).astype(BF16)
            self.send(p, s)

    def finish(self):
        for copy in self.copies.values():
            copy.wait_send()


def keys(orders):
    return [(p, s, m) for p, order in enumerate(orders) for s, stage in enumerate(order)
            for m in range(len(flips(stage)))]


def landing_shapes(parts, orders, extra):
    shapes = []
    for p, s, _ in keys(orders):
        left = sum(len(stage) for stage in orders[p][s + 1:])
        shapes.append((2,) * left + extra + (parts[p][1], parts[p][3]))
    return shapes


def layout(tok, dim, half, features):
    row_chunk = features // 64
    kv_parts = [(i * (tok // 8), tok // 8, 0, dim) for i in range(8)]
    kv_orders = [
        ((0,), (1,), (2, 3)), ((1,), (0,), (2, 3)), ((2,), (3,), (0, 1)), ((3,), (2,), (0, 1))] * 2
    wide = wide_parts(row_chunk, half)
    wide_orders = [
        ((0,), (1,), (2, 3), (4, 5)), ((1,), (0,), (4, 5), (2, 3)), ((2,), (3,), (4, 5), (0, 1)),
        ((3,), (2,), (0, 1), (4, 5)), ((4,), (5,), (0, 1), (2, 3)), ((5,), (4,), (2, 3), (0, 1))]
    thin = ring_parts(row_chunk, dim)
    thin_orders = [
        ((0, 1), (2, 3), (4, 5)), ((2, 3), (4, 5), (0, 1)), ((4, 5), (0, 1), (2, 3))]
    return row_chunk, kv_parts, kv_orders, wide, wide_orders, thin, thin_orders


def reduce_kernel(plan, scale, dkv_ref, dq_ref, xt_ref, qg_ref, kvg_ref, wg_ref, *scratch):
    row_chunk, kv_parts, kv_orders, wide, wide_orders, thin, thin_orders = plan
    (kv_acc, kv_in, kv_mine, t_acc, xt, dq, fin, kv_send, kv_recv, w_send, w_recv, t_send, t_recv,
     side_send, side_recv, local_sem) = scratch[:16]
    w_acc = list(scratch[16:16 + len(wide)])
    landing = scratch[16 + len(wide):]
    tok, dim = dkv_ref.shape[-2:]
    half = dq_ref.shape[2]
    here_w = Place(True)
    here = Place(False)
    c = here.core
    n_kv, n_w = len(keys(kv_orders)), len(keys(wide_orders))
    kv = Sums(here, kv_acc, kv_parts, kv_orders, landing[:n_kv], (kv_send, kv_recv))
    w = Sums(here_w, w_acc, wide, wide_orders, landing[n_kv:n_kv + n_w], (w_send, w_recv))
    t = Sums(here_w, t_acc, thin, thin_orders, landing[n_kv + n_w:], (t_send, t_recv))

    load_x = pltpu.make_async_copy(xt_ref, xt, local_sem.at[1])
    load_x.start()
    load_q = pltpu.make_async_copy(dq_ref, dq, local_sem.at[0])
    load_q.start()
    load_kv = pltpu.make_async_copy(dkv_ref.at[c], kv_acc, local_sem.at[2])
    load_kv.start()
    here_w.greet(here_w.opposite)
    sides = []

    def aside(src, dst):
        n = len(sides)
        sides.append(remote(src, dst, side_send.at[n], side_recv.at[n], here.sibling))
        sides[-1].start()

    rest = (slice(None),) * 5
    for p in range(len(kv_parts)):
        r0, nr, _, _ = kv_parts[p]
        aside(dkv_ref.at[(1 - c,) + rest + (pl.ds(r0, nr),)], kv_in.at[rest + (pl.ds(r0, nr),)])
    aside(dq_ref.at[1 - c], qg_ref.at[:, pl.ds(c * half, half)])

    def products(i, right, accs, parts):
        block = dot(xt[pl.ds(i * 8 * row_chunk, 8 * row_chunk), :], right).astype(BF16)
        y = i // 2
        for j in range(8):
            z = 2 * lax.rem(i, 2) + j // 4
            x = j % 4
            at = split_axis(y) + split_axis(z) + (x // 2, (x + x // 2) % 2)
            for acc, (r0, nr, c0, nc) in zip(accs, parts):
                acc[at] = block[j * row_chunk + r0:j * row_chunk + r0 + nr, c0:c0 + nc]

    load_x.wait()
    load_q.wait()
    own_q = pltpu.make_async_copy(dq.at[c], qg_ref.at[:, pl.ds(c * half, half)], local_sem.at[3])
    own_q.start()
    both = dq[...].reshape(2 * tok, half)

    def wide_products(i, carry):
        products(i, both, w_acc, wide)
        return carry

    lax.fori_loop(0, 8, wide_products, 0)
    load_kv.wait()
    for p in range(len(kv_parts)):
        r0, nr, _, _ = kv_parts[p]
        sides[p].wait_recv()

        def join(i, carry, r0=r0, nr=nr):
            at = (i // 8, lax.rem(i // 4, 2), lax.rem(i // 2, 2), lax.rem(i, 2), slice(None), pl.ds(r0, nr))
            kv_acc[at] = (kv_acc[at].astype(F32) + kv_in[at].astype(F32)).astype(BF16)
            return carry

        lax.fori_loop(0, 16, join, 0)
        kv.send(p, 0)

    for p in range(len(wide)):
        w.send(p, 0)
    kv.step(1)
    kv.step(2)
    w.step(1)
    kv_scale = jnp.where(c == 0, scale, 1.0).astype(F32)
    for p in range(len(kv_parts)):
        r0, nr, _, _ = kv_parts[p]
        kv_mine[:, pl.ds(r0, nr), :] = (kv.total(p, 2) * kv_scale).astype(BF16)
    own_kv = pltpu.make_async_copy(kv_mine.at[c], kvg_ref.at[c], local_sem.at[4])
    own_kv.start()
    aside(kv_mine.at[1 - c], kvg_ref.at[c])
    mine = kv_mine[...].reshape(2 * tok, dim)

    def thin_products(i, carry):
        products(i, mine, [t_acc], [(0, row_chunk, 0, dim)])
        return carry

    lax.fori_loop(0, 8, thin_products, 0)
    for p in range(len(thin)):
        t.send(p, 0)
    w.step(2)
    t.step(1)
    w.step(3)
    t.step(2)
    rows_out = row_chunk // 2
    own_w = []

    def hand_out(src, dst, width):
        own_w.append(pltpu.make_async_copy(
            fin.at[pl.ds(c * rows_out, rows_out), pl.ds(src, width)],
            wg_ref.at[:, pl.ds(dst, width)], local_sem.at[5 + len(own_w)]))
        own_w[-1].start()
        aside(fin.at[pl.ds((1 - c) * rows_out, rows_out), pl.ds(src, width)],
              wg_ref.at[:, pl.ds(dst, width)])

    for p, (r0, nr, c0, nc) in enumerate(wide):
        fin[pl.ds(r0, nr), pl.ds(c0, nc)] = w.total(p, 3)
    hand_out(0, c * half, half)
    for p, (r0, nr, c0, nc) in enumerate(thin):
        fin[pl.ds(r0, nr), pl.ds(half, nc)] = t.total(p, 2)
    hand_out(half, 2 * half + c * dim, dim)
    own_q.wait()
    own_kv.wait()
    for copy in own_w:
        copy.wait()
    for n, copy in enumerate(sides):
        copy.wait_send()
        if n >= len(kv_parts):
            copy.wait_recv()
    kv.finish()
    w.finish()
    t.finish()


def reduce(dkv, dq, xt, scale):
    tok, dim = dkv.shape[-2:]
    half = dq.shape[2]
    features = xt.shape[0]
    plan = layout(tok, dim, half, features)
    row_chunk, kv_parts, kv_orders, wide, wide_orders, thin, thin_orders = plan
    dma = pltpu.SemaphoreType.DMA
    shapes = (landing_shapes(kv_parts, kv_orders, (2,)) + landing_shapes(wide, wide_orders, ())
              + landing_shapes(thin, thin_orders, ()))
    return pl.pallas_call(
        functools.partial(reduce_kernel, plan, scale),
        out_shape=(
            jax.ShapeDtypeStruct((tok, 2 * half), BF16),
            jax.ShapeDtypeStruct((2, tok, dim), BF16),
            jax.ShapeDtypeStruct((row_chunk // 2, 2 * half + 2 * dim), F32),
        ),
        in_specs=[pl.BlockSpec(memory_space=pltpu.HBM)] * 3,
        out_specs=(pl.BlockSpec(memory_space=pltpu.HBM),) * 3,
        scratch_shapes=[
            pltpu.VMEM(dkv.shape[1:], BF16),
            pltpu.VMEM(dkv.shape[1:], BF16),
            pltpu.VMEM((2, tok, dim), BF16),
            pltpu.VMEM((2,) * 6 + (row_chunk, dim), BF16),
            pltpu.VMEM(xt.shape, BF16),
            pltpu.VMEM(dq.shape, BF16),
            pltpu.VMEM((row_chunk, half + dim), F32),
            *[dma((len(keys(orders)),)) for orders in (kv_orders, wide_orders, thin_orders) for _ in range(2)],
            dma((12,)), dma((12,)), dma((8,)),
        ] + [pltpu.VMEM((2,) * 6 + (nr, nc), BF16) for _, nr, _, nc in wide]
        + [pltpu.VMEM(shape, BF16) for shape in shapes],
        compiler_params=pltpu.CompilerParams(
            collective_id=2, has_side_effects=True, vmem_limit_bytes=58 * 2**20
        ),
        name="reduce",
    )(dkv, dq, xt)


def finish_kernel(qg_ref, kvg_ref, wg_ref, q_out, k_out, v_out, w_out, sems):
    pairs = ((qg_ref, q_out.at[0]), (kvg_ref.at[0], k_out.at[0]), (kvg_ref.at[1], v_out.at[0]), (wg_ref, w_out))
    copies = [pltpu.make_async_copy(src, dst, sems.at[n]) for n, (src, dst) in enumerate(pairs)]
    for copy in copies:
        copy.start()
    for copy in copies:
        copy.wait()


def finish(qg, kvg, wg):
    hbm = pl.BlockSpec(memory_space=pltpu.HBM)
    one = jax.ShapeDtypeStruct((1,) + kvg.shape[1:], BF16)
    return pl.pallas_call(
        finish_kernel,
        out_shape=(jax.ShapeDtypeStruct((1,) + qg.shape, BF16), one, one, jax.ShapeDtypeStruct(wg.shape, F32)),
        in_specs=[pl.BlockSpec(memory_space=pltpu.VMEM)] * 3,
        out_specs=(hbm,) * 4,
        scratch_shapes=[pltpu.SemaphoreType.DMA((4,))],
        compiler_params=pltpu.CompilerParams(vmem_limit_bytes=59 * 2**20),
        name="finish",
    )(qg, kvg, wg)


def local(
    queries, key_rows, value_rows, forward_out, out_grad, layer_input, doc_lengths, held_span
):
    tok = queries.shape[1]
    dim = key_rows.shape[2]
    k, v, q, do, delta, xt = gather(
        key_rows[0], value_rows[0], queries[0], out_grad[0], forward_out[0], layer_input[0]
    )
    dq, dkv = attention(
        doc_lengths, held_span, q, do, delta, k.reshape(-1, tok, dim), v.reshape(-1, tok, dim)
    )
    dkv = dkv.reshape(2, 2, 2, 2, 2, 2, tok, dim)
    return finish(*reduce(dkv, dq, xt, 1.0 / math.sqrt(dim)))


def solution(mesh):
    row = P("dp", "ctx", None)
    flat = P("dp", None)
    return jax.shard_map(
        local, mesh=mesh, in_specs=(row,) * 6 + (flat,) * 2,
        out_specs=(row, row, row, P(("dp", "ctx"), None)), check_vma=False,
    )
```

```python
import functools, math
import jax, jax.numpy as jnp
from jax import lax
from jax.experimental import pallas as pl
from jax.experimental.pallas import tpu as pltpu
from jax.sharding import PartitionSpec as P

F32 = jnp.float32
BF16 = jnp.bfloat16
MESH = pl.DeviceIdType.MESH
NEG = -1e30
LONGEST = 4096


def dot(a, b):
    return jnp.dot(a, b, preferred_element_type=F32)


def split_axis(t):
    return t // 2, lax.rem(t + t // 2, 2)


def join_bits(bits):
    return ((bits[0] * 2 + bits[1]) * 2 + bits[2]) * 2 + bits[3]


def attention_kernel(sets, heads, tok, dim, blocks,
                     lengths_ref, span_ref,
                     q_in, do_in, delta_in, k_in, v_in,
                     dq_out, dkv_out,
                     qt, dot_, kt, dqt, dka, dva, stat_m, stat_l, bias, seen,
                     ends_ref, held_ref, q_ref, do_ref, delta_ref, k_ref, v_ref, loads,
                     dq_ref, dkv_ref, q_stores, kv_stores,
                     q_flat, do_flat, kept, kept_m, p_all, ds_all, marked):
    logit_scale = 1.0 / math.sqrt(dim)
    log2_scale = logit_scale * math.log2(math.e)

    pairs = ((q_in, q_ref), (do_in, do_ref), (delta_in, delta_ref), (k_in, k_ref), (v_in, v_ref))
    copies = [pltpu.make_async_copy(src, dst, loads.at[n]) for n, (src, dst) in enumerate(pairs)]
    for copy in copies:
        copy.start()
    me = lax.axis_index("ctx")
    own_chip = join_bits(split_axis(me // 8) + split_axis(lax.rem(me // 2, 4)))
    doc_count = lengths_ref.shape[1]
    end = jnp.int32(0)
    for d in range(doc_count):
        end = end + lengths_ref[0, d]
        ends_ref[d] = end

    def place(i, carry):
        chip = join_bits(split_axis(i // 8) + split_axis(lax.rem(i // 2, 4)))
        held_ref[2 * chip + lax.rem(i, 2)] = span_ref[0, i]
        return carry

    lax.fori_loop(0, blocks, place, 0)
    dka[...] = jnp.zeros_like(dka)
    dva[...] = jnp.zeros_like(dva)
    def store(kind, b):
        return pltpu.make_async_copy(dkv_ref.at[kind, b], dkv_out.at[kind, b], kv_stores.at[kind, b])

    def write(b):
        for kind, acc in enumerate((dka, dva)):
            dkv_ref[kind, b] = acc[b].astype(BF16)
            store(kind, b).start()

    for copy in copies:
        copy.wait()

    for rs in range(sets):
        own = 2 * own_chip + rs
        span = held_ref[own]
        first = span * tok

        def count(d, lo):
            end = ends_ref[d]
            return jnp.where(end <= first, jnp.maximum(lo, end), lo)

        lo_first = lax.fori_loop(0, doc_count, count, jnp.int32(0))
        seen[0] = own

        def collect(b, n):
            h = held_ref[b]
            take = (h < span) & (h * tok + (tok - 1) >= lo_first)

            @pl.when(take)
            def _():
                seen[n] = b

            return n + take.astype(jnp.int32)

        total = lax.fori_loop(0, blocks, collect, jnp.int32(1))
        last = rs == sets - 1
        if last:
            def unmark(b, carry):
                marked[b] = 0
                return carry

            def mark(i, carry):
                marked[seen[i]] = 1
                return carry

            def write_other(b, carry):
                @pl.when(marked[b] == 0)
                def _():
                    write(b)

                return carry

            lax.fori_loop(0, blocks, unmark, 0)
            lax.fori_loop(0, total, mark, 0)
            lax.fori_loop(0, blocks, write_other, 0)
        for h in range(heads):
            rows = pl.ds(h * dim, dim)
            flat = pl.ds(h * tok, tok)
            q_flat[flat, :] = q_ref[rs, :, rows]
            do_flat[flat, :] = do_ref[rs, :, rows]
            qt[:, flat] = q_flat[flat, :].T
            dot_[:, flat] = do_flat[flat, :].T
        pos = first + lax.broadcasted_iota(jnp.int32, (1, tok), 1)
        low = jnp.zeros((1, tok), jnp.int32)
        for d in range(doc_count):
            end = ends_ref[d]
            low = jnp.where(pos >= end, jnp.maximum(low, end), low)

        stat_m[...] = jnp.full_like(stat_m, NEG)
        stat_l[...] = jnp.zeros_like(stat_l)
        dqt[...] = jnp.zeros_like(dqt)

        def set_bias(b):
            kp = held_ref[b] * tok + lax.broadcasted_iota(jnp.int32, (tok, tok), 0)
            bias[...] = jnp.where((kp >= low) & (kp <= pos), 0.0, NEG)

        def pass_one(i, carry):
            b = seen[i]
            set_bias(b)
            k = k_ref[b]
            kt[b] = k.T
            for h in range(heads):
                row, cols = pl.ds(h, 1), pl.ds(h * tok, tok)
                s = dot(k, qt[:, cols]) * log2_scale + bias[...]
                m_old = stat_m[row, :]
                m_new = jnp.maximum(m_old, jnp.max(s, axis=0, keepdims=True))
                p = jnp.exp2(s - m_new)
                kept[i, :, cols] = p.astype(BF16)
                add = jnp.sum(p, axis=0, keepdims=True)
                stat_l[row, :] = stat_l[row, :] * jnp.exp2(m_old - m_new) + add
                stat_m[row, :] = m_new
                kept_m[i, row, :] = m_new
            return carry

        lax.fori_loop(0, total, pass_one, 0)
        stat_m[...] = stat_m[...] + jnp.log2(stat_l[...])

        def pass_two(i, carry):
            b = seen[i]
            v = v_ref[b]
            for h in range(heads):
                row, cols = pl.ds(h, 1), pl.ds(h * tok, tok)
                scaled = jnp.exp2(kept_m[i, row, :] - stat_m[row, :])
                p = kept[i, :, cols].astype(F32) * scaled
                dp = dot(v, dot_[:, cols])
                p_all[:, cols] = p.astype(BF16)
                ds_all[:, cols] = (p * (dp - delta_ref[rs, row, :])).astype(BF16)
            dva[b] += dot(p_all[...], do_flat[...])
            dka[b] += dot(ds_all[...], q_flat[...])
            dqt[...] += dot(kt[b], ds_all[...])
            if last:
                write(b)
            return carry

        lax.fori_loop(0, total, pass_two, 0)
        for h in range(heads):
            rows = pl.ds(h * dim, dim)
            dq_ref[rs, :, rows] = (logit_scale * dqt[:, pl.ds(h * tok, tok)]).T.astype(BF16)
        pltpu.make_async_copy(dq_ref.at[rs], dq_out.at[rs], q_stores.at[rs]).start()

    def stored(b, carry):
        store(0, b).wait()
        store(1, b).wait()
        return carry

    lax.fori_loop(0, blocks, stored, 0)
    for rs in range(sets):
        pltpu.make_async_copy(dq_ref.at[rs], dq_out.at[rs], q_stores.at[rs]).wait()


def attention(lengths, spans, q, do, delta, k, v):
    sets, tok, width = q.shape
    blocks, _, dim = k.shape
    heads = width // dim
    smem = pl.BlockSpec(memory_space=pltpu.SMEM)
    return pl.pallas_call(
        functools.partial(attention_kernel, sets, heads, tok, dim, blocks),
        out_shape=(
            jax.ShapeDtypeStruct(q.shape, BF16),
            jax.ShapeDtypeStruct((2,) + k.shape, BF16),
        ),
        in_specs=[smem, smem] + [pl.BlockSpec(memory_space=pltpu.HBM)] * 5,
        out_specs=(pl.BlockSpec(memory_space=pltpu.HBM),) * 2,
        scratch_shapes=[
            pltpu.VMEM((dim, heads * tok), BF16),
            pltpu.VMEM((dim, heads * tok), BF16),
            pltpu.VMEM((blocks, dim, tok), BF16),
            pltpu.VMEM((dim, heads * tok), F32),
            pltpu.VMEM((blocks, tok, dim), F32),
            pltpu.VMEM((blocks, tok, dim), F32),
            pltpu.VMEM((heads, tok), F32),
            pltpu.VMEM((heads, tok), F32),
            pltpu.VMEM((tok, tok), F32),
            pltpu.SMEM((blocks + 1,), jnp.int32),
            pltpu.SMEM((8,), jnp.int32),
            pltpu.SMEM((blocks,), jnp.int32),
            pltpu.VMEM(q.shape, BF16),
            pltpu.VMEM(do.shape, BF16),
            pltpu.VMEM(delta.shape, F32),
            pltpu.VMEM(k.shape, BF16),
            pltpu.VMEM(v.shape, BF16),
            pltpu.SemaphoreType.DMA((5,)),
            pltpu.VMEM(q.shape, BF16),
            pltpu.VMEM((2,) + k.shape, BF16),
            pltpu.SemaphoreType.DMA((sets,)),
            pltpu.SemaphoreType.DMA((2, blocks)),
            pltpu.VMEM((heads * tok, dim), BF16),
            pltpu.VMEM((heads * tok, dim), BF16),
            pltpu.VMEM((LONGEST // tok + 1, tok, heads * tok), BF16),
            pltpu.VMEM((LONGEST // tok + 1, heads, tok), F32),
            pltpu.VMEM((tok, heads * tok), BF16),
            pltpu.VMEM((tok, heads * tok), BF16),
            pltpu.SMEM((blocks,), jnp.int32),
        ],
        compiler_params=pltpu.CompilerParams(vmem_limit_bytes=59 * 2**20),
        name="attention",
    )(lengths, spans, q, do, delta, k, v)


class Place:
    def __init__(self, with_dp):
        y = lax.axis_index("dp")
        me = lax.axis_index("ctx")
        z, x, c = me // 8, lax.rem(me // 2, 4), lax.rem(me, 2)
        self.core = c
        self.sibling = {"dp": y, "ctx": me + 1 - 2 * c}

        def at(y, z, x):
            return {"dp": y, "ctx": z * 8 + x * 2 + c}

        def low(t):
            return t + 1 - 2 * lax.rem(t, 2)

        def far(t):
            return lax.rem(t + 2, 4)

        self.opposite = (at(y, far(z), x), at(y, z, far(x)))
        self.bits = split_axis(z) + split_axis(x)
        self.partners = (at(y, 3 - z, x), at(y, low(z), x), at(y, z, 3 - x), at(y, z, low(x)))
        if with_dp:
            self.bits = split_axis(y) + self.bits
            self.partners = (at(3 - y, z, x), at(low(y), z, x)) + self.partners
            self.opposite = (at(far(y), z, x),) + self.opposite
        self.dims = len(self.bits)

    def greet(self, others=()):
        barrier = pltpu.get_barrier_semaphore()
        everyone = (self.sibling,) + self.partners + others
        for other in everyone:
            pl.semaphore_signal(barrier, inc=1, device_id=other, device_id_type=MESH)
        pl.semaphore_wait(barrier, len(everyone))

    def spot(self, free, flipped=()):
        found = []
        for d in range(self.dims):
            if d in free:
                found.append(slice(None))
            elif d in flipped:
                found.append(1 - self.bits[d])
            else:
                found.append(self.bits[d])
        return tuple(found)


def remote(src, dst, send, recv, to):
    return pltpu.make_async_remote_copy(
        src_ref=src, dst_ref=dst, send_sem=send, recv_sem=recv, device_id=to, device_id_type=MESH
    )


def turns(dims, start):
    return [(start + s) % dims for s in range(dims)]


GATHER_PARTS = 8


def gather_kernel(k_ref, v_ref, q_ref, do_ref, o_ref, x_ref,
                  k_out, v_out, q_two, do_two, delta_two, xt_two,
                  kv_all, q_buf, x_buf, do_buf, o_buf, xt_buf, delta_buf,
                  hop_send, hop_recv, pass_send, pass_recv, side_send, side_recv, local_sem):
    tok, dim = k_ref.shape
    half = q_two.shape[2]
    here = Place(False)
    c = here.core
    dims = here.dims
    quarter = tok // GATHER_PARTS
    own = kv_all.at[here.bits + (c,)]
    loads = [
        pltpu.make_async_copy(src, dst, local_sem.at[n])
        for n, (src, dst) in enumerate((
            (k_ref, own.at[0]), (v_ref, own.at[1]), (q_ref, q_buf), (do_ref, do_buf), (o_ref, o_buf), (x_ref, x_buf)))
    ]
    for copy in loads:
        copy.start()
    here.greet()
    loads[0].wait()
    loads[1].wait()

    def rows(p):
        return (slice(None), pl.ds(p * quarter, quarter), slice(None))

    hops, passes = {}, []

    def hop(p, s):
        order = turns(dims, p % dims)
        n = p * dims + s
        part = kv_all.at[here.spot(order[:s]) + (c,) + rows(p)]
        hops[p, s] = remote(part, part, hop_send.at[n], hop_recv.at[n], here.partners[order[s]])
        hops[p, s].start()

    def hand_on(p, s):
        order = turns(dims, p % dims)
        n = p * dims + s
        hops[p, s].wait_recv()
        part = kv_all.at[here.spot(order[:s], (order[s],)) + (c,) + rows(p)]
        copy = remote(part, part, pass_send.at[n], pass_recv.at[n], here.sibling)
        passes.append(copy)
        return copy

    def next_hop(s):
        for p in range(GATHER_PARTS):
            copy = hand_on(p, s)
            if s < dims - 1:
                hop(p, s + 1)
            copy.start()

    for p in range(GATHER_PARTS):
        hop(p, 0)
    sides = []
    def aside(src, dst):
        n = len(sides)
        sides.append(remote(src, dst, side_send.at[n], side_recv.at[n], here.sibling))
        sides[-1].start()

    for copy in loads[2:5]:
        copy.wait()
    theirs, mine = pl.ds((1 - c) * half, half), pl.ds(c * half, half)
    aside(own, own)
    aside(q_buf.at[:, theirs], q_two.at[c])
    aside(do_buf.at[:, theirs], do_two.at[c])
    keeps = []

    def keep(src, dst):
        keeps.append(pltpu.make_async_copy(src, dst, local_sem.at[6 + len(keeps)]))
        keeps[-1].start()

    keep(q_buf.at[:, mine], q_two.at[c])
    keep(do_buf.at[:, mine], do_two.at[c])

    next_hop(0)
    heads = half // dim
    for h in range(2 * heads):
        cols = pl.ds(h * dim, dim)
        products = do_buf[:, cols].astype(F32) * o_buf[:, cols].astype(F32)
        delta_buf[h // heads, pl.ds(h % heads, 1), :] = jnp.sum(products.T, axis=0, keepdims=True)
    for h in range(heads, delta_buf.shape[1]):
        delta_buf[:, pl.ds(h, 1), :] = jnp.zeros((2, 1, tok), F32)
    keep(delta_buf.at[c], delta_two.at[c])
    aside(delta_buf.at[1 - c], delta_two.at[c])
    loads[5].wait()

    def turn(i, carry):
        xt_buf[pl.ds(i * 128, 128), :] = x_buf[:, pl.ds(i * 128, 128)].T
        return carry

    steps = x_ref.shape[1] // 128
    next_hop(1)
    lax.fori_loop(0, steps // 2, turn, 0)
    mine = xt_two.at[:, pl.ds(c * tok, tok)]
    next_hop(2)
    lax.fori_loop(steps // 2, steps, turn, 0)
    keep(xt_buf, mine)
    aside(xt_buf, mine)
    next_hop(3)
    everywhere = (slice(None),) * dims
    keep(kv_all.at[everywhere + (c, 0)], k_out.at[everywhere + (c,)])
    keep(kv_all.at[everywhere + (c, 1)], v_out.at[everywhere + (c,)])
    for copy in passes:
        copy.wait()
    for copy in sides:
        copy.wait()
    keep(kv_all.at[everywhere + (1 - c, 0)], k_out.at[everywhere + (1 - c,)])
    keep(kv_all.at[everywhere + (1 - c, 1)], v_out.at[everywhere + (1 - c,)])
    for copy in hops.values():
        copy.wait_send()
    for copy in keeps:
        copy.wait()


def gather(k, v, q, do, o, x):
    tok, dim = k.shape
    half = q.shape[1] // 2
    anywhere = pl.BlockSpec(memory_space=pltpu.HBM)
    dma = pltpu.SemaphoreType.DMA
    full = jax.ShapeDtypeStruct((2, 2, 2, 2, 2, tok, dim), BF16)
    return pl.pallas_call(
        gather_kernel,
        out_shape=(
            full, full,
            jax.ShapeDtypeStruct((2, tok, half), BF16),
            jax.ShapeDtypeStruct((2, tok, half), BF16),
            jax.ShapeDtypeStruct((2, 8, tok), F32),
            jax.ShapeDtypeStruct((x.shape[1], 2 * tok), BF16),
        ),
        in_specs=[anywhere] * 6,
        out_specs=(anywhere,) * 6,
        scratch_shapes=[
            pltpu.VMEM((2, 2, 2, 2, 2, 2, tok, dim), BF16),
            pltpu.VMEM(q.shape, BF16),
            pltpu.VMEM(x.shape, BF16),
            pltpu.VMEM(q.shape, BF16),
            pltpu.VMEM(q.shape, BF16),
            pltpu.VMEM((x.shape[1], tok), BF16),
            pltpu.VMEM((2, 8, tok), F32),
            *[dma((4 * GATHER_PARTS,))] * 4, dma((6,)), dma((6,)), dma((14,)),
        ],
        compiler_params=pltpu.CompilerParams(
            collective_id=1, has_side_effects=True, vmem_limit_bytes=59 * 2**20
        ),
        name="gather",
    )(k, v, q, do, o, x)


def wide_parts(rows, cols):
    cut = cols // 2
    quarter, half = rows // 4, rows // 2
    return [(i * half, half, 0, cut) for i in range(2)] + [
        (i * quarter, quarter, cut, cols - cut) for i in range(4)
    ]


def ring_parts(rows, cols):
    half, quarter = rows // 2, rows // 4
    return [(0, half, 0, cols), (half, quarter, 0, cols), (half + quarter, quarter, 0, cols)]


def flips(stage):
    return (stage,) if len(stage) == 1 else (stage, stage[:1], stage[1:])


class Sums:
    def __init__(self, here, acc, parts, orders, landing, sems):
        self.here, self.acc, self.parts, self.orders = here, acc, parts, orders
        self.send_sem, self.recv_sem = sems
        self.copies, self.landing = {}, {}
        for n, key in enumerate(keys(orders)):
            self.landing[key] = (n, landing[n])

    def index(self, p, s, flipped):
        r0, nr, c0, nc = self.parts[p]
        free = [d for stage in self.orders[p][s + 1:] for d in stage]
        if isinstance(self.acc, list):
            return self.here.spot(free, flipped)
        middle = (slice(None),) * (len(self.acc.shape) - self.here.dims - 2)
        return self.here.spot(free, flipped) + middle + (pl.ds(r0, nr), pl.ds(c0, nc))

    def buffer(self, p):
        return self.acc[p] if isinstance(self.acc, list) else self.acc

    def send(self, p, s):
        for m, flipped in enumerate(flips(self.orders[p][s])):
            n, landing = self.landing[p, s, m]
            partner = self.here.partners[flipped[0]] if len(flipped) == 1 else self.here.opposite[flipped[0] // 2]
            copy = remote(
                self.buffer(p).at[self.index(p, s, flipped)], landing, self.send_sem.at[n], self.recv_sem.at[n], partner)
            copy.start()
            self.copies[p, s, m] = copy

    def total(self, p, s):
        found = self.buffer(p)[self.index(p, s, ())].astype(F32)
        for m in range(len(flips(self.orders[p][s]))):
            self.copies[p, s, m].wait_recv()
            found = found + self.landing[p, s, m][1][...].astype(F32)
        return found

    def step(self, s):
        for p in range(len(self.parts)):
            self.buffer(p)[self.index(p, s - 1, ())] = self.total(p, s - 1).astype(BF16)
            self.send(p, s)

    def finish(self):
        for copy in self.copies.values():
            copy.wait_send()


def keys(orders):
    return [(p, s, m) for p, order in enumerate(orders) for s, stage in enumerate(order)
            for m in range(len(flips(stage)))]


def landing_shapes(parts, orders, extra):
    shapes = []
    for p, s, _ in keys(orders):
        left = sum(len(stage) for stage in orders[p][s + 1:])
        shapes.append((2,) * left + extra + (parts[p][1], parts[p][3]))
    return shapes


def layout(tok, dim, half, features):
    row_chunk = features // 64
    kv_parts = [(i * (tok // 8), tok // 8, 0, dim) for i in range(8)]
    kv_orders = [
        ((0,), (1,), (2, 3)), ((1,), (0,), (2, 3)), ((2,), (3,), (0, 1)), ((3,), (2,), (0, 1))] * 2
    wide = wide_parts(row_chunk, half)
    wide_orders = [
        ((0,), (1,), (2, 3), (4, 5)), ((1,), (0,), (4, 5), (2, 3)), ((2,), (3,), (4, 5), (0, 1)),
        ((3,), (2,), (0, 1), (4, 5)), ((4,), (5,), (0, 1), (2, 3)), ((5,), (4,), (2, 3), (0, 1))]
    thin = ring_parts(row_chunk, dim)
    thin_orders = [
        ((0, 1), (2, 3), (4, 5)), ((2, 3), (4, 5), (0, 1)), ((4, 5), (0, 1), (2, 3))]
    return row_chunk, kv_parts, kv_orders, wide, wide_orders, thin, thin_orders


def reduce_kernel(plan, scale, dkv_ref, dq_ref, xt_ref, qg_ref, kvg_ref, wg_ref, *scratch):
    row_chunk, kv_parts, kv_orders, wide, wide_orders, thin, thin_orders = plan
    (kv_acc, kv_in, kv_mine, t_acc, xt, dq, fin, kv_send, kv_recv, w_send, w_recv, t_send, t_recv,
     side_send, side_recv, local_sem) = scratch[:16]
    w_acc = list(scratch[16:16 + len(wide)])
    landing = scratch[16 + len(wide):]
    tok, dim = dkv_ref.shape[-2:]
    half = dq_ref.shape[2]
    here_w = Place(True)
    here = Place(False)
    c = here.core
    n_kv, n_w = len(keys(kv_orders)), len(keys(wide_orders))
    kv = Sums(here, kv_acc, kv_parts, kv_orders, landing[:n_kv], (kv_send, kv_recv))
    w = Sums(here_w, w_acc, wide, wide_orders, landing[n_kv:n_kv + n_w], (w_send, w_recv))
    t = Sums(here_w, t_acc, thin, thin_orders, landing[n_kv + n_w:], (t_send, t_recv))

    load_x = pltpu.make_async_copy(xt_ref, xt, local_sem.at[1])
    load_x.start()
    load_q = pltpu.make_async_copy(dq_ref, dq, local_sem.at[0])
    load_q.start()
    load_kv = pltpu.make_async_copy(dkv_ref.at[c], kv_acc, local_sem.at[2])
    load_kv.start()
    here_w.greet(here_w.opposite)
    sides = []

    def aside(src, dst):
        n = len(sides)
        sides.append(remote(src, dst, side_send.at[n], side_recv.at[n], here.sibling))
        sides[-1].start()

    rest = (slice(None),) * 5
    for p in range(len(kv_parts)):
        r0, nr, _, _ = kv_parts[p]
        aside(dkv_ref.at[(1 - c,) + rest + (pl.ds(r0, nr),)], kv_in.at[rest + (pl.ds(r0, nr),)])
    aside(dq_ref.at[1 - c], qg_ref.at[:, pl.ds(c * half, half)])

    def products(i, right, accs, parts):
        block = dot(xt[pl.ds(i * 8 * row_chunk, 8 * row_chunk), :], right).astype(BF16)
        y = i // 2
        for j in range(8):
            z = 2 * lax.rem(i, 2) + j // 4
            x = j % 4
            at = split_axis(y) + split_axis(z) + (x // 2, (x + x // 2) % 2)
            for acc, (r0, nr, c0, nc) in zip(accs, parts):
                acc[at] = block[j * row_chunk + r0:j * row_chunk + r0 + nr, c0:c0 + nc]

    load_x.wait()
    load_q.wait()
    own_q = pltpu.make_async_copy(dq.at[c], qg_ref.at[:, pl.ds(c * half, half)], local_sem.at[3])
    own_q.start()
    both = dq[...].reshape(2 * tok, half)

    def wide_products(i, carry):
        products(i, both, w_acc, wide)
        return carry

    lax.fori_loop(0, 8, wide_products, 0)
    for p in range(2):
        w.send(p, 0)
    load_kv.wait()
    for p in range(len(kv_parts)):
        r0, nr, _, _ = kv_parts[p]
        sides[p].wait_recv()

        def join(i, carry, r0=r0, nr=nr):
            at = (i // 8, lax.rem(i // 4, 2), lax.rem(i // 2, 2), lax.rem(i, 2), slice(None), pl.ds(r0, nr))
            kv_acc[at] = (kv_acc[at].astype(F32) + kv_in[at].astype(F32)).astype(BF16)
            return carry

        lax.fori_loop(0, 16, join, 0)
        kv.send(p, 0)

    kv.step(1)
    for p in range(2, len(wide)):
        w.send(p, 0)
    kv.step(2)
    w.step(1)
    kv_scale = jnp.where(c == 0, scale, 1.0).astype(F32)
    for p in range(len(kv_parts)):
        r0, nr, _, _ = kv_parts[p]
        kv_mine[:, pl.ds(r0, nr), :] = (kv.total(p, 2) * kv_scale).astype(BF16)
    own_kv = pltpu.make_async_copy(kv_mine.at[c], kvg_ref.at[c], local_sem.at[4])
    own_kv.start()
    aside(kv_mine.at[1 - c], kvg_ref.at[c])
    mine = kv_mine[...].reshape(2 * tok, dim)

    def thin_products(i, carry):
        products(i, mine, [t_acc], [(0, row_chunk, 0, dim)])
        return carry

    lax.fori_loop(0, 8, thin_products, 0)
    for p in range(len(thin)):
        t.send(p, 0)
    w.step(2)
    t.step(1)
    w.step(3)
    t.step(2)
    rows_out = row_chunk // 2
    own_w = []

    def hand_out(src, dst, width):
        own_w.append(pltpu.make_async_copy(
            fin.at[pl.ds(c * rows_out, rows_out), pl.ds(src, width)],
            wg_ref.at[:, pl.ds(dst, width)], local_sem.at[5 + len(own_w)]))
        own_w[-1].start()
        aside(fin.at[pl.ds((1 - c) * rows_out, rows_out), pl.ds(src, width)],
              wg_ref.at[:, pl.ds(dst, width)])

    for p, (r0, nr, c0, nc) in enumerate(wide):
        fin[pl.ds(r0, nr), pl.ds(c0, nc)] = w.total(p, 3)
    hand_out(0, c * half, half)
    for p, (r0, nr, c0, nc) in enumerate(thin):
        fin[pl.ds(r0, nr), pl.ds(half, nc)] = t.total(p, 2)
    hand_out(half, 2 * half + c * dim, dim)
    own_q.wait()
    own_kv.wait()
    for copy in own_w:
        copy.wait()
    for n, copy in enumerate(sides):
        copy.wait_send()
        if n >= len(kv_parts):
            copy.wait_recv()
    kv.finish()
    w.finish()
    t.finish()


def reduce(dkv, dq, xt, scale):
    tok, dim = dkv.shape[-2:]
    half = dq.shape[2]
    features = xt.shape[0]
    plan = layout(tok, dim, half, features)
    row_chunk, kv_parts, kv_orders, wide, wide_orders, thin, thin_orders = plan
    dma = pltpu.SemaphoreType.DMA
    shapes = (landing_shapes(kv_parts, kv_orders, (2,)) + landing_shapes(wide, wide_orders, ())
              + landing_shapes(thin, thin_orders, ()))
    return pl.pallas_call(
        functools.partial(reduce_kernel, plan, scale),
        out_shape=(
            jax.ShapeDtypeStruct((tok, 2 * half), BF16),
            jax.ShapeDtypeStruct((2, tok, dim), BF16),
            jax.ShapeDtypeStruct((row_chunk // 2, 2 * half + 2 * dim), F32),
        ),
        in_specs=[pl.BlockSpec(memory_space=pltpu.HBM)] * 3,
        out_specs=(pl.BlockSpec(memory_space=pltpu.HBM),) * 3,
        scratch_shapes=[
            pltpu.VMEM(dkv.shape[1:], BF16),
            pltpu.VMEM(dkv.shape[1:], BF16),
            pltpu.VMEM((2, tok, dim), BF16),
            pltpu.VMEM((2,) * 6 + (row_chunk, dim), BF16),
            pltpu.VMEM(xt.shape, BF16),
            pltpu.VMEM(dq.shape, BF16),
            pltpu.VMEM((row_chunk, half + dim), F32),
            *[dma((len(keys(orders)),)) for orders in (kv_orders, wide_orders, thin_orders) for _ in range(2)],
            dma((12,)), dma((12,)), dma((8,)),
        ] + [pltpu.VMEM((2,) * 6 + (nr, nc), BF16) for _, nr, _, nc in wide]
        + [pltpu.VMEM(shape, BF16) for shape in shapes],
        compiler_params=pltpu.CompilerParams(
            collective_id=2, has_side_effects=True, vmem_limit_bytes=58 * 2**20
        ),
        name="reduce",
    )(dkv, dq, xt)


def finish_kernel(qg_ref, kvg_ref, wg_ref, q_out, k_out, v_out, w_out, sems):
    pairs = ((qg_ref, q_out.at[0]), (kvg_ref.at[0], k_out.at[0]), (kvg_ref.at[1], v_out.at[0]), (wg_ref, w_out))
    copies = [pltpu.make_async_copy(src, dst, sems.at[n]) for n, (src, dst) in enumerate(pairs)]
    for copy in copies:
        copy.start()
    for copy in copies:
        copy.wait()


def finish(qg, kvg, wg):
    hbm = pl.BlockSpec(memory_space=pltpu.HBM)
    one = jax.ShapeDtypeStruct((1,) + kvg.shape[1:], BF16)
    return pl.pallas_call(
        finish_kernel,
        out_shape=(jax.ShapeDtypeStruct((1,) + qg.shape, BF16), one, one, jax.ShapeDtypeStruct(wg.shape, F32)),
        in_specs=[pl.BlockSpec(memory_space=pltpu.VMEM)] * 3,
        out_specs=(hbm,) * 4,
        scratch_shapes=[pltpu.SemaphoreType.DMA((4,))],
        compiler_params=pltpu.CompilerParams(vmem_limit_bytes=59 * 2**20),
        name="finish",
    )(qg, kvg, wg)


def local(
    queries, key_rows, value_rows, forward_out, out_grad, layer_input, doc_lengths, held_span
):
    tok = queries.shape[1]
    dim = key_rows.shape[2]
    k, v, q, do, delta, xt = gather(
        key_rows[0], value_rows[0], queries[0], out_grad[0], forward_out[0], layer_input[0]
    )
    dq, dkv = attention(
        doc_lengths, held_span, q, do, delta, k.reshape(-1, tok, dim), v.reshape(-1, tok, dim)
    )
    dkv = dkv.reshape(2, 2, 2, 2, 2, 2, tok, dim)
    return finish(*reduce(dkv, dq, xt, 1.0 / math.sqrt(dim)))


def solution(mesh):
    row = P("dp", "ctx", None)
    flat = P("dp", None)
    return jax.shard_map(
        local, mesh=mesh, in_specs=(row,) * 6 + (flat,) * 2,
        out_specs=(row, row, row, P(("dp", "ctx"), None)), check_vma=False,
    )
```

```python
import functools, math
import jax, jax.numpy as jnp
from jax import lax
from jax.experimental import pallas as pl
from jax.experimental.pallas import tpu as pltpu
from jax.sharding import PartitionSpec as P

F32 = jnp.float32
BF16 = jnp.bfloat16
MESH = pl.DeviceIdType.MESH
NEG = -1e30
LONGEST = 4096


def dot(a, b):
    return jnp.dot(a, b, preferred_element_type=F32)


def split_axis(t):
    return t // 2, lax.rem(t + t // 2, 2)


def join_bits(bits):
    return ((bits[0] * 2 + bits[1]) * 2 + bits[2]) * 2 + bits[3]


def attention_kernel(sets, heads, tok, dim, blocks,
                     lengths_ref, span_ref,
                     q_in, do_in, delta_in, k_in, v_in,
                     dq_out, dkv_out,
                     qt, dot_, kt, dqt, dka, dva, stat_m, stat_l, bias, seen,
                     ends_ref, held_ref, q_ref, do_ref, delta_ref, k_ref, v_ref, loads,
                     dq_ref, dkv_ref, q_stores, kv_stores,
                     q_flat, do_flat, kept, kept_m, p_all, ds_all, marked):
    logit_scale = 1.0 / math.sqrt(dim)
    log2_scale = logit_scale * math.log2(math.e)

    pairs = ((q_in, q_ref), (do_in, do_ref), (delta_in, delta_ref), (k_in, k_ref), (v_in, v_ref))
    copies = [pltpu.make_async_copy(src, dst, loads.at[n]) for n, (src, dst) in enumerate(pairs)]
    for copy in copies:
        copy.start()
    me = lax.axis_index("ctx")
    own_chip = join_bits(split_axis(me // 8) + split_axis(lax.rem(me // 2, 4)))
    doc_count = lengths_ref.shape[1]
    end = jnp.int32(0)
    for d in range(doc_count):
        end = end + lengths_ref[0, d]
        ends_ref[d] = end

    def place(i, carry):
        chip = join_bits(split_axis(i // 8) + split_axis(lax.rem(i // 2, 4)))
        held_ref[2 * chip + lax.rem(i, 2)] = span_ref[0, i]
        return carry

    lax.fori_loop(0, blocks, place, 0)
    dka[...] = jnp.zeros_like(dka)
    dva[...] = jnp.zeros_like(dva)
    def store(kind, b):
        return pltpu.make_async_copy(dkv_ref.at[kind, b], dkv_out.at[kind, b], kv_stores.at[kind, b])

    def write(b):
        for kind, acc in enumerate((dka, dva)):
            dkv_ref[kind, b] = acc[b].astype(BF16)
            store(kind, b).start()

    for copy in copies:
        copy.wait()

    for rs in range(sets):
        own = 2 * own_chip + rs
        span = held_ref[own]
        first = span * tok

        def count(d, lo):
            end = ends_ref[d]
            return jnp.where(end <= first, jnp.maximum(lo, end), lo)

        lo_first = lax.fori_loop(0, doc_count, count, jnp.int32(0))
        seen[0] = own

        def collect(b, n):
            h = held_ref[b]
            take = (h < span) & (h * tok + (tok - 1) >= lo_first)

            @pl.when(take)
            def _():
                seen[n] = b

            return n + take.astype(jnp.int32)

        total = lax.fori_loop(0, blocks, collect, jnp.int32(1))
        last = rs == sets - 1
        if last:
            def unmark(b, carry):
                marked[b] = 0
                return carry

            def mark(i, carry):
                marked[seen[i]] = 1
                return carry

            def write_other(b, carry):
                @pl.when(marked[b] == 0)
                def _():
                    write(b)

                return carry

            lax.fori_loop(0, blocks, unmark, 0)
            lax.fori_loop(0, total, mark, 0)
            lax.fori_loop(0, blocks, write_other, 0)
        for h in range(heads):
            rows = pl.ds(h * dim, dim)
            flat = pl.ds(h * tok, tok)
            q_flat[flat, :] = q_ref[rs, :, rows]
            do_flat[flat, :] = do_ref[rs, :, rows]
            qt[:, flat] = q_flat[flat, :].T
            dot_[:, flat] = do_flat[flat, :].T
        pos = first + lax.broadcasted_iota(jnp.int32, (1, tok), 1)
        low = jnp.zeros((1, tok), jnp.int32)
        for d in range(doc_count):
            end = ends_ref[d]
            low = jnp.where(pos >= end, jnp.maximum(low, end), low)

        stat_m[...] = jnp.full_like(stat_m, NEG)
        stat_l[...] = jnp.zeros_like(stat_l)
        dqt[...] = jnp.zeros_like(dqt)

        def set_bias(b):
            kp = held_ref[b] * tok + lax.broadcasted_iota(jnp.int32, (tok, tok), 0)
            bias[...] = jnp.where((kp >= low) & (kp <= pos), 0.0, NEG)

        def pass_one(i, carry):
            b = seen[i]
            set_bias(b)
            k = k_ref[b]
            kt[b] = k.T
            for h in range(heads):
                row, cols = pl.ds(h, 1), pl.ds(h * tok, tok)
                s = dot(k, qt[:, cols]) * log2_scale + bias[...]
                m_old = stat_m[row, :]
                m_new = jnp.maximum(m_old, jnp.max(s, axis=0, keepdims=True))
                p = jnp.exp2(s - m_new)
                kept[i, :, cols] = p.astype(BF16)
                add = jnp.sum(p, axis=0, keepdims=True)
                stat_l[row, :] = stat_l[row, :] * jnp.exp2(m_old - m_new) + add
                stat_m[row, :] = m_new
                kept_m[i, row, :] = m_new
            return carry

        lax.fori_loop(0, total, pass_one, 0)
        stat_m[...] = stat_m[...] + jnp.log2(stat_l[...])

        def pass_two(i, carry):
            b = seen[i]
            v = v_ref[b]
            for h in range(heads):
                row, cols = pl.ds(h, 1), pl.ds(h * tok, tok)
                scaled = jnp.exp2(kept_m[i, row, :] - stat_m[row, :])
                p = kept[i, :, cols].astype(F32) * scaled
                dp = dot(v, dot_[:, cols])
                p_all[:, cols] = p.astype(BF16)
                ds_all[:, cols] = (p * (dp - delta_ref[rs, row, :])).astype(BF16)
            dva[b] += dot(p_all[...], do_flat[...])
            dka[b] += dot(ds_all[...], q_flat[...])
            dqt[...] += dot(kt[b], ds_all[...])
            if last:
                write(b)
            return carry

        lax.fori_loop(0, total, pass_two, 0)
        for h in range(heads):
            rows = pl.ds(h * dim, dim)
            dq_ref[rs, :, rows] = (logit_scale * dqt[:, pl.ds(h * tok, tok)]).T.astype(BF16)
        pltpu.make_async_copy(dq_ref.at[rs], dq_out.at[rs], q_stores.at[rs]).start()

    def stored(b, carry):
        store(0, b).wait()
        store(1, b).wait()
        return carry

    lax.fori_loop(0, blocks, stored, 0)
    for rs in range(sets):
        pltpu.make_async_copy(dq_ref.at[rs], dq_out.at[rs], q_stores.at[rs]).wait()


def attention(lengths, spans, q, do, delta, k, v):
    sets, tok, width = q.shape
    blocks, _, dim = k.shape
    heads = width // dim
    smem = pl.BlockSpec(memory_space=pltpu.SMEM)
    return pl.pallas_call(
        functools.partial(attention_kernel, sets, heads, tok, dim, blocks),
        out_shape=(
            jax.ShapeDtypeStruct(q.shape, BF16),
            jax.ShapeDtypeStruct((2,) + k.shape, BF16),
        ),
        in_specs=[smem, smem] + [pl.BlockSpec(memory_space=pltpu.HBM)] * 5,
        out_specs=(pl.BlockSpec(memory_space=pltpu.HBM),) * 2,
        scratch_shapes=[
            pltpu.VMEM((dim, heads * tok), BF16),
            pltpu.VMEM((dim, heads * tok), BF16),
            pltpu.VMEM((blocks, dim, tok), BF16),
            pltpu.VMEM((dim, heads * tok), F32),
            pltpu.VMEM((blocks, tok, dim), F32),
            pltpu.VMEM((blocks, tok, dim), F32),
            pltpu.VMEM((heads, tok), F32),
            pltpu.VMEM((heads, tok), F32),
            pltpu.VMEM((tok, tok), F32),
            pltpu.SMEM((blocks + 1,), jnp.int32),
            pltpu.SMEM((8,), jnp.int32),
            pltpu.SMEM((blocks,), jnp.int32),
            pltpu.VMEM(q.shape, BF16),
            pltpu.VMEM(do.shape, BF16),
            pltpu.VMEM(delta.shape, F32),
            pltpu.VMEM(k.shape, BF16),
            pltpu.VMEM(v.shape, BF16),
            pltpu.SemaphoreType.DMA((5,)),
            pltpu.VMEM(q.shape, BF16),
            pltpu.VMEM((2,) + k.shape, BF16),
            pltpu.SemaphoreType.DMA((sets,)),
            pltpu.SemaphoreType.DMA((2, blocks)),
            pltpu.VMEM((heads * tok, dim), BF16),
            pltpu.VMEM((heads * tok, dim), BF16),
            pltpu.VMEM((LONGEST // tok + 1, tok, heads * tok), BF16),
            pltpu.VMEM((LONGEST // tok + 1, heads, tok), F32),
            pltpu.VMEM((tok, heads * tok), BF16),
            pltpu.VMEM((tok, heads * tok), BF16),
            pltpu.SMEM((blocks,), jnp.int32),
        ],
        compiler_params=pltpu.CompilerParams(vmem_limit_bytes=59 * 2**20),
        name="attention",
    )(lengths, spans, q, do, delta, k, v)


class Place:
    def __init__(self, with_dp):
        y = lax.axis_index("dp")
        me = lax.axis_index("ctx")
        z, x, c = me // 8, lax.rem(me // 2, 4), lax.rem(me, 2)
        self.core = c
        self.sibling = {"dp": y, "ctx": me + 1 - 2 * c}

        def at(y, z, x):
            return {"dp": y, "ctx": z * 8 + x * 2 + c}

        def low(t):
            return t + 1 - 2 * lax.rem(t, 2)

        def far(t):
            return lax.rem(t + 2, 4)

        self.opposite = (at(y, far(z), x), at(y, z, far(x)))
        self.bits = split_axis(z) + split_axis(x)
        self.partners = (at(y, 3 - z, x), at(y, low(z), x), at(y, z, 3 - x), at(y, z, low(x)))
        if with_dp:
            self.bits = split_axis(y) + self.bits
            self.partners = (at(3 - y, z, x), at(low(y), z, x)) + self.partners
            self.opposite = (at(far(y), z, x),) + self.opposite
        self.dims = len(self.bits)

    def greet(self, others=()):
        barrier = pltpu.get_barrier_semaphore()
        everyone = (self.sibling,) + self.partners + others
        for other in everyone:
            pl.semaphore_signal(barrier, inc=1, device_id=other, device_id_type=MESH)
        pl.semaphore_wait(barrier, len(everyone))

    def partner(self, flipped):
        return self.partners[flipped[0]] if len(flipped) == 1 else self.opposite[flipped[0] // 2]

    def spot(self, free, flipped=()):
        found = []
        for d in range(self.dims):
            if d in free:
                found.append(slice(None))
            elif d in flipped:
                found.append(1 - self.bits[d])
            else:
                found.append(self.bits[d])
        return tuple(found)


def remote(src, dst, send, recv, to):
    return pltpu.make_async_remote_copy(
        src_ref=src, dst_ref=dst, send_sem=send, recv_sem=recv, device_id=to, device_id_type=MESH
    )


def turns(dims, start):
    return [(start + s) % dims for s in range(dims)]


GATHER_PARTS = 8
GATHER_ORDERS = (
    ((2, 3), (0,), (1,)), ((2, 3), (1,), (0,)), ((0, 1), (2,), (3,)), ((0, 1), (3,), (2,)))


def gather_kernel(k_ref, v_ref, q_ref, do_ref, o_ref, x_ref,
                  k_out, v_out, q_two, do_two, delta_two, xt_two,
                  kv_all, q_buf, x_buf, do_buf, o_buf, xt_buf, delta_buf,
                  hop_send, hop_recv, pass_send, pass_recv, side_send, side_recv, local_sem):
    tok, dim = k_ref.shape
    half = q_two.shape[2]
    here = Place(False)
    c = here.core
    dims = here.dims
    quarter = tok // GATHER_PARTS
    own = kv_all.at[here.bits + (c,)]
    loads = [
        pltpu.make_async_copy(src, dst, local_sem.at[n])
        for n, (src, dst) in enumerate((
            (k_ref, own.at[0]), (v_ref, own.at[1]), (q_ref, q_buf), (do_ref, do_buf), (o_ref, o_buf), (x_ref, x_buf)))
    ]
    for copy in loads:
        copy.start()
    here.greet(here.opposite)
    loads[0].wait()
    loads[1].wait()

    def rows(p):
        return (slice(None), pl.ds(p * quarter, quarter), slice(None))

    hops, passes = {}, []

    def held(p, s, flipped=()):
        free = [d for stage in GATHER_ORDERS[p % dims][:s] for d in stage]
        return kv_all.at[here.spot(free, flipped) + (c,) + rows(p)]

    def hop(p, s):
        for m, flipped in enumerate(flips(GATHER_ORDERS[p % dims][s])):
            n = p * 5 + (m if s == 0 else s + 2)
            part = held(p, s)
            hops[p, s, m] = remote(part, part, hop_send.at[n], hop_recv.at[n], here.partner(flipped))
            hops[p, s, m].start()

    def next_hop(s):
        for p in range(GATHER_PARTS):
            ways = flips(GATHER_ORDERS[p % dims][s])
            for m in range(len(ways)):
                hops[p, s, m].wait_recv()
            if s < 2:
                hop(p, s + 1)
            for m, flipped in enumerate(ways):
                n = p * 5 + (m if s == 0 else s + 2)
                part = held(p, s, flipped)
                passes.append(remote(part, part, pass_send.at[n], pass_recv.at[n], here.sibling))
                passes[-1].start()

    for p in range(GATHER_PARTS):
        hop(p, 0)
    sides = []
    def aside(src, dst):
        n = len(sides)
        sides.append(remote(src, dst, side_send.at[n], side_recv.at[n], here.sibling))
        sides[-1].start()

    for copy in loads[2:5]:
        copy.wait()
    theirs, mine = pl.ds((1 - c) * half, half), pl.ds(c * half, half)
    aside(own, own)
    aside(q_buf.at[:, theirs], q_two.at[c])
    aside(do_buf.at[:, theirs], do_two.at[c])
    keeps = []

    def keep(src, dst):
        keeps.append(pltpu.make_async_copy(src, dst, local_sem.at[6 + len(keeps)]))
        keeps[-1].start()

    keep(q_buf.at[:, mine], q_two.at[c])
    keep(do_buf.at[:, mine], do_two.at[c])

    next_hop(0)
    heads = half // dim
    for h in range(2 * heads):
        cols = pl.ds(h * dim, dim)
        products = do_buf[:, cols].astype(F32) * o_buf[:, cols].astype(F32)
        delta_buf[h // heads, pl.ds(h % heads, 1), :] = jnp.sum(products.T, axis=0, keepdims=True)
    for h in range(heads, delta_buf.shape[1]):
        delta_buf[:, pl.ds(h, 1), :] = jnp.zeros((2, 1, tok), F32)
    keep(delta_buf.at[c], delta_two.at[c])
    aside(delta_buf.at[1 - c], delta_two.at[c])
    loads[5].wait()

    def turn(i, carry):
        xt_buf[pl.ds(i * 128, 128), :] = x_buf[:, pl.ds(i * 128, 128)].T
        return carry

    steps = x_ref.shape[1] // 128
    next_hop(1)
    mine = xt_two.at[:, pl.ds(c * tok, tok)]
    lax.fori_loop(0, steps, turn, 0)
    keep(xt_buf, mine)
    aside(xt_buf, mine)
    next_hop(2)
    everywhere = (slice(None),) * dims
    keep(kv_all.at[everywhere + (c, 0)], k_out.at[everywhere + (c,)])
    keep(kv_all.at[everywhere + (c, 1)], v_out.at[everywhere + (c,)])
    for copy in passes:
        copy.wait()
    for copy in sides:
        copy.wait()
    keep(kv_all.at[everywhere + (1 - c, 0)], k_out.at[everywhere + (1 - c,)])
    keep(kv_all.at[everywhere + (1 - c, 1)], v_out.at[everywhere + (1 - c,)])
    for copy in hops.values():
        copy.wait_send()
    for copy in keeps:
        copy.wait()


def gather(k, v, q, do, o, x):
    tok, dim = k.shape
    half = q.shape[1] // 2
    anywhere = pl.BlockSpec(memory_space=pltpu.HBM)
    dma = pltpu.SemaphoreType.DMA
    full = jax.ShapeDtypeStruct((2, 2, 2, 2, 2, tok, dim), BF16)
    return pl.pallas_call(
        gather_kernel,
        out_shape=(
            full, full,
            jax.ShapeDtypeStruct((2, tok, half), BF16),
            jax.ShapeDtypeStruct((2, tok, half), BF16),
            jax.ShapeDtypeStruct((2, 8, tok), F32),
            jax.ShapeDtypeStruct((x.shape[1], 2 * tok), BF16),
        ),
        in_specs=[anywhere] * 6,
        out_specs=(anywhere,) * 6,
        scratch_shapes=[
            pltpu.VMEM((2, 2, 2, 2, 2, 2, tok, dim), BF16),
            pltpu.VMEM(q.shape, BF16),
            pltpu.VMEM(x.shape, BF16),
            pltpu.VMEM(q.shape, BF16),
            pltpu.VMEM(q.shape, BF16),
            pltpu.VMEM((x.shape[1], tok), BF16),
            pltpu.VMEM((2, 8, tok), F32),
            *[dma((5 * GATHER_PARTS,))] * 4, dma((6,)), dma((6,)), dma((14,)),
        ],
        compiler_params=pltpu.CompilerParams(
            collective_id=1, has_side_effects=True, vmem_limit_bytes=59 * 2**20
        ),
        name="gather",
    )(k, v, q, do, o, x)


def wide_parts(rows, cols):
    cut = cols // 2
    quarter, half = rows // 4, rows // 2
    return [(i * half, half, 0, cut) for i in range(2)] + [
        (i * quarter, quarter, cut, cols - cut) for i in range(4)
    ]


def ring_parts(rows, cols):
    half, quarter = rows // 2, rows // 4
    return [(0, half, 0, cols), (half, quarter, 0, cols), (half + quarter, quarter, 0, cols)]


def flips(stage):
    return (stage,) if len(stage) == 1 else (stage, stage[:1], stage[1:])


class Sums:
    def __init__(self, here, acc, parts, orders, landing, sems):
        self.here, self.acc, self.parts, self.orders = here, acc, parts, orders
        self.send_sem, self.recv_sem = sems
        self.copies, self.landing = {}, {}
        for n, key in enumerate(keys(orders)):
            self.landing[key] = (n, landing[n])

    def index(self, p, s, flipped):
        r0, nr, c0, nc = self.parts[p]
        free = [d for stage in self.orders[p][s + 1:] for d in stage]
        if isinstance(self.acc, list):
            return self.here.spot(free, flipped)
        middle = (slice(None),) * (len(self.acc.shape) - self.here.dims - 2)
        return self.here.spot(free, flipped) + middle + (pl.ds(r0, nr), pl.ds(c0, nc))

    def buffer(self, p):
        return self.acc[p] if isinstance(self.acc, list) else self.acc

    def send(self, p, s):
        for m, flipped in enumerate(flips(self.orders[p][s])):
            n, landing = self.landing[p, s, m]
            partner = self.here.partner(flipped)
            copy = remote(
                self.buffer(p).at[self.index(p, s, flipped)], landing, self.send_sem.at[n], self.recv_sem.at[n], partner)
            copy.start()
            self.copies[p, s, m] = copy

    def total(self, p, s):
        found = self.buffer(p)[self.index(p, s, ())].astype(F32)
        for m in range(len(flips(self.orders[p][s]))):
            self.copies[p, s, m].wait_recv()
            found = found + self.landing[p, s, m][1][...].astype(F32)
        return found

    def step(self, s):
        for p in range(len(self.parts)):
            self.buffer(p)[self.index(p, s - 1, ())] = self.total(p, s - 1).astype(BF16)
            self.send(p, s)

    def finish(self):
        for copy in self.copies.values():
            copy.wait_send()


def keys(orders):
    return [(p, s, m) for p, order in enumerate(orders) for s, stage in enumerate(order)
            for m in range(len(flips(stage)))]


def landing_shapes(parts, orders, extra):
    shapes = []
    for p, s, _ in keys(orders):
        left = sum(len(stage) for stage in orders[p][s + 1:])
        shapes.append((2,) * left + extra + (parts[p][1], parts[p][3]))
    return shapes


def layout(tok, dim, half, features):
    row_chunk = features // 64
    kv_parts = [(i * (tok // 8), tok // 8, 0, dim) for i in range(8)]
    kv_orders = [
        ((0,), (1,), (2, 3)), ((1,), (0,), (2, 3)), ((2,), (3,), (0, 1)), ((3,), (2,), (0, 1))] * 2
    wide = wide_parts(row_chunk, half)
    wide_orders = [
        ((0,), (1,), (2, 3), (4, 5)), ((1,), (0,), (4, 5), (2, 3)), ((2,), (3,), (4, 5), (0, 1)),
        ((3,), (2,), (0, 1), (4, 5)), ((4,), (5,), (0, 1), (2, 3)), ((5,), (4,), (2, 3), (0, 1))]
    thin = ring_parts(row_chunk, dim)
    thin_orders = [
        ((0, 1), (2, 3), (4, 5)), ((2, 3), (4, 5), (0, 1)), ((4, 5), (0, 1), (2, 3))]
    return row_chunk, kv_parts, kv_orders, wide, wide_orders, thin, thin_orders


def reduce_kernel(plan, scale, dkv_ref, dq_ref, xt_ref, qg_ref, kvg_ref, wg_ref, *scratch):
    row_chunk, kv_parts, kv_orders, wide, wide_orders, thin, thin_orders = plan
    (kv_acc, kv_in, kv_mine, t_acc, xt, dq, fin, kv_send, kv_recv, w_send, w_recv, t_send, t_recv,
     side_send, side_recv, local_sem) = scratch[:16]
    w_acc = list(scratch[16:16 + len(wide)])
    landing = scratch[16 + len(wide):]
    tok, dim = dkv_ref.shape[-2:]
    half = dq_ref.shape[2]
    here_w = Place(True)
    here = Place(False)
    c = here.core
    n_kv, n_w = len(keys(kv_orders)), len(keys(wide_orders))
    kv = Sums(here, kv_acc, kv_parts, kv_orders, landing[:n_kv], (kv_send, kv_recv))
    w = Sums(here_w, w_acc, wide, wide_orders, landing[n_kv:n_kv + n_w], (w_send, w_recv))
    t = Sums(here_w, t_acc, thin, thin_orders, landing[n_kv + n_w:], (t_send, t_recv))

    load_x = pltpu.make_async_copy(xt_ref, xt, local_sem.at[1])
    load_x.start()
    load_q = pltpu.make_async_copy(dq_ref, dq, local_sem.at[0])
    load_q.start()
    load_kv = pltpu.make_async_copy(dkv_ref.at[c], kv_acc, local_sem.at[2])
    load_kv.start()
    here_w.greet(here_w.opposite)
    sides = []

    def aside(src, dst):
        n = len(sides)
        sides.append(remote(src, dst, side_send.at[n], side_recv.at[n], here.sibling))
        sides[-1].start()

    rest = (slice(None),) * 5
    for p in range(len(kv_parts)):
        r0, nr, _, _ = kv_parts[p]
        aside(dkv_ref.at[(1 - c,) + rest + (pl.ds(r0, nr),)], kv_in.at[rest + (pl.ds(r0, nr),)])
    aside(dq_ref.at[1 - c], qg_ref.at[:, pl.ds(c * half, half)])

    def products(i, right, accs, parts):
        block = dot(xt[pl.ds(i * 8 * row_chunk, 8 * row_chunk), :], right).astype(BF16)
        y = i // 2
        for j in range(8):
            z = 2 * lax.rem(i, 2) + j // 4
            x = j % 4
            at = split_axis(y) + split_axis(z) + (x // 2, (x + x // 2) % 2)
            for acc, (r0, nr, c0, nc) in zip(accs, parts):
                acc[at] = block[j * row_chunk + r0:j * row_chunk + r0 + nr, c0:c0 + nc]

    load_x.wait()
    load_q.wait()
    own_q = pltpu.make_async_copy(dq.at[c], qg_ref.at[:, pl.ds(c * half, half)], local_sem.at[3])
    own_q.start()
    both = dq[...].reshape(2 * tok, half)

    def wide_products(i, carry):
        products(i, both, w_acc, wide)
        return carry

    lax.fori_loop(0, 8, wide_products, 0)
    for p in range(2):
        w.send(p, 0)
    load_kv.wait()
    for p in range(len(kv_parts)):
        r0, nr, _, _ = kv_parts[p]
        sides[p].wait_recv()

        def join(i, carry, r0=r0, nr=nr):
            at = (i // 8, lax.rem(i // 4, 2), lax.rem(i // 2, 2), lax.rem(i, 2), slice(None), pl.ds(r0, nr))
            kv_acc[at] = (kv_acc[at].astype(F32) + kv_in[at].astype(F32)).astype(BF16)
            return carry

        lax.fori_loop(0, 16, join, 0)
        kv.send(p, 0)

    kv.step(1)
    for p in range(2, len(wide)):
        w.send(p, 0)
    kv.step(2)
    w.step(1)
    kv_scale = jnp.where(c == 0, scale, 1.0).astype(F32)
    for p in range(len(kv_parts)):
        r0, nr, _, _ = kv_parts[p]
        kv_mine[:, pl.ds(r0, nr), :] = (kv.total(p, 2) * kv_scale).astype(BF16)
    own_kv = pltpu.make_async_copy(kv_mine.at[c], kvg_ref.at[c], local_sem.at[4])
    own_kv.start()
    aside(kv_mine.at[1 - c], kvg_ref.at[c])
    mine = kv_mine[...].reshape(2 * tok, dim)

    def thin_products(i, carry):
        products(i, mine, [t_acc], [(0, row_chunk, 0, dim)])
        return carry

    lax.fori_loop(0, 8, thin_products, 0)
    for p in range(len(thin)):
        t.send(p, 0)
    w.step(2)
    t.step(1)
    w.step(3)
    t.step(2)
    rows_out = row_chunk // 2
    own_w = []

    def hand_out(src, dst, width):
        own_w.append(pltpu.make_async_copy(
            fin.at[pl.ds(c * rows_out, rows_out), pl.ds(src, width)],
            wg_ref.at[:, pl.ds(dst, width)], local_sem.at[5 + len(own_w)]))
        own_w[-1].start()
        aside(fin.at[pl.ds((1 - c) * rows_out, rows_out), pl.ds(src, width)],
              wg_ref.at[:, pl.ds(dst, width)])

    for p, (r0, nr, c0, nc) in enumerate(wide):
        fin[pl.ds(r0, nr), pl.ds(c0, nc)] = w.total(p, 3)
    hand_out(0, c * half, half)
    for p, (r0, nr, c0, nc) in enumerate(thin):
        fin[pl.ds(r0, nr), pl.ds(half, nc)] = t.total(p, 2)
    hand_out(half, 2 * half + c * dim, dim)
    own_q.wait()
    own_kv.wait()
    for copy in own_w:
        copy.wait()
    for n, copy in enumerate(sides):
        copy.wait_send()
        if n >= len(kv_parts):
            copy.wait_recv()
    kv.finish()
    w.finish()
    t.finish()


def reduce(dkv, dq, xt, scale):
    tok, dim = dkv.shape[-2:]
    half = dq.shape[2]
    features = xt.shape[0]
    plan = layout(tok, dim, half, features)
    row_chunk, kv_parts, kv_orders, wide, wide_orders, thin, thin_orders = plan
    dma = pltpu.SemaphoreType.DMA
    shapes = (landing_shapes(kv_parts, kv_orders, (2,)) + landing_shapes(wide, wide_orders, ())
              + landing_shapes(thin, thin_orders, ()))
    return pl.pallas_call(
        functools.partial(reduce_kernel, plan, scale),
        out_shape=(
            jax.ShapeDtypeStruct((tok, 2 * half), BF16),
            jax.ShapeDtypeStruct((2, tok, dim), BF16),
            jax.ShapeDtypeStruct((row_chunk // 2, 2 * half + 2 * dim), F32),
        ),
        in_specs=[pl.BlockSpec(memory_space=pltpu.HBM)] * 3,
        out_specs=(pl.BlockSpec(memory_space=pltpu.HBM),) * 3,
        scratch_shapes=[
            pltpu.VMEM(dkv.shape[1:], BF16),
            pltpu.VMEM(dkv.shape[1:], BF16),
            pltpu.VMEM((2, tok, dim), BF16),
            pltpu.VMEM((2,) * 6 + (row_chunk, dim), BF16),
            pltpu.VMEM(xt.shape, BF16),
            pltpu.VMEM(dq.shape, BF16),
            pltpu.VMEM((row_chunk, half + dim), F32),
            *[dma((len(keys(orders)),)) for orders in (kv_orders, wide_orders, thin_orders) for _ in range(2)],
            dma((12,)), dma((12,)), dma((8,)),
        ] + [pltpu.VMEM((2,) * 6 + (nr, nc), BF16) for _, nr, _, nc in wide]
        + [pltpu.VMEM(shape, BF16) for shape in shapes],
        compiler_params=pltpu.CompilerParams(
            collective_id=2, has_side_effects=True, vmem_limit_bytes=58 * 2**20
        ),
        name="reduce",
    )(dkv, dq, xt)


def finish_kernel(qg_ref, kvg_ref, wg_ref, q_out, k_out, v_out, w_out, sems):
    pairs = ((qg_ref, q_out.at[0]), (kvg_ref.at[0], k_out.at[0]), (kvg_ref.at[1], v_out.at[0]), (wg_ref, w_out))
    copies = [pltpu.make_async_copy(src, dst, sems.at[n]) for n, (src, dst) in enumerate(pairs)]
    for copy in copies:
        copy.start()
    for copy in copies:
        copy.wait()


def finish(qg, kvg, wg):
    hbm = pl.BlockSpec(memory_space=pltpu.HBM)
    one = jax.ShapeDtypeStruct((1,) + kvg.shape[1:], BF16)
    return pl.pallas_call(
        finish_kernel,
        out_shape=(jax.ShapeDtypeStruct((1,) + qg.shape, BF16), one, one, jax.ShapeDtypeStruct(wg.shape, F32)),
        in_specs=[pl.BlockSpec(memory_space=pltpu.VMEM)] * 3,
        out_specs=(hbm,) * 4,
        scratch_shapes=[pltpu.SemaphoreType.DMA((4,))],
        compiler_params=pltpu.CompilerParams(vmem_limit_bytes=59 * 2**20),
        name="finish",
    )(qg, kvg, wg)


def local(
    queries, key_rows, value_rows, forward_out, out_grad, layer_input, doc_lengths, held_span
):
    tok = queries.shape[1]
    dim = key_rows.shape[2]
    k, v, q, do, delta, xt = gather(
        key_rows[0], value_rows[0], queries[0], out_grad[0], forward_out[0], layer_input[0]
    )
    dq, dkv = attention(
        doc_lengths, held_span, q, do, delta, k.reshape(-1, tok, dim), v.reshape(-1, tok, dim)
    )
    dkv = dkv.reshape(2, 2, 2, 2, 2, 2, tok, dim)
    return finish(*reduce(dkv, dq, xt, 1.0 / math.sqrt(dim)))


def solution(mesh):
    row = P("dp", "ctx", None)
    flat = P("dp", None)
    return jax.shard_map(
        local, mesh=mesh, in_specs=(row,) * 6 + (flat,) * 2,
        out_specs=(row, row, row, P(("dp", "ctx"), None)), check_vma=False,
    )
```
